512 devices in a mesh: gx: 8 (over y), gy: 8 (over x, core), gz: 8 (over z).
Axes of the slice: x: 4, y: 8, z: 8, core: 2. Of those that a mesh axis runs over, the one named last changes fastest.
Arguments:
- positions: float32 [3, 96, 48, 48, 128], P(None, 'gx', 'gy', 'gz'), may hold values from 0 to 96, as said below
- mass: float32 [96, 48, 48, 128], P('gx', 'gy', 'gz'), may hold values from 0.003 to 0.03
- support: float32 [96, 48, 48, 128], P('gx', 'gy', 'gz'), may hold values from 0.5 to 1
- counts: int32 [96, 48, 48], P('gx', 'gy', 'gz'), may hold values from 32 to 128
- entropy: float32 [96, 48, 48, 128], P('gx', 'gy', 'gz'), may hold values from 0.2 to 2
- density_old: float32 [96, 48, 48, 128], P('gx', 'gy', 'gz'), may hold values from 0.3 to 3
- active: int32 [96, 48, 48], P('gx', 'gy', 'gz'), may hold values from 0 to 1, as said below
Outputs:
- density: float32 [96, 48, 48, 128], P('gx', 'gy', 'gz')
- accel: float32 [3, 96, 48, 48, 128], P(None, 'gx', 'gy', 'gz')
The draws below stay inside these ranges and needn't reach their ends.
Inputs may be any that keep to these rules, and one draw needn't show every extreme that they name: At most 9 cells are active in the block of 12 x 6 x 6 cells of one device, and exactly 9 in some device's block; every device's block has at least one. `positions`: each particle lies in its own cell: the unit cube whose lower corner is the cell's index.
All inputs are finite; a program needn't handle non-finite values.
Results may differ from the reference program's by a relative error of at most 0.0003.
Values sent between devices are 32-bit elements; how exact they have to be, the bound alone decides.
No kernel may reach another device: no remote copies, remote signals or barrier semaphores. Data moves between devices by JAX's collectives and lax.ppermute only.
A program may use at most 64 MiB of HBM per device.

```python
import math
import jax
import jax.numpy as jnp
from jax import lax

S = 128
CY = 6
CX = 12
CZ = 6
ACT_MAX = 9
NX = 96
NY = 48
NZ = 48


def draw_positions(key, part):
    key = jax.random.fold_in(key, 5)
    unit = jax.random.uniform(key, (3, NX, NY, NZ, S), jnp.float32, 0.0, 0.999)
    offset = unit
    first = jnp.broadcast_to(jnp.arange(NX, dtype=jnp.float32)[:, None, None, None], (NX, NY, NZ, 1))
    second = jnp.broadcast_to(jnp.arange(NY, dtype=jnp.float32)[None, :, None, None], (NX, NY, NZ, 1))
    third = jnp.broadcast_to(jnp.arange(NZ, dtype=jnp.float32)[None, None, :, None], (NX, NY, NZ, 1))
    corner = jnp.stack([first, second, third], axis=0)
    return corner + offset


def draw_active(key, part):
    key = jax.random.fold_in(key, 11)
    blocks_x = NX // CX
    blocks_y = NY // CY
    blocks_z = NZ // CZ
    blocks = blocks_x * blocks_y * blocks_z
    cells = CX * CY * CZ
    key_count, key_full, key_order = jax.random.split(key, 3)
    upper = max(ACT_MAX * 2 // 3, 1)
    numbers = jax.random.randint(key_count, (blocks,), 1, upper + 1)
    full = jax.random.randint(key_full, (), 0, blocks)
    numbers = jnp.where(jnp.arange(blocks) == full, ACT_MAX, numbers)
    order_keys = jax.random.split(key_order, blocks)
    orders = jax.vmap(lambda one: jax.random.permutation(one, cells))(order_keys)
    ranks = jnp.argsort(orders, axis=1, stable=True)
    chosen = (ranks < numbers[:, None]).astype(jnp.int32)
    chosen = chosen.reshape(blocks_x, blocks_y, blocks_z, CX, CY, CZ)
    chosen = jnp.transpose(chosen, (0, 3, 1, 4, 2, 5))
    return chosen.reshape(NX, NY, NZ).astype(jnp.int32)


def with_ends(result, key, least, top_value):
    longest = result.shape.index(max(result.shape))
    spots = []
    for shift in (0, 1):
        where = [jax.random.randint(jax.random.fold_in(key, axis), (), 0, length) for axis, length in enumerate(result.shape)]
        where[longest] = (where[longest] + shift) % result.shape[longest]
        spots.append(tuple(where))
    return result.at[spots[0]].set(least).at[spots[1]].set(top_value)


def level_of(stream_key, extent, cuts, least, high):
    level, own = 1.0, jax.random.fold_in(stream_key, 6)
    for position, parts in cuts:
        steps = jnp.exp(jax.random.uniform(jax.random.fold_in(own, position), (parts,), jnp.float32, least / len(cuts), high / len(cuts)))
        level = level * jnp.repeat(steps, extent[position] // parts).reshape([-1 if axis == position else 1 for axis in range(len(extent))])
    return level


def setup_inputs(seed: int = 0) -> dict:
    splits = jax.random.split(jax.random.key(seed), 8)
    return {
        "positions": draw_positions(jax.random.fold_in(splits[7], 71), 0),
        "mass": jnp.clip(jnp.exp(math.log(0.03) - 2.3025851 * jax.random.uniform(splits[1], (NX, NY, NZ, S), jnp.float32) ** level_of(splits[1], (NX, NY, NZ, S), ((0, 8), (1, 8), (2, 8)), -0.2, 0.2)), 0.003, 0.03),
        "support": jnp.clip(jnp.exp(math.log(1.0) - 0.6931472 * jax.random.uniform(splits[2], (NX, NY, NZ, S), jnp.float32) ** level_of(splits[2], (NX, NY, NZ, S), ((0, 8), (1, 8), (2, 8)), -0.2, 0.2)), 0.5, 1.0),
        "counts": with_ends(jax.random.randint(splits[3], (NX, NY, NZ), 32, 129), jax.random.fold_in(splits[3], 1), 32, 128).astype(jnp.int32),
        "entropy": jnp.clip(jnp.exp(math.log(2.0) - 2.3025851 * jax.random.uniform(splits[4], (NX, NY, NZ, S), jnp.float32) ** level_of(splits[4], (NX, NY, NZ, S), ((0, 8), (1, 8), (2, 8)), -0.2, 0.2)), 0.2, 2.0),
        "density_old": jnp.clip(jnp.exp(math.log(3.0) - 2.3025851 * jax.random.uniform(splits[5], (NX, NY, NZ, S), jnp.float32) ** level_of(splits[5], (NX, NY, NZ, S), ((0, 8), (1, 8), (2, 8)), -0.2, 0.2)), 0.3, 3.0),
        "active": draw_active(jax.random.fold_in(splits[7], 71), 0),
    }


KC = 21.0 / (2.0 * math.pi)

def density_terms(own, near):
    diff = own[:3, :, None] - near[:3, None, :]
    dist = jnp.sqrt(lax.optimization_barrier(jnp.sum(diff * diff, axis=0)))
    qval = dist * own[4][:, None]
    wval = jnp.maximum(1.0 - qval, 0.0)
    kern = wval ** 4 * (1.0 + 4.0 * qval) * own[4][:, None] ** 3
    return KC * lax.optimization_barrier(jnp.sum(near[3][None, :] * kern, axis=1))

def force_terms(own, own_p, near, near_p):
    diff = own[:3, :, None] - near[:3, None, :]
    dist = jnp.sqrt(lax.optimization_barrier(jnp.sum(diff * diff, axis=0)))
    w_own = jnp.maximum(1.0 - dist * own[4][:, None], 0.0)
    w_near = jnp.maximum(1.0 - dist * near[4][None, :], 0.0)
    g_own = w_own ** 3 * own[4][:, None] ** 5
    g_near = w_near ** 3 * near[4][None, :] ** 5
    coef = near[3][None, :] * (own_p[:, None] * g_own + near_p[None, :] * g_near)
    return 20.0 * KC * lax.optimization_barrier(jnp.sum(coef[None] * diff, axis=2))

def reference(positions, mass, support, counts, entropy, density_old, active):
    slots = jnp.arange(S, dtype=jnp.int32)
    valid = slots[None, None, None, :] < counts[..., None]
    m_eff = jnp.where(valid, mass, jnp.float32(0.0))
    pack = jnp.concatenate([positions, m_eff[None], (1.0 / support)[None]], axis=0)
    extended = jnp.pad(pack, ((0, 0), (1, 1), (1, 1), (1, 1), (0, 0)))
    flat = active.reshape(-1)
    capacity = ACT_MAX * (NX // CX) * (NY // CY) * (NZ // CZ)
    cell_ids = jnp.nonzero(flat, size=capacity, fill_value=0)[0].astype(jnp.int32)
    live = jnp.arange(capacity, dtype=jnp.int32) < jnp.sum(flat)

    def corner(cell):
        return (cell // (NY * NZ), cell // NZ % NY, cell % NZ)

    def dens_one(cell):
        a, b, d = corner(cell)
        zero = jnp.int32(0)
        near = lax.dynamic_slice(extended, (zero, a, b, d, zero), (5, 3, 3, 3, S)).reshape(5, 27 * S)
        own = lax.dynamic_slice(extended, (zero, a + 1, b + 1, d + 1, zero), (5, 1, 1, 1, S)).reshape(5, S)
        return density_terms(own, near)
    fresh = lax.map(dens_one, cell_ids)
    fresh = jnp.where(live[:, None], fresh, jnp.float32(0.0))
    grid_new = jnp.zeros((NX * NY * NZ, S), jnp.float32).at[cell_ids].add(fresh).reshape(NX, NY, NZ, S)
    act = (active > 0)[..., None]
    density = jnp.where(act & valid, grid_new, density_old)
    pterm = entropy * density ** (-1.0 / 3.0)
    p_ext = jnp.pad(pterm, ((1, 1), (1, 1), (1, 1), (0, 0)))

    def force_one(cell):
        a, b, d = corner(cell)
        zero = jnp.int32(0)
        near = lax.dynamic_slice(extended, (zero, a, b, d, zero), (5, 3, 3, 3, S)).reshape(5, 27 * S)
        own = lax.dynamic_slice(extended, (zero, a + 1, b + 1, d + 1, zero), (5, 1, 1, 1, S)).reshape(5, S)
        near_p = lax.dynamic_slice(p_ext, (a, b, d, zero), (3, 3, 3, S)).reshape(27 * S)
        own_p = lax.dynamic_slice(p_ext, (a + 1, b + 1, d + 1, zero), (1, 1, 1, S)).reshape(S)
        return force_terms(own, own_p, near, near_p)
    pushes = lax.map(force_one, cell_ids)
    pushes = jnp.where(live[:, None, None], pushes, jnp.float32(0.0))
    grid_acc = jnp.zeros((NX * NY * NZ, 3, S), jnp.float32).at[cell_ids].add(pushes)
    accel = jnp.transpose(grid_acc.reshape(NX, NY, NZ, 3, S), (3, 0, 1, 2, 4)) * valid[None].astype(jnp.float32)
    return (density, accel)
```

```python
import math

import jax
import jax.numpy as jnp
from jax import lax
from jax.experimental import pallas as pl
from jax.experimental.pallas import tpu as pltpu
from jax.sharding import PartitionSpec as P

KC = 21.0 / (2.0 * math.pi)
HALO = 2


def padded(value, sides, width):
    for axis, dim in sides:
        size, length = (lax.axis_size(axis), value.shape[dim])
        up = [(i, (i + 1) % size) for i in range(size - 1)]
        down = [(j, i) for i, j in up]
        last = lax.slice_in_dim(value, length - width, length, axis=dim)
        initial = lax.slice_in_dim(value, 0, width, axis=dim)
        before = lax.ppermute(last, axis, up)
        after = lax.ppermute(initial, axis, down)
        value = jnp.concatenate([before, value, after], axis=dim)
    return value


def kernel(dims, flags_ref, ext_ref, old_ref, dens_ref, acc_ref, ids_ref, cols_ref, pt_ref):
    size_x, size_y, size_z = dims
    near_y, near_z = size_y + 2, size_z + 2
    total = (size_x + 2) * near_y * near_z

    def scan(k, n):
        ids_ref[n] = k
        return n + flags_ref[k]

    number = lax.fori_loop(0, total, scan, jnp.int32(0), unroll=8)

    def place(slot):
        k = ids_ref[slot]
        a = lax.div(k, near_y * near_z)
        b = lax.rem(lax.div(k, near_z), near_y)
        return a, b, lax.rem(k, near_z)

    def row(c, a, b, d):
        return ext_ref[c, a, b, pl.ds(d, 1), :]

    def load_columns(a, b, d):
        for n, c in enumerate((0, 1, 2, 4)):
            cols_ref[n] = jnp.broadcast_to(row(c, a + 1, b + 1, d + 1), (128, 128)).T

    def lane_sum(value):
        ones = jnp.ones((8, 128), jnp.float32)
        dims_ = (((1,), (1,)), ((), ()))
        out = lax.dot_general(
            ones, value, dims_, precision=lax.Precision.HIGHEST, preferred_element_type=jnp.float32
        )
        return out[0:1]

    pt_ref[...] = ext_ref[5, 1 : size_x + 3, 1 : size_y + 3]
    dens_ref[...] = old_ref[...]
    acc_ref[...] = jnp.zeros(acc_ref.shape, jnp.float32)

    def is_own(a, b, d):
        return (
            (a >= 1) & (a <= size_x) & (b >= 1) & (b <= size_y) & (d >= 1) & (d <= size_z)
        )

    def density(slot, _):
        a, b, d = place(slot)
        load_columns(a, b, d)

        def near(k, acc):
            na, nb, nd = a + lax.div(k, 9), b + lax.rem(lax.div(k, 3), 3), d + lax.rem(k, 3)
            dx = cols_ref[0] - row(0, na, nb, nd)
            dy = cols_ref[1] - row(1, na, nb, nd)
            dz = cols_ref[2] - row(2, na, nb, nd)
            sq = jnp.maximum(dx * dx + dy * dy + dz * dz, 1e-30)
            qv = sq * lax.rsqrt(sq) * cols_ref[3]
            w = jnp.maximum(1.0 - qv, 0.0)
            w2 = w * w
            return acc + row(3, na, nb, nd) * (w2 * w2 * (1.0 + 4.0 * qv))

        acc = lax.fori_loop(0, 27, near, jnp.zeros((128, 128), jnp.float32))
        inv = row(4, a + 1, b + 1, d + 1)
        fresh = KC * lane_sum(acc) * (inv * inv * inv)
        good = row(3, a + 1, b + 1, d + 1) > 0.0
        safe = jnp.where(good, fresh, 1.0)
        pt_ref[a, b, pl.ds(d + 1, 1), :] = row(5, a + 1, b + 1, d + 1) * jnp.exp(
            jnp.log(safe) * (-1.0 / 3.0)
        )

        @pl.when(is_own(a, b, d))
        def _():
            spot = (a - 1, b - 1, pl.ds(d - 1, 1), slice(None))
            dens_ref[spot] = jnp.where(good, fresh, old_ref[spot])

        return 0

    lax.fori_loop(0, number, density, 0)

    def force(slot, _):
        a, b, d = place(slot)

        @pl.when(is_own(a, b, d))
        def _():
            load_columns(a, b, d)
            inv = row(4, a + 1, b + 1, d + 1)
            inv2 = inv * inv
            own = pt_ref[a, b, pl.ds(d + 1, 1), :] * (inv2 * inv2 * inv)
            cols_ref[4] = jnp.broadcast_to(own, (128, 128)).T
            outs = [[], [], []]
            for half in range(2):
                part = slice(64 * half, 64 * half + 64)

                def near(k, sums):
                    na, nb, nd = a + lax.div(k, 9), b + lax.rem(lax.div(k, 3), 3), d + lax.rem(k, 3)
                    dx = cols_ref[0, part] - row(0, na, nb, nd)
                    dy = cols_ref[1, part] - row(1, na, nb, nd)
                    dz = cols_ref[2, part] - row(2, na, nb, nd)
                    sq = jnp.maximum(dx * dx + dy * dy + dz * dz, 1e-30)
                    dist = sq * lax.rsqrt(sq)
                    near_inv = row(4, na, nb, nd)
                    near_m = row(3, na, nb, nd)
                    near_2 = near_inv * near_inv
                    weight = (
                        near_m
                        * pt_ref[na - 1, nb - 1, pl.ds(nd, 1), :]
                        * (near_2 * near_2 * near_inv)
                    )
                    wi = jnp.maximum(1.0 - dist * cols_ref[3, part], 0.0)
                    wj = jnp.maximum(1.0 - dist * near_inv, 0.0)
                    coef = near_m * (cols_ref[4, part] * (wi * wi * wi)) + weight * (wj * wj * wj)
                    sx, sy, sz = sums
                    return sx + coef * dx, sy + coef * dy, sz + coef * dz

                zero = jnp.zeros((64, 128), jnp.float32)
                sums = lax.fori_loop(0, 27, near, (zero, zero, zero))
                for n in range(3):
                    outs[n].append(sums[n])
            good = row(3, a + 1, b + 1, d + 1) > 0.0
            for n in range(3):
                total_n = lane_sum(jnp.concatenate(outs[n], axis=0)) * (20.0 * KC)
                acc_ref[n, a - 1, b - 1, pl.ds(d - 1, 1), :] = jnp.where(good, total_n, 0.0)

        return 0

    lax.fori_loop(0, number, force, 0)


def per_device(positions, mass, support, counts, entropy, density_old, active):
    size_x, size_y, size_z, slots = mass.shape
    shape = mass.shape
    valid = jnp.arange(slots, dtype=jnp.int32)[None, None, None, :] < counts[..., None]
    m_eff = jnp.where(valid, mass, jnp.float32(0.0))
    act = (active > 0)[..., None]
    term = jnp.where(act, entropy, entropy * density_old ** (-1.0 / 3.0))
    flag = jnp.broadcast_to(act.astype(jnp.float32), shape)
    pack = jnp.concatenate(
        [positions, m_eff[None], (1.0 / support)[None], term[None], flag[None]], axis=0
    )
    extended = padded(pack, (("gz", 3), ("gx", 1), ("gy", 2)), HALO)
    flags = extended[6, 1 : size_x + 3, 1 : size_y + 3, 1 : size_z + 3, 0].astype(jnp.int32)
    total = (size_x + 2) * (size_y + 2) * (size_z + 2)
    import functools

    vmem = pl.BlockSpec(memory_space=pltpu.VMEM)
    return pl.pallas_call(
        functools.partial(kernel, (size_x, size_y, size_z)),
        out_shape=(
            jax.ShapeDtypeStruct(shape, jnp.float32),
            jax.ShapeDtypeStruct((3, *shape), jnp.float32),
        ),
        in_specs=[pl.BlockSpec(memory_space=pltpu.SMEM), vmem, vmem],
        out_specs=(vmem, vmem),
        scratch_shapes=[
            pltpu.SMEM((total + 1,), jnp.int32),
            pltpu.VMEM((5, 128, 128), jnp.float32),
            pltpu.VMEM((size_x + 2, size_y + 2, size_z + 4, slots), jnp.float32),
        ],
        compiler_params=pltpu.CompilerParams(vmem_limit_bytes=48 * 1024 * 1024),
    )(flags.reshape(total), extended, density_old)


def solution(mesh):
    return jax.shard_map(
        per_device,
        mesh=mesh,
        in_specs=(
            P(None, "gx", "gy", "gz", None),
            P("gx", "gy", "gz", None),
            P("gx", "gy", "gz", None),
            P("gx", "gy", "gz"),
            P("gx", "gy", "gz", None),
            P("gx", "gy", "gz", None),
            P("gx", "gy", "gz"),
        ),
        out_specs=(P("gx", "gy", "gz", None), P(None, "gx", "gy", "gz", None)),
        check_vma=False,
    )
```

```python
import functools
import math

import jax
import jax.numpy as jnp
from jax import lax
from jax.experimental import pallas as pl
from jax.experimental.pallas import tpu as pltpu
from jax.sharding import PartitionSpec as P

KC = 21.0 / (2.0 * math.pi)
SX, SY, SZ, S = 12, 6, 6, 128
MOST = 9
CELLS = SX * SY * SZ

ZERO = CELLS * 8
OWN_TAIL = ZERO + 8
OWN_ROWS = OWN_TAIL + 8

Z_TWO, Z_FAR, Z_TAIL, Z_ROWS = 288, 432, 720, 728
X_TWO, X_FAR, X_TAIL, X_ROWS = 240, 336, 576, 584
Y_TWO, Y_SUM, Y_TAIL, Y_ROWS = 640, 864, 976, 992

ZLO = OWN_ROWS
ZHI = ZLO + Z_ROWS
XLO = ZHI + Z_ROWS
XHI = XLO + X_ROWS
SLAB = XHI + X_ROWS

SLAB_MOST = 96
ALL_MOST = 256

VMEM = pl.BlockSpec(memory_space=pltpu.VMEM)
SMEM = pl.BlockSpec(memory_space=pltpu.SMEM)
GROUPS = 2
NEAR = 3
PARAMS = pltpu.CompilerParams(vmem_limit_bytes=40 * 1024 * 1024)

BLOCKS = [(0, 0), (0, -1), (0, 1), (-1, 0), (-1, -1), (-1, 1), (1, 0), (1, -1), (1, 1)]


def step(mode, i, near, sums):
    xi, yi, zi, hi, bi = i
    xj, yj, zj, mj, hj, wj = near
    dx, dy, dz = xi - xj, yi - yj, zi - zj
    sq = jnp.maximum(dx * dx + dy * dy + dz * dz, 1e-30)
    dist = sq * lax.rsqrt(sq)
    out = []
    if mode != "near":
        wi = jnp.maximum(hi - dist, 0.0)
        own = mj * (wi * wi * wi)
        out.append(sums[0] + own * (wi * (bi - wi)))
        if mode == "all":
            out += [sums[1] + own * dx, sums[2] + own * dy, sums[3] + own * dz]
    if mode != "density":
        wj_ = jnp.maximum(hj - dist, 0.0)
        other = wj * (wj_ * wj_ * wj_)
        last = sums[-3:]
        out += [last[0] + other * dx, last[1] + other * dy, last[2] + other * dz]
    return tuple(out)


WIDTH = {"all": 7, "density": 1, "near": 3}
FIRST = {"all": 0, "density": 0, "near": 4}


def pairs(mode, src, four, two, use, count, tile, cols, table):
    for u in range(NEAR - 1):
        four[count + u] = jnp.int32(0)
        two[count + u] = jnp.int32(0)
        use[count + u] = jnp.float32(0.0)
    steps = lax.div(count + (NEAR - 1), NEAR)
    used = jnp.sum(jnp.where(tile[3:4] > 0.0, 1.0, 0.0)).astype(jnp.int32)
    cols[:, 0:8] = tile.T
    width = WIDTH[mode]
    lane = lax.broadcasted_iota(jnp.int32, (8, 128), 1)
    zero = jnp.zeros((8, 128), jnp.float32)

    def group(g, _):
        spots, own = [], []
        for v in range(GROUPS):
            spot = pl.ds(pl.multiple_of((g * GROUPS + v) * 8, 8), 8)
            block = cols[spot, :]
            x, y, z, h = [
                jnp.broadcast_to(block[:, c : c + 1], (8, 128)) for c in (0, 1, 2, 4)
            ]
            spots.append(spot)
            own.append((x, y, z, h, 1.25 * h))

        def body(q, sums):
            sums = list(sums)
            for u in range(NEAR):
                at = q * NEAR + u
                f = four[at]
                near = [
                    jnp.broadcast_to(src[pl.ds(f + c, 1), :], (8, 128)) for c in range(4)
                ]
                flag = use[at]
                if mode != "near":
                    near[3] = near[3] * jnp.where(flag >= 0.5, 1.0, 0.0)
                if mode != "density":
                    t = two[at]
                    near.append(jnp.broadcast_to(src[pl.ds(t, 1), :], (8, 128)))
                    weight = jnp.broadcast_to(src[pl.ds(t + 1, 1), :], (8, 128))
                    near.append(weight * jnp.where(flag == 1.0, 1.0, 0.0))
                else:
                    near += [None, None]
                for v in range(GROUPS):
                    sums[v] = step(mode, own[v], near, sums[v])
            return tuple(sums)

        sums = lax.fori_loop(0, steps, body, ((zero,) * width,) * GROUPS)
        for v in range(GROUPS):
            line = zero
            for c in range(width):
                total = jnp.sum(sums[v][c], axis=1, keepdims=True)
                line = jnp.where(lane == FIRST[mode] + c, total, line)
            table[spots[v], :] = line
        return 0

    lax.fori_loop(0, lax.div(used + (8 * GROUPS - 1), 8 * GROUPS), group, 0)
    return table[...].T[0:8]


def corner(k):
    return lax.div(k, SY * SZ), lax.rem(lax.div(k, SZ), SY), lax.rem(k, SZ)


def pack(counts, active, pos, mass, support, entropy, old, own, up, down, ids):
    def scan(q, n):
        y, z = lax.div(q, SZ), lax.rem(q, SZ)
        for x in range(SX):
            ids[n] = (x * SY + y) * SZ + z
            n = n + active[y, z, x]
        return n

    number = lax.fori_loop(0, SY * SZ, scan, jnp.int32(0))
    for s in range(MOST, 15):
        ids[s] = jnp.int32(0)
    ids[15] = number
    lane = lax.broadcasted_iota(jnp.int32, (8, 128), 1)
    tail = jnp.zeros((8, 128), jnp.int32)
    for s in range(MOST):
        tail = jnp.where(lane == s, ids[s], tail)
    tail = jnp.where(lane == 15, number, tail).astype(jnp.float32)
    own[ZERO : ZERO + 8] = jnp.zeros((8, 128), jnp.float32)
    own[OWN_TAIL : OWN_TAIL + 8] = tail
    up[Z_TAIL : Z_TAIL + 8] = tail
    down[Z_TAIL : Z_TAIL + 8] = tail
    sub = lax.broadcasted_iota(jnp.int32, (SZ, 128), 0)
    slot = lax.broadcasted_iota(jnp.int32, (SZ, 128), 1)

    def cells(x2, _):
        for u in range(2):
            x = x2 * 2 + u
            for y in range(SY):
                many = jnp.zeros((SZ, 128), jnp.int32)
                act = jnp.zeros((SZ, 128), jnp.int32)
                for z in range(SZ):
                    many = jnp.where(sub == z, counts[y, z, x], many)
                    act = jnp.where(sub == z, active[y, z, x], act)
                h = support[x, y]
                inv = 1.0 / h
                inv2 = inv * inv
                inv4 = inv2 * inv2
                m = jnp.where(slot < many, mass[x, y], 0.0)
                gain = entropy[x, y] * (inv4 * inv4)
                power = jnp.exp(jnp.log(old[x, y]) * (-1.0 / 3.0))
                weight = m * gain * jnp.where(act > 0, 1.0, power)
                base = pl.multiple_of(x2 * (2 * SY * SZ * 8), 8) + (u * SY + y) * SZ * 8
                for c, value in enumerate(
                    (pos[0, x, y], pos[1, x, y], pos[2, x, y], m, h, weight, gain)
                ):
                    own[pl.ds(base + c, SZ, stride=8), :] = value
                four = pl.multiple_of(x2 * (2 * SY * 4), 8) + (u * SY + y) * 4
                two = pl.multiple_of(x2 * (2 * SY * 2), 8) + (u * SY + y) * 2
                for out, z1, z2 in ((up, SZ - 1, SZ - 2), (down, 0, 1)):
                    out[pl.ds(four, 4), :] = own[pl.ds(base + z1 * 8, 4), :]
                    out[pl.ds(two + Z_TWO, 2), :] = own[pl.ds(base + z1 * 8 + 4, 2), :]
                    out[pl.ds(four + Z_FAR, 4), :] = own[pl.ds(base + z2 * 8, 4), :]
        return 0

    lax.fori_loop(0, SX // 2, cells, 0)


def own_row(x, y, z):
    return ((x * SY + y) * SZ + z) * 8


def local(part, ids, own, before, sums, four, two, use, flags, cols, table):
    number = ids[15]
    half = lax.div(number + 1, 2)

    def clear(k, _):
        flags[k] = jnp.int32(0)
        return 0

    lax.fori_loop(0, CELLS, clear, 0, unroll=16)

    def mark(s, _):
        flags[ids[s]] = jnp.int32(1)
        return 0

    lax.fori_loop(0, number, mark, 0)
    if before is not None:
        sums[...] = before[...]

    def slot(s, _):
        k = ids[s]
        a, b, d = corner(k)
        count = jnp.int32(0)
        for ea in (-1, 0, 1):
            for eb in (-1, 0, 1):
                for ed in (-1, 0, 1):
                    na, nb, nd = a + ea, b + eb, d + ed
                    inside = (
                        (na >= 0) & (na < SX) & (nb >= 0) & (nb < SY) & (nd >= 0) & (nd < SZ)
                    )
                    cell = k + (ea * SY + eb) * SZ + ed
                    four[count] = cell * 8
                    two[count] = cell * 8 + 4
                    known = flags[jnp.where(inside, cell, 0)]
                    use[count] = jnp.where(known > 0, jnp.float32(0.5), jnp.float32(1.0))
                    count = count + inside.astype(jnp.int32)
        row = pl.multiple_of(k * 8, 8)
        tile = own[pl.ds(row, 8), :]
        sums[s] = pairs("all", own, four, two, use, count, tile, cols, table)
        return 0

    if part == 0:
        lax.fori_loop(0, half, slot, 0)
    else:
        lax.fori_loop(half, number, slot, 0)


def local_first(ids, own, sums, *scratch):
    local(0, ids, own, None, sums, *scratch)


def local_second(ids, own, before, _, sums, *scratch):
    local(1, ids, own, before, sums, *scratch)


def pack_x(own, zlo, zhi, up, down):
    for out, x1, x2 in ((up, SX - 1, SX - 2), (down, 0, 1)):
        for y in range(SY):
            for z in range(-2, SZ + 2):
                for x, base in ((x1, 0), (x2, X_FAR)):
                    spot = base + (y * (SZ + 4) + z + 2) * 4
                    if 0 <= z < SZ:
                        row = own_row(x, y, z)
                        out[spot : spot + 4] = own[row : row + 4]
                    else:
                        src = zlo if z < 0 else zhi
                        far = Z_FAR if z in (-2, SZ + 1) else 0
                        row = far + (x * SY + y) * 4
                        out[spot : spot + 4] = src[row : row + 4]
                if -1 <= z <= SZ:
                    spot = X_TWO + (y * (SZ + 2) + z + 1) * 2
                    if 0 <= z < SZ:
                        row = own_row(x1, y, z) + 4
                        out[spot : spot + 2] = own[row : row + 2]
                    else:
                        src = zlo if z < 0 else zhi
                        row = Z_TWO + (x1 * SY + y) * 2
                        out[spot : spot + 2] = src[row : row + 2]
        out[X_TAIL : X_TAIL + 8] = jnp.zeros((8, 128), jnp.float32)
        out[X_TAIL : X_TAIL + 1] = own[OWN_TAIL : OWN_TAIL + 1]
        out[X_TAIL + 1 : X_TAIL + 2] = zlo[Z_TAIL : Z_TAIL + 1]
        out[X_TAIL + 2 : X_TAIL + 3] = zhi[Z_TAIL : Z_TAIL + 1]


def slab_rows(x, y, z):
    k = x * SY + y
    four = own_row(x, y, z)
    two = four + 4
    zbase = jnp.where(z < 0, ZLO, ZHI)
    zfar = (z == -2) | (z == SZ + 1)
    zout = (z < 0) | (z >= SZ)
    four = jnp.where(zout, zbase + jnp.where(zfar, Z_FAR, 0) + k * 4, four)
    two = jnp.where(zout, zbase + Z_TWO + k * 2, two)
    xbase = jnp.where(x < 0, XLO, XHI)
    xfar = (x == -2) | (x == SX + 1)
    xout = (x < 0) | (x >= SX)
    four = jnp.where(xout, xbase + jnp.where(xfar, X_FAR, 0) + (y * (SZ + 4) + z + 2) * 4, four)
    two = jnp.where(xout, xbase + X_TWO + (y * (SZ + 2) + z + 1) * 2, two)
    return four, two


def slab_rows_at(x, y, z):
    if 0 <= x < SX and 0 <= z < SZ:
        return own_row(x, y, z), own_row(x, y, z) + 4
    if 0 <= x < SX:
        base, far, k = ZLO if z < 0 else ZHI, z in (-2, SZ + 1), x * SY + y
        return base + (Z_FAR if far else 0) + k * 4, base + Z_TWO + k * 2
    base, far = XLO if x < 0 else XHI, x in (-2, SX + 1)
    four = base + (X_FAR if far else 0) + (y * (SZ + 4) + z + 2) * 4
    return four, base + X_TWO + (y * (SZ + 2) + z + 1) * 2


def slab(
    ids, own, zlo, zhi, xlo, xhi, before, up, down, tiles, sums, places,
    rows, tails, lists, sem, four, two, use, flags, cols, table,
):
    rows[0:OWN_ROWS] = own[...]
    rows[ZLO:ZHI] = zlo[...]
    rows[ZHI:XLO] = zhi[...]
    rows[XLO:XHI] = xlo[...]
    rows[XHI:SLAB] = xhi[...]
    tails[...] = jnp.zeros(tails.shape, jnp.int32)
    tails[0:1] = own[OWN_TAIL : OWN_TAIL + 1].astype(jnp.int32)
    tails[1:2] = zlo[Z_TAIL : Z_TAIL + 1].astype(jnp.int32)
    tails[2:3] = zhi[Z_TAIL : Z_TAIL + 1].astype(jnp.int32)
    tails[3:6] = xlo[X_TAIL : X_TAIL + 3].astype(jnp.int32)
    tails[6:9] = xhi[X_TAIL : X_TAIL + 3].astype(jnp.int32)
    copy = pltpu.make_async_copy(tails, lists, sem)
    copy.start()

    def clear(k, _):
        flags[k] = jnp.int32(0)
        return 0

    lax.fori_loop(0, (SX + 2) * SY * (SZ + 2), clear, 0, unroll=16)
    for out, y in ((up, SY - 1), (down, 0)):
        for x in range(-2, SX + 2):
            for z in range(-2, SZ + 2):
                row4, row2 = slab_rows_at(x, y, z)
                spot = ((x + 2) * (SZ + 4) + z + 2) * 4
                out[spot : spot + 4] = rows[row4 : row4 + 4]
                if -1 <= x <= SX and -1 <= z <= SZ:
                    spot = Y_TWO + ((x + 1) * (SZ + 2) + z + 1) * 2
                    out[spot : spot + 2] = rows[row2 : row2 + 2]
        out[Y_SUM:Y_TAIL] = jnp.zeros((Y_TAIL - Y_SUM, 128), jnp.float32)
        out[Y_TAIL:Y_ROWS] = jnp.zeros((Y_ROWS - Y_TAIL, 128), jnp.float32)
        out[Y_TAIL : Y_TAIL + 1] = own[OWN_TAIL : OWN_TAIL + 1]
        out[Y_TAIL + 1 : Y_TAIL + 2] = zlo[Z_TAIL : Z_TAIL + 1]
        out[Y_TAIL + 2 : Y_TAIL + 3] = zhi[Z_TAIL : Z_TAIL + 1]
        out[Y_TAIL + 3 : Y_TAIL + 6] = xlo[X_TAIL : X_TAIL + 3]
        out[Y_TAIL + 6 : Y_TAIL + 9] = xhi[X_TAIL : X_TAIL + 3]
    copy.wait()

    def flag_at(x, y, z):
        return ((x + 1) * SY + y) * (SZ + 2) + z + 1

    number = jnp.int32(0)
    for q, (bx, bz) in enumerate(BLOCKS):

        def one(s, n, q=q, bx=bx, bz=bz):
            a, b, d = corner(lists[q, s])
            x, z = a + bx * SX, d + bz * SZ
            inside = (x >= -1) & (x <= SX) & (z >= -1) & (z <= SZ)
            places[0, n] = x
            places[1, n] = b
            places[2, n] = z

            @pl.when(inside)
            def _():
                flags[flag_at(x, b, z)] = jnp.int32(1)

            return n + inside.astype(jnp.int32)

        number = lax.fori_loop(0, lists[q, 15], one, number)
    places[3, 0] = number
    places[3, 1] = lists[0, 15]
    mine = lists[0, 15]

    def slot(s, _):
        x, y, z = places[0, s], places[1, s], places[2, s]
        row4, row2 = slab_rows(x, y, z)
        first = rows[pl.ds(row4, 4), :]
        second = rows[pl.ds(row2, 2), :]
        tile = jnp.concatenate([first, second, jnp.zeros((2, 128), jnp.float32)], axis=0)
        is_mine = s < mine
        count = jnp.int32(0)
        for ea in (-1, 0, 1):
            for eb in (-1, 0, 1):
                for ed in (-1, 0, 1):
                    na, nb, nd = x + ea, y + eb, z + ed
                    n4, n2 = slab_rows(na, nb, nd)
                    outer = (na < 0) | (na >= SX) | (nd < 0) | (nd >= SZ)
                    wanted = (nb >= 0) & (nb < SY) & (outer | jnp.logical_not(is_mine))
                    four[count] = n4
                    two[count] = n2
                    seen = wanted & is_mine
                    known = flags[jnp.where(seen, flag_at(na, nb, nd), 0)]
                    use[count] = jnp.where(known > 0, jnp.float32(0.5), jnp.float32(1.0))
                    count = count + wanted.astype(jnp.int32)

        @pl.when(is_mine)
        def _():
            sums[s] = before[s]

            @pl.when(count > 0)
            def _():
                sums[s] = sums[s] + pairs("all", rows, four, two, use, count, tile, cols, table)

            tiles[s] = tile
            tiles[s, 6:7] = sums[s, 0:1]
            sums[s, 7:8] = rows[pl.ds(row4 + 6, 1), :]

        @pl.when(jnp.logical_not(is_mine))
        def _():
            result = pairs("density", rows, four, two, use, count, tile, cols, table)
            tiles[s] = tile
            tiles[s, 6:7] = result[0:1]

        spot = Y_SUM + (x + 1) * (SZ + 2) + z + 1

        @pl.when(y == 0)
        def _():
            down[pl.ds(spot, 1), :] = tiles[s, 6:7]

        @pl.when(y == SY - 1)
        def _():
            up[pl.ds(spot, 1), :] = tiles[s, 6:7]

        return 0

    lax.fori_loop(0, number, slot, 0)


def finish(
    places, ylo, yhi, up, down, tiles, sums, old, density, accel,
    rows, cells, final, spots, tails, lists, sem, four, two, use, flags, cols, table,
):
    rows[0:Y_ROWS] = ylo[...]
    rows[Y_ROWS : 2 * Y_ROWS] = yhi[...]
    rows[2 * Y_ROWS : 3 * Y_ROWS] = down[...]
    rows[3 * Y_ROWS : 4 * Y_ROWS] = up[...]
    tails[0:16] = ylo[Y_TAIL:Y_ROWS].astype(jnp.int32)
    tails[16:32] = yhi[Y_TAIL:Y_ROWS].astype(jnp.int32)
    copy = pltpu.make_async_copy(tails, lists, sem)
    copy.start()
    density[...] = old[...]
    accel[...] = jnp.zeros(accel.shape, jnp.float32)
    wide = (SX + 2) * (SZ + 2)

    def clear(k, _):
        flags[k] = jnp.int32(0)
        return 0

    lax.fori_loop(0, 2 * wide, clear, 0, unroll=16)
    number, mine = places[3, 0], places[3, 1]

    def take(s, _):
        for c in range(3):
            spots[c, s] = places[c, s]
        cells[pl.ds(pl.multiple_of(s * 8, 8), 8), :] = tiles[s]

        @pl.when(s < mine)
        def _():
            final[s] = sums[s]

        return 0

    lax.fori_loop(0, number, take, 0)
    copy.wait()
    total = number
    for side in range(2):
        for q, (bx, bz) in enumerate(BLOCKS):
            row = side * 16 + q

            def one(s, n, row=row, side=side, bx=bx, bz=bz):
                a, b, d = corner(lists[row, s])
                x, z = a + bx * SX, d + bz * SZ
                edge = (SY - 1) if side == 0 else 0
                inside = (x >= -1) & (x <= SX) & (z >= -1) & (z <= SZ) & (b == edge)

                @pl.when(inside)
                def _():
                    spots[0, n] = x
                    spots[1, n] = jnp.int32(-1 if side == 0 else SY)
                    spots[2, n] = z
                    at = (x + 1) * (SZ + 2) + z + 1
                    flags[side * wide + at] = jnp.int32(1)
                    base = side * Y_ROWS
                    spot = pl.multiple_of(n * 8, 8)
                    row4 = base + ((x + 2) * (SZ + 4) + z + 2) * 4
                    row2 = base + Y_TWO + at * 2
                    cells[pl.ds(spot, 8), :] = jnp.concatenate(
                        [
                            rows[pl.ds(row4, 4), :],
                            rows[pl.ds(row2, 2), :],
                            rows[pl.ds(base + Y_SUM + at, 1), :],
                            jnp.zeros((1, 128), jnp.float32),
                        ],
                        axis=0,
                    )

                return n + inside.astype(jnp.int32)

            total = lax.fori_loop(0, lists[row, 15], one, total)

    def across(s, _):
        x, y, z = spots[0, s], spots[1, s], spots[2, s]
        is_mine = s < mine
        low = (y == 0) | (y == -1)
        high = (y == SY - 1) | (y == SY)
        outer = (y == -1) | (y == SY)
        base = jnp.where(outer, 2 * Y_ROWS, 0) + jnp.where(high, Y_ROWS, 0)
        side = jnp.where(high, wide, 0)

        @pl.when(low | high)
        def _():
            for e, (ea, ed) in enumerate((p, q) for p in (-1, 0, 1) for q in (-1, 0, 1)):
                na, nd = x + ea, z + ed
                at = (na + 1) * (SZ + 2) + nd + 1
                four[e] = base + ((na + 2) * (SZ + 4) + nd + 2) * 4
                two[e] = base + Y_TWO + at * 2
                known = flags[jnp.where(is_mine, side + at, 0)]
                use[e] = jnp.where(known > 0, jnp.float32(0.5), jnp.float32(1.0))
            spot = pl.multiple_of(s * 8, 8)
            tile = cells[pl.ds(spot, 8), :]
            count = jnp.int32(9)

            @pl.when(is_mine)
            def _():
                result = pairs("all", rows, four, two, use, count, tile, cols, table)
                final[s, 0:7] = final[s, 0:7] + result[0:7]
                cells[pl.ds(spot + 6, 1), :] = tile[6:7] + result[0:1]

            @pl.when(jnp.logical_not(is_mine))
            def _():
                result = pairs("density", rows, four, two, use, count, tile, cols, table)
                cells[pl.ds(spot + 6, 1), :] = tile[6:7] + result[0:1]

        return 0

    lax.fori_loop(0, total, across, 0)

    def weigh(s, _):
        spot = pl.multiple_of(s * 8, 8)
        tile = cells[pl.ds(spot, 8), :]
        inv = 1.0 / jnp.where(tile[3:4] > 0.0, tile[4:5], 1.0)
        inv2 = inv * inv
        inv4 = inv2 * inv2
        fresh = (4.0 * KC) * (inv4 * inv4) * tile[6:7]
        safe = jnp.where(tile[3:4] > 0.0, fresh, 1.0)
        power = jnp.exp(jnp.log(safe) * (-1.0 / 3.0))
        cells[pl.ds(spot + 5, 1), :] = tile[5:6] * power
        cells[pl.ds(spot + 6, 1), :] = safe
        cells[pl.ds(spot + 7, 1), :] = power
        return 0

    lax.fori_loop(0, total, weigh, 0)

    def last(s, _):
        x, y, z = spots[0, s], spots[1, s], spots[2, s]

        def check(t, n):
            close = (
                (jnp.abs(spots[0, t] - x) <= 1)
                & (jnp.abs(spots[1, t] - y) <= 1)
                & (jnp.abs(spots[2, t] - z) <= 1)
            )
            four[n] = t * 8
            two[n] = t * 8 + 4
            use[n] = jnp.float32(1.0)
            return n + close.astype(jnp.int32)

        count = lax.fori_loop(0, total, check, jnp.int32(0))
        spot = pl.multiple_of(s * 8, 8)
        tile = cells[pl.ds(spot, 8), :]
        result = final[s] + pairs("near", cells, four, two, use, count, tile, cols, table)
        good = tile[3:4] > 0.0
        own = final[s, 7:8] * tile[7:8]
        place = (x, y, pl.ds(z, 1), slice(None))
        density[place] = jnp.where(good, tile[6:7], old[place])
        for c in range(3):
            push = (20.0 * KC) * (own * final[s, 1 + c : 2 + c] + result[4 + c : 5 + c])
            accel[(c, *place)] = jnp.where(good, push, 0.0)
        return 0

    lax.fori_loop(0, mine, last, 0)


def f32(*shape):
    return jax.ShapeDtypeStruct(shape, jnp.float32)


def i32(*shape):
    return jax.ShapeDtypeStruct(shape, jnp.int32)


def neighbours(up, down, axis):
    size = lax.axis_size(axis)
    pairs_ = [(i, i + 1) for i in range(size - 1)]
    low = lax.ppermute(up, axis, pairs_)
    high = lax.ppermute(down, axis, [(j, i) for i, j in pairs_])
    return low, high


def work(flags, near):
    return [
        pltpu.SMEM((near,), jnp.int32),
        pltpu.SMEM((near,), jnp.int32),
        pltpu.SMEM((near,), jnp.float32),
        pltpu.SMEM((flags,), jnp.int32),
        pltpu.VMEM((128, 128), jnp.float32),
        pltpu.VMEM((128, 128), jnp.float32),
    ]


def cost(us):
    return pl.CostEstimate(flops=us * 10_000_000, bytes_accessed=us * 2_000_000, transcendentals=0)


def call(body, outs, out_specs, in_specs, scratch, us):
    return pl.pallas_call(
        body,
        out_shape=outs,
        in_specs=in_specs,
        out_specs=out_specs,
        scratch_shapes=scratch,
        compiler_params=PARAMS,
        cost_estimate=cost(us),
    )


def per_device(positions, mass, support, counts, entropy, density_old, active):
    small = [jnp.transpose(v, (1, 2, 0)) for v in (counts, active)]
    own, z_up, z_down, ids = call(
        pack,
        (f32(OWN_ROWS, S), f32(Z_ROWS, S), f32(Z_ROWS, S), i32(16)),
        (VMEM, VMEM, VMEM, SMEM),
        [SMEM, SMEM] + [VMEM] * 5,
        [],
        2,
    )(*small, positions, mass, support, entropy, density_old)
    zlo, zhi = neighbours(z_up, z_down, "gz")
    first = call(
        local_first, f32(16, 8, S), VMEM, [SMEM, VMEM], work(CELLS, 32), 8
    )(ids, own)
    x_up, x_down = call(
        pack_x, (f32(X_ROWS, S), f32(X_ROWS, S)), (VMEM, VMEM), [VMEM] * 3, [], 1
    )(own, zlo, zhi)
    xlo, xhi = neighbours(x_up, x_down, "gx")
    second = call(
        local_second,
        f32(16, 8, S),
        VMEM,
        [SMEM, VMEM, VMEM, pl.BlockSpec(memory_space=pl.ANY)],
        work(CELLS, 32),
        8,
    )(ids, own, first, x_up)
    y_up, y_down, tiles, sums, places = call(
        slab,
        (f32(Y_ROWS, S), f32(Y_ROWS, S), f32(SLAB_MOST, 8, S), f32(16, 8, S), i32(4, 128)),
        (VMEM, VMEM, VMEM, VMEM, SMEM),
        [SMEM] + [VMEM] * 6,
        [
            pltpu.VMEM((SLAB, S), jnp.float32),
            pltpu.VMEM((16, S), jnp.int32),
            pltpu.SMEM((16, S), jnp.int32),
            pltpu.SemaphoreType.DMA,
        ]
        + work((SX + 2) * SY * (SZ + 2), 32),
        4,
    )(ids, own, zlo, zhi, xlo, xhi, second)
    ylo, yhi = neighbours(y_up, y_down, "gy")
    return call(
        finish,
        (f32(SX, SY, SZ, S), f32(3, SX, SY, SZ, S)),
        (VMEM, VMEM),
        [SMEM] + [VMEM] * 7,
        [
            pltpu.VMEM((4 * Y_ROWS, S), jnp.float32),
            pltpu.VMEM((ALL_MOST * 8, S), jnp.float32),
            pltpu.VMEM((16, 8, S), jnp.float32),
            pltpu.SMEM((4, ALL_MOST), jnp.int32),
            pltpu.VMEM((32, S), jnp.int32),
            pltpu.SMEM((32, S), jnp.int32),
            pltpu.SemaphoreType.DMA,
        ]
        + work(2 * (SX + 2) * (SZ + 2), ALL_MOST + 16),
        8,
    )(places, ylo, yhi, y_up, y_down, tiles, sums, density_old)


def solution(mesh):
    return jax.shard_map(
        per_device,
        mesh=mesh,
        in_specs=(
            P(None, "gx", "gy", "gz", None),
            P("gx", "gy", "gz", None),
            P("gx", "gy", "gz", None),
            P("gx", "gy", "gz"),
            P("gx", "gy", "gz", None),
            P("gx", "gy", "gz", None),
            P("gx", "gy", "gz"),
        ),
        out_specs=(P("gx", "gy", "gz", None), P(None, "gx", "gy", "gz", None)),
        check_vma=False,
    )
```

```python
import functools
import math

import jax
import jax.numpy as jnp
from jax import lax
from jax.experimental import pallas as pl
from jax.experimental.pallas import tpu as pltpu
from jax.sharding import PartitionSpec as P

KC = 21.0 / (2.0 * math.pi)
SX, SY, SZ, S = 12, 6, 6, 128
MOST = 9
CELLS = SX * SY * SZ

ZERO = CELLS * 8
OWN_TAIL = ZERO + 8
OWN_ROWS = OWN_TAIL + 8

Z_TWO, Z_FAR, Z_TAIL, Z_ROWS = 288, 432, 720, 728
X_TWO, X_FAR, X_TAIL, X_ROWS = 240, 336, 576, 584
Y_TWO, Y_SUM, Y_TAIL, Y_ROWS = 640, 864, 976, 984

ZLO = OWN_ROWS
ZHI = ZLO + Z_ROWS
XLO = ZHI + Z_ROWS
XHI = XLO + X_ROWS
SLAB = XHI + X_ROWS

SLAB_MOST = 96
ALL_MOST = 256

VMEM = pl.BlockSpec(memory_space=pltpu.VMEM)
SMEM = pl.BlockSpec(memory_space=pltpu.SMEM)
ANY = pl.BlockSpec(memory_space=pl.ANY)
PARAMS = pltpu.CompilerParams(vmem_limit_bytes=40 * 1024 * 1024)

BLOCKS = [(0, 0), (0, -1), (0, 1), (-1, 0), (-1, -1), (-1, 1), (1, 0), (1, -1), (1, 1)]


def step(mode, i, near, sums):
    xi, yi, zi, hi, bi = i
    xj, yj, zj, mj, hj, wj = near
    dx, dy, dz = xi - xj, yi - yj, zi - zj
    sq = jnp.maximum(dx * dx + dy * dy + dz * dz, 1e-30)
    dist = sq * lax.rsqrt(sq)
    out = []
    if mode != "near":
        wi = jnp.maximum(hi - dist, 0.0)
        own = mj * (wi * wi * wi)
        out.append(sums[0] + own * (wi * (bi - wi)))
        if mode == "all":
            out += [sums[1] + own * dx, sums[2] + own * dy, sums[3] + own * dz]
    if mode != "density":
        wj_ = jnp.maximum(hj - dist, 0.0)
        other = wj * (wj_ * wj_ * wj_)
        last = sums[-3:]
        out += [last[0] + other * dx, last[1] + other * dy, last[2] + other * dz]
    return tuple(out)


WIDTH = {"all": 7, "density": 1, "near": 3}
FIRST = {"all": 0, "density": 0, "near": 4}
NEAR = {"all": 3, "density": 9, "near": 1}
GROUPS = {"all": 2, "density": 2, "near": 8}


def pairs(mode, src, four, two, use, count, tile, cols, table):
    many, regs = NEAR[mode], GROUPS[mode]
    for u in range(many - 1):
        four[count + u] = jnp.int32(0)
        two[count + u] = jnp.int32(0)
        use[count + u] = jnp.float32(0.0)
    steps = lax.div(count + (many - 1), many)
    used = jnp.sum(jnp.where(tile[3:4] > 0.0, 1.0, 0.0)).astype(jnp.int32)
    for n, c in enumerate((0, 1, 2, 4)):
        if mode == "near" and n == 3:
            break
        cols[n] = jnp.broadcast_to(tile[c : c + 1], (128, 128)).T
    width = WIDTH[mode]
    zero = jnp.zeros((8, 128), jnp.float32)

    def group(g, _):
        spots, own = [], []
        for v in range(regs):
            spot = pl.ds(pl.multiple_of((g * regs + v) * 8, 8), 8)
            x, y, z = [cols[n, spot, :] for n in range(3)]
            h = cols[3, spot, :] if mode != "near" else None
            spots.append(spot)
            own.append((x, y, z, h, 1.25 * h if mode != "near" else None))

        def body(q, sums):
            sums = list(sums)
            for u in range(many):
                at = q * many + u
                f = four[at]
                near = [
                    jnp.broadcast_to(src[pl.ds(f + c, 1), :], (8, 128)) for c in range(4)
                ]
                flag = use[at]
                if mode != "near":
                    near[3] = near[3] * jnp.where(flag >= 0.5, 1.0, 0.0)
                if mode != "density":
                    t = two[at]
                    near.append(jnp.broadcast_to(src[pl.ds(t, 1), :], (8, 128)))
                    weight = jnp.broadcast_to(src[pl.ds(t + 1, 1), :], (8, 128))
                    near.append(weight * jnp.where(flag == 1.0, 1.0, 0.0))
                else:
                    near += [None, None]
                for v in range(regs):
                    sums[v] = step(mode, own[v], near, sums[v])
            return tuple(sums)

        sums = lax.fori_loop(0, steps, body, ((zero,) * width,) * regs)
        for v in range(regs):
            for c in range(width):
                table[c, spots[v], :] = sums[v][c]
        return 0

    lax.fori_loop(0, lax.div(used + (8 * regs - 1), 8 * regs), group, 0)
    lines = [jnp.sum(table[c].T, axis=0, keepdims=True) for c in range(width)]
    if mode == "density":
        return lines[0]
    before = [jnp.zeros((1, 128), jnp.float32)] * FIRST[mode]
    after = [jnp.zeros((1, 128), jnp.float32)] * (8 - FIRST[mode] - width)
    return jnp.concatenate(before + lines + after, axis=0)


def bit(word, at):
    return lax.shift_right_logical(word, at) & 1


def clear(words, count):
    def one(k, _):
        words[k] = jnp.int32(0)
        return 0

    lax.fori_loop(0, count, one, 0, unroll=14)


def mark(words, at, place):
    words[at] = words[at] | lax.shift_left(jnp.int32(1), place)


def corner(k):
    return lax.div(k, SY * SZ), lax.rem(lax.div(k, SZ), SY), lax.rem(k, SZ)


def pack(
    counts_in, active_in, pos_in, mass_in, support_in, entropy_in, old_in, own, up, down, ids,
    counts, active, pos, mass, support, entropy, old, sems,
):
    given = (active_in, counts_in, pos_in, mass_in, support_in, entropy_in, old_in)
    held = (active, counts, pos, mass, support, entropy, old)
    copies = [pltpu.make_async_copy(a, b, sems.at[n]) for n, (a, b) in enumerate(zip(given, held))]
    for copy in copies:
        copy.start()
    copies[0].wait()

    def scan(q, n):
        y, z = lax.div(q, SZ), lax.rem(q, SZ)
        for x in range(SX):
            ids[n] = (x * SY + y) * SZ + z
            n = n + active[y, z, x]
        return n

    number = lax.fori_loop(0, SY * SZ, scan, jnp.int32(0))
    for s in range(MOST, 15):
        ids[s] = jnp.int32(0)
    ids[15] = number
    lane = lax.broadcasted_iota(jnp.int32, (8, 128), 1)
    tail = jnp.zeros((8, 128), jnp.int32)
    for s in range(MOST):
        tail = jnp.where(lane == s, ids[s], tail)
    tail = jnp.where(lane == 15, number, tail).astype(jnp.float32)
    own[ZERO : ZERO + 8] = jnp.zeros((8, 128), jnp.float32)
    own[OWN_TAIL : OWN_TAIL + 8] = tail
    up[Z_TAIL : Z_TAIL + 8] = tail
    down[Z_TAIL : Z_TAIL + 8] = tail
    for copy in copies[1:]:
        copy.wait()
    sub = lax.broadcasted_iota(jnp.int32, (SZ, 128), 0)
    slot = lax.broadcasted_iota(jnp.int32, (SZ, 128), 1)

    def cells(x, _):
        for y in range(SY):
            many = jnp.zeros((SZ, 128), jnp.int32)
            act = jnp.zeros((SZ, 128), jnp.int32)
            for z in range(SZ):
                many = jnp.where(sub == z, counts[y, z, x], many)
                act = jnp.where(sub == z, active[y, z, x], act)
            h = support[x, y]
            inv = 1.0 / h
            inv2 = inv * inv
            inv4 = inv2 * inv2
            m = jnp.where(slot < many, mass[x, y], 0.0)
            gain = entropy[x, y] * (inv4 * inv4)
            power = jnp.exp(jnp.log(old[x, y]) * (-1.0 / 3.0))
            weight = m * gain * jnp.where(act > 0, 1.0, power)
            base = pl.multiple_of(x * (SY * SZ * 8), 8) + y * SZ * 8
            for c, value in enumerate(
                (pos[0, x, y], pos[1, x, y], pos[2, x, y], m, h, weight, gain)
            ):
                own[pl.ds(base + c, SZ, stride=8), :] = value
        return 0

    lax.fori_loop(0, SX, cells, 0)

    def faces(x2, _):
        for u in range(2):
            for y in range(SY):
                base = pl.multiple_of(x2 * (2 * SY * SZ * 8), 8) + (u * SY + y) * SZ * 8
                four = pl.multiple_of(x2 * (2 * SY * 4), 8) + (u * SY + y) * 4
                two = pl.multiple_of(x2 * (2 * SY * 2), 8) + (u * SY + y) * 2
                for out, z1, z2 in ((up, SZ - 1, SZ - 2), (down, 0, 1)):
                    out[pl.ds(four, 4), :] = own[pl.ds(base + z1 * 8, 4), :]
                    out[pl.ds(two + Z_TWO, 2), :] = own[pl.ds(base + z1 * 8 + 4, 2), :]
                    out[pl.ds(four + Z_FAR, 4), :] = own[pl.ds(base + z2 * 8, 4), :]
        return 0

    lax.fori_loop(0, SX // 2, faces, 0)


def own_row(x, y, z):
    return ((x * SY + y) * SZ + z) * 8


def local(part, ids, own, before, sums, four, two, use, flags, cols, table):
    number = ids[15]
    half = lax.div(number + 1, 2)

    clear(flags, SX * SY)

    def one(s, _):
        k = ids[s]
        mark(flags, lax.div(k, SZ), lax.rem(k, SZ))
        return 0

    lax.fori_loop(0, number, one, 0)
    if before is not None:
        sums[...] = before[...]

    def slot(s, _):
        k = ids[s]
        a, b, d = corner(k)
        count = jnp.int32(0)
        in_z = [(d + ed >= 0) & (d + ed < SZ) for ed in (-1, 0, 1)]
        for ea in (-1, 0, 1):
            for eb in (-1, 0, 1):
                na, nb = a + ea, b + eb
                inside = (na >= 0) & (na < SX) & (nb >= 0) & (nb < SY)
                column = na * SY + nb
                word = flags[jnp.where(inside, column, 0)]
                row = column * (SZ * 8) + d * 8
                for n, ed in enumerate((-1, 0, 1)):
                    four[count] = row + ed * 8
                    two[count] = row + (ed * 8 + 4)
                    known = bit(word, jnp.maximum(d + ed, 0))
                    use[count] = jnp.where(known > 0, jnp.float32(0.5), jnp.float32(1.0))
                    count = count + (inside & in_z[n]).astype(jnp.int32)
        row = pl.multiple_of(k * 8, 8)
        tile = own[pl.ds(row, 8), :]
        sums[s] = pairs("all", own, four, two, use, count, tile, cols, table)
        return 0

    if part == 0:
        lax.fori_loop(0, half, slot, 0)
    else:
        lax.fori_loop(half, number, slot, 0)


def local_first(ids, own, sums, *scratch):
    local(0, ids, own, None, sums, *scratch)


def local_second(ids, own, before, _, sums, *scratch):
    local(1, ids, own, before, sums, *scratch)


def pack_x(own, zlo, zhi, _, up, down):
    for out, x1, x2 in ((up, SX - 1, SX - 2), (down, 0, 1)):
        for y in range(SY):
            for z in range(-2, SZ + 2):
                for x, base in ((x1, 0), (x2, X_FAR)):
                    spot = base + (y * (SZ + 4) + z + 2) * 4
                    if 0 <= z < SZ:
                        row = own_row(x, y, z)
                        out[spot : spot + 4] = own[row : row + 4]
                    else:
                        src = zlo if z < 0 else zhi
                        far = Z_FAR if z in (-2, SZ + 1) else 0
                        row = far + (x * SY + y) * 4
                        out[spot : spot + 4] = src[row : row + 4]
                if -1 <= z <= SZ:
                    spot = X_TWO + (y * (SZ + 2) + z + 1) * 2
                    if 0 <= z < SZ:
                        row = own_row(x1, y, z) + 4
                        out[spot : spot + 2] = own[row : row + 2]
                    else:
                        src = zlo if z < 0 else zhi
                        row = Z_TWO + (x1 * SY + y) * 2
                        out[spot : spot + 2] = src[row : row + 2]
        out[X_TAIL : X_TAIL + 8] = jnp.zeros((8, 128), jnp.float32)
        out[X_TAIL : X_TAIL + 1] = own[OWN_TAIL : OWN_TAIL + 1]
        out[X_TAIL + 1 : X_TAIL + 2] = zlo[Z_TAIL : Z_TAIL + 1]
        out[X_TAIL + 2 : X_TAIL + 3] = zhi[Z_TAIL : Z_TAIL + 1]


def slab_rows(x, z):
    zlow, xlow = z < 0, x < 0
    zout = zlow | (z >= SZ)
    xout = xlow | (x >= SX)
    zbase = jnp.where(zlow, ZLO, ZHI)
    zfar = jnp.where((z == -2) | (z == SZ + 1), Z_FAR, 0)
    xbase = jnp.where(xlow, XLO, XHI)
    xfar = jnp.where((x == -2) | (x == SX + 1), X_FAR, 0)
    four = jnp.where(zout, zbase + zfar + x * (SY * 4), x * (SY * SZ * 8) + z * 8)
    two = jnp.where(zout, zbase + Z_TWO + x * (SY * 2), x * (SY * SZ * 8) + z * 8 + 4)
    four = jnp.where(xout, xbase + xfar + (z + 2) * 4, four)
    two = jnp.where(xout, xbase + X_TWO + (z + 1) * 2, two)
    add4 = jnp.where(xout, (SZ + 4) * 4, jnp.where(zout, 4, SZ * 8))
    add2 = jnp.where(xout, (SZ + 2) * 2, jnp.where(zout, 2, SZ * 8))
    return four, two, add4, add2


def slab_rows_at(x, y, z):
    if 0 <= x < SX and 0 <= z < SZ:
        return own_row(x, y, z), own_row(x, y, z) + 4
    if 0 <= x < SX:
        base, far, k = ZLO if z < 0 else ZHI, z in (-2, SZ + 1), x * SY + y
        return base + (Z_FAR if far else 0) + k * 4, base + Z_TWO + k * 2
    base, far = XLO if x < 0 else XHI, x in (-2, SX + 1)
    four = base + (X_FAR if far else 0) + (y * (SZ + 4) + z + 2) * 4
    return four, base + X_TWO + (y * (SZ + 2) + z + 1) * 2


def slab(
    ids, own, zlo, zhi, xlo, xhi, before, up, down, tiles, sums, places,
    rows, tails, lists, sem, four, two, use, flags, cols, table,
):
    rows[0:OWN_ROWS] = own[...]
    rows[ZLO:ZHI] = zlo[...]
    rows[ZHI:XLO] = zhi[...]
    rows[XLO:XHI] = xlo[...]
    rows[XHI:SLAB] = xhi[...]
    tails[...] = jnp.zeros(tails.shape, jnp.int32)
    tails[0:1] = own[OWN_TAIL : OWN_TAIL + 1].astype(jnp.int32)
    tails[1:2] = zlo[Z_TAIL : Z_TAIL + 1].astype(jnp.int32)
    tails[2:3] = zhi[Z_TAIL : Z_TAIL + 1].astype(jnp.int32)
    tails[3:6] = xlo[X_TAIL : X_TAIL + 3].astype(jnp.int32)
    tails[6:9] = xhi[X_TAIL : X_TAIL + 3].astype(jnp.int32)
    copy = pltpu.make_async_copy(tails, lists, sem)
    copy.start()

    clear(flags, (SX + 2) * SY)
    for out, y in ((up, SY - 1), (down, 0)):
        for x in range(-2, SX + 2):
            for z in range(-2, SZ + 2):
                row4, row2 = slab_rows_at(x, y, z)
                spot = ((x + 2) * (SZ + 4) + z + 2) * 4
                out[spot : spot + 4] = rows[row4 : row4 + 4]
                if -1 <= x <= SX and -1 <= z <= SZ:
                    spot = Y_TWO + ((x + 1) * (SZ + 2) + z + 1) * 2
                    out[spot : spot + 2] = rows[row2 : row2 + 2]
        out[Y_SUM:Y_TAIL] = jnp.zeros((Y_TAIL - Y_SUM, 128), jnp.float32)
    copy.wait()

    number = jnp.int32(0)
    for q, (bx, bz) in enumerate(BLOCKS):

        def one(s, n, q=q, bx=bx, bz=bz):
            a, b, d = corner(lists[q, s])
            x, z = a + bx * SX, d + bz * SZ
            inside = (x >= -1) & (x <= SX) & (z >= -1) & (z <= SZ)
            places[0, n] = x
            places[1, n] = b
            places[2, n] = z

            @pl.when(inside)
            def _():
                mark(flags, (x + 1) * SY + b, z + 1)

            return n + inside.astype(jnp.int32)

        number = lax.fori_loop(0, lists[q, 15], one, number)
    places[3, 0] = number
    places[3, 1] = lists[0, 15]
    mine = lists[0, 15]

    lane = lax.broadcasted_iota(jnp.int32, (8, 128), 1)
    line = lax.broadcasted_iota(jnp.int32, (8, 128), 0)

    def tell(s, state):
        lists_, numbers = list(state[0]), list(state[1])
        x, y, z = places[0, s], places[1, s], places[2, s]
        for n, edge in enumerate((SY - 1, 0)):
            here = y == edge
            at = jnp.where(here, numbers[n], 126)
            value = jnp.where(line == 0, x, z)
            lists_[n] = jnp.where(lane == at, value, lists_[n])
            numbers[n] = numbers[n] + here.astype(jnp.int32)
        return tuple(lists_), tuple(numbers)

    nothing = jnp.zeros((8, 128), jnp.int32)
    told, numbers = lax.fori_loop(
        0, number, tell, ((nothing, nothing), (jnp.int32(0), jnp.int32(0)))
    )
    for n, out in enumerate((up, down)):
        out[Y_TAIL:Y_ROWS] = jnp.where(lane == 127, numbers[n], told[n]).astype(jnp.float32)

    def near_list(x, y, z, own_cell):
        count = jnp.int32(0)
        for ea in (-1, 0, 1):
            for ed in (-1, 0, 1):
                na, nd = x + ea, z + ed
                f4, f2, add4, add2 = slab_rows(na, nd)
                if own_cell:
                    outer = (na < 0) | (na >= SX) | (nd < 0) | (nd >= SZ)
                for eb in (-1, 0, 1):
                    nb = y + eb
                    wanted = (nb >= 0) & (nb < SY)
                    four[count] = f4 + nb * add4
                    if own_cell:
                        wanted = wanted & outer
                        two[count] = f2 + nb * add2
                        word = flags[(na + 1) * SY + jnp.where(wanted, nb, 0)]
                        known = bit(word, nd + 1)
                        use[count] = jnp.where(known > 0, jnp.float32(0.5), jnp.float32(1.0))
                    else:
                        use[count] = jnp.float32(1.0)
                    count = count + wanted.astype(jnp.int32)
        return count

    def cell(x, y, z):
        f4, f2, add4, add2 = slab_rows(x, z)
        first = rows[pl.ds(f4 + y * add4, 4), :]
        second = rows[pl.ds(f2 + y * add2, 2), :]
        return jnp.concatenate([first, second, jnp.zeros((2, 128), jnp.float32)], axis=0)

    def send_sum(s, x, y, z):
        spot = Y_SUM + (x + 1) * (SZ + 2) + z + 1

        @pl.when(y == 0)
        def _():
            down[pl.ds(spot, 1), :] = tiles[s, 6:7]

        @pl.when(y == SY - 1)
        def _():
            up[pl.ds(spot, 1), :] = tiles[s, 6:7]

    def own_slot(s, _):
        x, y, z = places[0, s], places[1, s], places[2, s]
        sums[s] = before[s]

        @pl.when((x == 0) | (x == SX - 1) | (z == 0) | (z == SZ - 1))
        def _():
            count = near_list(x, y, z, True)
            tile = cell(x, y, z)
            sums[s] = sums[s] + pairs("all", rows, four, two, use, count, tile, cols, table)

        row = pl.multiple_of(own_row(x, y, z), 8)
        whole = rows[pl.ds(row, 8), :]
        tiles[s] = whole
        tiles[s, 6:7] = sums[s, 0:1]
        sums[s, 7:8] = whole[6:7]
        send_sum(s, x, y, z)
        return 0

    def halo_slot(s, _):
        x, y, z = places[0, s], places[1, s], places[2, s]
        count = near_list(x, y, z, False)
        tile = cell(x, y, z)
        tiles[s] = tile
        tiles[s, 6:7] = pairs("density", rows, four, two, use, count, tile, cols, table)
        send_sum(s, x, y, z)
        return 0

    lax.fori_loop(0, mine, own_slot, 0)
    lax.fori_loop(mine, number, halo_slot, 0)


def finish(
    places, ylo, yhi, up, down, tiles, sums, old, density, accel,
    rows, cells, final, spots, tails, lists, sem, four, two, use, flags, cols, table,
):
    tails[0:8] = ylo[Y_TAIL:Y_ROWS].astype(jnp.int32)
    tails[8:16] = yhi[Y_TAIL:Y_ROWS].astype(jnp.int32)
    copy = pltpu.make_async_copy(tails, lists, sem)
    copy.start()
    rows[0:Y_ROWS] = ylo[...]
    rows[Y_ROWS : 2 * Y_ROWS] = yhi[...]
    rows[2 * Y_ROWS : 3 * Y_ROWS] = down[...]
    rows[3 * Y_ROWS : 4 * Y_ROWS] = up[...]
    density[...] = old[...]
    accel[...] = jnp.zeros(accel.shape, jnp.float32)
    clear(flags, 2 * (SX + 2))
    number, mine = places[3, 0], places[3, 1]

    def take(s, _):
        for c in range(3):
            spots[c, s] = places[c, s]
        cells[pl.ds(pl.multiple_of(s * 8, 8), 8), :] = tiles[s]
        return 0

    lax.fori_loop(0, number, take, 0)
    final[...] = sums[...]
    copy.wait()
    total = number
    for side in range(2):

        def one(s, n, side=side):
            x, z = lists[side * 8, s], lists[side * 8 + 1, s]
            spots[0, n] = x
            spots[1, n] = jnp.int32(-1 if side == 0 else SY)
            spots[2, n] = z
            mark(flags, side * (SX + 2) + x + 1, z + 1)
            at = (x + 1) * (SZ + 2) + z + 1
            base = side * Y_ROWS
            row4 = base + ((x + 2) * (SZ + 4) + z + 2) * 4
            row2 = base + Y_TWO + at * 2
            cells[pl.ds(pl.multiple_of(n * 8, 8), 8), :] = jnp.concatenate(
                [
                    rows[pl.ds(row4, 4), :],
                    rows[pl.ds(row2, 2), :],
                    rows[pl.ds(base + Y_SUM + at, 1), :],
                    jnp.zeros((1, 128), jnp.float32),
                ],
                axis=0,
            )
            return n + 1

        total = lax.fori_loop(0, lists[side * 8, 127], one, total)

    def near_list(s, own_cell):
        x, y, z = spots[0, s], spots[1, s], spots[2, s]
        high = y >= SY - 1
        outer = (y == -1) | (y == SY)
        base = jnp.where(outer, 2 * Y_ROWS, 0) + jnp.where(high, Y_ROWS, 0)
        for e, (ea, ed) in enumerate((p, q) for p in (-1, 0, 1) for q in (-1, 0, 1)):
            na, nd = x + ea, z + ed
            four[e] = base + ((na + 2) * (SZ + 4) + nd + 2) * 4
            use[e] = jnp.float32(1.0)
            if own_cell:
                two[e] = base + Y_TWO + ((na + 1) * (SZ + 2) + nd + 1) * 2
                word = flags[jnp.where(high, SX + 2, 0) + na + 1]
                use[e] = jnp.where(bit(word, nd + 1) > 0, jnp.float32(0.5), jnp.float32(1.0))

    def across_own(s, _):
        y = spots[1, s]

        @pl.when((y <= 0) | (y >= SY - 1))
        def _():
            near_list(s, True)
            spot = pl.multiple_of(s * 8, 8)
            tile = cells[pl.ds(spot, 8), :]
            count = jnp.int32(9)
            result = pairs("all", rows, four, two, use, count, tile, cols, table)
            final[s, 0:7] = final[s, 0:7] + result[0:7]
            cells[pl.ds(spot + 6, 1), :] = tile[6:7] + result[0:1]

        return 0

    def across_halo(s, _):
        y = spots[1, s]

        @pl.when((y <= 0) | (y >= SY - 1))
        def _():
            near_list(s, False)
            spot = pl.multiple_of(s * 8, 8)
            tile = cells[pl.ds(spot, 8), :]
            count = jnp.int32(9)
            result = pairs("density", rows, four, two, use, count, tile, cols, table)
            cells[pl.ds(spot + 6, 1), :] = tile[6:7] + result

        return 0

    lax.fori_loop(0, mine, across_own, 0)
    lax.fori_loop(mine, total, across_halo, 0)

    def weigh(q, _):
        base = pl.multiple_of(q * 64, 64)

        def get(c):
            return cells[pl.ds(base + c, 8, stride=8), :]

        good = get(3) > 0.0
        inv = 1.0 / jnp.where(good, get(4), 1.0)
        inv2 = inv * inv
        inv4 = inv2 * inv2
        fresh = (4.0 * KC) * (inv4 * inv4) * get(6)
        safe = jnp.where(good, fresh, 1.0)
        power = jnp.exp(jnp.log(safe) * (-1.0 / 3.0))
        weight = get(5) * power
        cells[pl.ds(base + 5, 8, stride=8), :] = jnp.where(good, weight, 0.0)
        cells[pl.ds(base + 6, 8, stride=8), :] = safe
        cells[pl.ds(base + 7, 8, stride=8), :] = power
        return 0

    lax.fori_loop(0, lax.div(total + 7, 8), weigh, 0)

    def last(s, _):
        x, y, z = spots[0, s], spots[1, s], spots[2, s]

        def check(t, n):
            close = (
                (jnp.abs(spots[0, t] - x) <= 1)
                & (jnp.abs(spots[1, t] - y) <= 1)
                & (jnp.abs(spots[2, t] - z) <= 1)
            )
            four[n] = t * 8
            two[n] = t * 8 + 4
            use[n] = jnp.float32(1.0)
            return n + close.astype(jnp.int32)

        count = lax.fori_loop(0, total, check, jnp.int32(0))
        spot = pl.multiple_of(s * 8, 8)
        tile = cells[pl.ds(spot, 8), :]
        result = final[s] + pairs("near", cells, four, two, use, count, tile, cols, table)
        good = tile[3:4] > 0.0
        own = final[s, 7:8] * tile[7:8]
        place = (x, y, pl.ds(z, 1), slice(None))
        density[place] = jnp.where(good, tile[6:7], old[place])
        for c in range(3):
            push = (20.0 * KC) * (own * final[s, 1 + c : 2 + c] + result[4 + c : 5 + c])
            accel[(c, *place)] = jnp.where(good, push, 0.0)
        return 0

    lax.fori_loop(0, mine, last, 0)


def f32(*shape):
    return jax.ShapeDtypeStruct(shape, jnp.float32)


def i32(*shape):
    return jax.ShapeDtypeStruct(shape, jnp.int32)


def neighbours(up, down, axis):
    size = lax.axis_size(axis)
    pairs_ = [(i, i + 1) for i in range(size - 1)]
    low = lax.ppermute(up, axis, pairs_)
    high = lax.ppermute(down, axis, [(j, i) for i, j in pairs_])
    return low, high


def work(flags, near):
    return [
        pltpu.SMEM((near,), jnp.int32),
        pltpu.SMEM((near,), jnp.int32),
        pltpu.SMEM((near,), jnp.float32),
        pltpu.SMEM((flags,), jnp.int32),
        pltpu.VMEM((4, 128, 128), jnp.float32),
        pltpu.VMEM((7, 128, 128), jnp.float32),
    ]


def cost(us):
    return pl.CostEstimate(flops=us * 10_000_000, bytes_accessed=us * 2_000_000, transcendentals=0)


def call(body, outs, out_specs, in_specs, scratch, us):
    return pl.pallas_call(
        body,
        out_shape=outs,
        in_specs=in_specs,
        out_specs=out_specs,
        scratch_shapes=scratch,
        compiler_params=PARAMS,
        cost_estimate=cost(us),
    )


def per_device(positions, mass, support, counts, entropy, density_old, active):
    small = [jnp.transpose(v, (1, 2, 0)) for v in (counts, active)]
    own, z_up, z_down, ids = call(
        pack,
        (f32(OWN_ROWS, S), f32(Z_ROWS, S), f32(Z_ROWS, S), i32(16)),
        (VMEM, VMEM, VMEM, SMEM),
        [ANY] * 7,
        [
            pltpu.SMEM((SY, SZ, SX), jnp.int32),
            pltpu.SMEM((SY, SZ, SX), jnp.int32),
            pltpu.VMEM((3, SX, SY, SZ, S), jnp.float32),
        ]
        + [pltpu.VMEM((SX, SY, SZ, S), jnp.float32)] * 4
        + [pltpu.SemaphoreType.DMA((7,))],
        2,
    )(*small, positions, mass, support, entropy, density_old)
    zlo, zhi = neighbours(z_up, z_down, "gz")
    first = call(
        local_first, f32(16, 8, S), VMEM, [SMEM, VMEM], work(SX * SY, 48), 8
    )(ids, own)
    x_up, x_down = call(
        pack_x, (f32(X_ROWS, S), f32(X_ROWS, S)), (VMEM, VMEM), [VMEM] * 3 + [ANY], [], 1
    )(own, zlo, zhi, first)
    xlo, xhi = neighbours(x_up, x_down, "gx")
    second = call(
        local_second,
        f32(16, 8, S),
        VMEM,
        [SMEM, VMEM, VMEM, ANY],
        work(SX * SY, 48),
        8,
    )(ids, own, first, x_up)
    y_up, y_down, tiles, sums, places = call(
        slab,
        (f32(Y_ROWS, S), f32(Y_ROWS, S), f32(SLAB_MOST, 8, S), f32(16, 8, S), i32(4, 128)),
        (VMEM, VMEM, VMEM, VMEM, SMEM),
        [SMEM] + [VMEM] * 6,
        [
            pltpu.VMEM((SLAB, S), jnp.float32),
            pltpu.VMEM((16, S), jnp.int32),
            pltpu.SMEM((16, S), jnp.int32),
            pltpu.SemaphoreType.DMA,
        ]
        + work((SX + 2) * SY, 48),
        4,
    )(ids, own, zlo, zhi, xlo, xhi, second)
    ylo, yhi = neighbours(y_up, y_down, "gy")
    return call(
        finish,
        (f32(SX, SY, SZ, S), f32(3, SX, SY, SZ, S)),
        (VMEM, VMEM),
        [SMEM] + [VMEM] * 7,
        [
            pltpu.VMEM((4 * Y_ROWS, S), jnp.float32),
            pltpu.VMEM((ALL_MOST * 8, S), jnp.float32),
            pltpu.VMEM((16, 8, S), jnp.float32),
            pltpu.SMEM((4, ALL_MOST), jnp.int32),
            pltpu.VMEM((16, S), jnp.int32),
            pltpu.SMEM((16, S), jnp.int32),
            pltpu.SemaphoreType.DMA,
        ]
        + work(2 * (SX + 2), ALL_MOST + 16),
        8,
    )(places, ylo, yhi, y_up, y_down, tiles, sums, density_old)


def solution(mesh):
    return jax.shard_map(
        per_device,
        mesh=mesh,
        in_specs=(
            P(None, "gx", "gy", "gz", None),
            P("gx", "gy", "gz", None),
            P("gx", "gy", "gz", None),
            P("gx", "gy", "gz"),
            P("gx", "gy", "gz", None),
            P("gx", "gy", "gz", None),
            P("gx", "gy", "gz"),
        ),
        out_specs=(P("gx", "gy", "gz", None), P(None, "gx", "gy", "gz", None)),
        check_vma=False,
    )
```

```python
import functools
import math

import jax
import jax.numpy as jnp
from jax import lax
from jax.experimental import pallas as pl
from jax.experimental.pallas import tpu as pltpu
from jax.sharding import PartitionSpec as P

KC = 21.0 / (2.0 * math.pi)
SX, SY, SZ, S = 12, 6, 6, 128
MOST = 9
CELLS = SX * SY * SZ

ZERO = CELLS * 8
OWN_TAIL = ZERO + 8
OWN_ROWS = OWN_TAIL + 8

Z_TWO, Z_FAR, Z_TAIL, Z_ROWS = 288, 432, 720, 728
X_TWO, X_FAR, X_TAIL, X_ROWS = 240, 336, 576, 584
Y_TWO, Y_SUM, Y_TAIL, Y_ROWS = 640, 864, 976, 984

ZLO = OWN_ROWS
ZHI = ZLO + Z_ROWS
XLO = ZHI + Z_ROWS
XHI = XLO + X_ROWS
SLAB = XHI + X_ROWS

SLAB_MOST = 96
ALL_MOST = 256

VMEM = pl.BlockSpec(memory_space=pltpu.VMEM)
SMEM = pl.BlockSpec(memory_space=pltpu.SMEM)
ANY = pl.BlockSpec(memory_space=pl.ANY)
PARAMS = pltpu.CompilerParams(vmem_limit_bytes=40 * 1024 * 1024)

BLOCKS = [(0, 0), (0, -1), (0, 1), (-1, 0), (-1, -1), (-1, 1), (1, 0), (1, -1), (1, 1)]


def step(mode, i, near, sums):
    xi, yi, zi, hi, bi = i
    xj, yj, zj, mj, hj, wj = near
    dx, dy, dz = xi - xj, yi - yj, zi - zj
    sq = jnp.maximum(dx * dx + dy * dy + dz * dz, 1e-30)
    dist = sq * lax.rsqrt(sq)
    out = []
    if mode != "near":
        wi = jnp.maximum(hi - dist, 0.0)
        own = mj * (wi * wi * wi)
        out.append(sums[0] + own * (wi * (bi - wi)))
        if mode == "all":
            out += [sums[1] + own * dx, sums[2] + own * dy, sums[3] + own * dz]
    if mode != "density":
        wj_ = jnp.maximum(hj - dist, 0.0)
        other = wj * (wj_ * wj_ * wj_)
        last = sums[-3:]
        out += [last[0] + other * dx, last[1] + other * dy, last[2] + other * dz]
    return tuple(out)


WIDTH = {"all": 7, "density": 1, "near": 3}
FIRST = {"all": 0, "density": 0, "near": 4}
NEAR = {"all": 3, "density": 9, "near": 1}
GROUPS = {"all": 2, "density": 2, "near": 8}


def pairs(mode, src, four, two, use, count, tile, cols, table):
    many, regs = NEAR[mode], GROUPS[mode]
    for u in range(many - 1):
        four[count + u] = jnp.int32(0)
        two[count + u] = jnp.int32(0)
        use[count + u] = jnp.float32(0.0)
    steps = lax.div(count + (many - 1), many)
    used = jnp.sum(jnp.where(tile[3:4] > 0.0, 1.0, 0.0)).astype(jnp.int32)
    for n, c in enumerate((0, 1, 2, 4)):
        if mode == "near" and n == 3:
            break
        cols[n] = jnp.broadcast_to(tile[c : c + 1], (128, 128)).T
    width = WIDTH[mode]
    zero = jnp.zeros((8, 128), jnp.float32)

    def group(g, _):
        spots, own = [], []
        for v in range(regs):
            spot = pl.ds(pl.multiple_of((g * regs + v) * 8, 8), 8)
            x, y, z = [cols[n, spot, :] for n in range(3)]
            h = cols[3, spot, :] if mode != "near" else None
            spots.append(spot)
            own.append((x, y, z, h, 1.25 * h if mode != "near" else None))

        def body(q, sums):
            sums = list(sums)
            for u in range(many):
                at = q * many + u
                f = four[at]
                near = [
                    jnp.broadcast_to(src[pl.ds(f + c, 1), :], (8, 128)) for c in range(4)
                ]
                flag = use[at]
                if mode != "near":
                    near[3] = near[3] * jnp.where(flag >= 0.5, 1.0, 0.0)
                if mode != "density":
                    t = two[at]
                    near.append(jnp.broadcast_to(src[pl.ds(t, 1), :], (8, 128)))
                    weight = jnp.broadcast_to(src[pl.ds(t + 1, 1), :], (8, 128))
                    near.append(weight * jnp.where(flag == 1.0, 1.0, 0.0))
                else:
                    near += [None, None]
                for v in range(regs):
                    sums[v] = step(mode, own[v], near, sums[v])
            return tuple(sums)

        sums = lax.fori_loop(0, steps, body, ((zero,) * width,) * regs)
        for v in range(regs):
            for c in range(width):
                table[c, spots[v], :] = sums[v][c]
        return 0

    lax.fori_loop(0, lax.div(used + (8 * regs - 1), 8 * regs), group, 0)
    lines = [jnp.sum(table[c].T, axis=0, keepdims=True) for c in range(width)]
    if mode == "density":
        return lines[0]
    before = [jnp.zeros((1, 128), jnp.float32)] * FIRST[mode]
    after = [jnp.zeros((1, 128), jnp.float32)] * (8 - FIRST[mode] - width)
    return jnp.concatenate(before + lines + after, axis=0)


def bit(word, at):
    return lax.shift_right_logical(word, at) & 1


def clear(words, count):
    def one(k, _):
        words[k] = jnp.int32(0)
        return 0

    lax.fori_loop(0, count, one, 0, unroll=14)


def mark(words, at, place):
    words[at] = words[at] | lax.shift_left(jnp.int32(1), place)


def corner(k):
    return lax.div(k, SY * SZ), lax.rem(lax.div(k, SZ), SY), lax.rem(k, SZ)


def pack(
    counts_in, active_in, pos_in, mass_in, support_in, entropy_in, old_in, own, up, down, ids,
    counts, active, pos, mass, support, entropy, old, sems,
):
    given = (active_in, counts_in, pos_in, mass_in, support_in, entropy_in, old_in)
    held = (active, counts, pos, mass, support, entropy, old)
    copies = [pltpu.make_async_copy(a, b, sems.at[n]) for n, (a, b) in enumerate(zip(given, held))]
    for copy in copies:
        copy.start()
    copies[0].wait()

    def scan(q, n):
        y, z = lax.div(q, SZ), lax.rem(q, SZ)
        for x in range(SX):
            ids[n] = (x * SY + y) * SZ + z
            n = n + active[y, z, x]
        return n

    number = lax.fori_loop(0, SY * SZ, scan, jnp.int32(0))
    for s in range(MOST, 15):
        ids[s] = jnp.int32(0)
    ids[15] = number
    lane = lax.broadcasted_iota(jnp.int32, (8, 128), 1)
    tail = jnp.zeros((8, 128), jnp.int32)
    for s in range(MOST):
        tail = jnp.where(lane == s, ids[s], tail)
    tail = jnp.where(lane == 15, number, tail).astype(jnp.float32)
    own[ZERO : ZERO + 8] = jnp.zeros((8, 128), jnp.float32)
    own[OWN_TAIL : OWN_TAIL + 8] = tail
    up[Z_TAIL : Z_TAIL + 8] = tail
    down[Z_TAIL : Z_TAIL + 8] = tail
    for copy in copies[1:]:
        copy.wait()
    sub = lax.broadcasted_iota(jnp.int32, (SZ, 128), 0)
    slot = lax.broadcasted_iota(jnp.int32, (SZ, 128), 1)

    def cells(x, _):
        for y in range(SY):
            many = jnp.zeros((SZ, 128), jnp.int32)
            act = jnp.zeros((SZ, 128), jnp.int32)
            for z in range(SZ):
                many = jnp.where(sub == z, counts[y, z, x], many)
                act = jnp.where(sub == z, active[y, z, x], act)
            h = support[x, y]
            inv = 1.0 / h
            inv2 = inv * inv
            inv4 = inv2 * inv2
            m = jnp.where(slot < many, mass[x, y], 0.0)
            gain = entropy[x, y] * (inv4 * inv4)
            power = jnp.exp(jnp.log(old[x, y]) * (-1.0 / 3.0))
            weight = m * gain * jnp.where(act > 0, 1.0, power)
            base = pl.multiple_of(x * (SY * SZ * 8), 8) + y * SZ * 8
            for c, value in enumerate(
                (pos[0, x, y], pos[1, x, y], pos[2, x, y], m, h, weight, gain)
            ):
                own[pl.ds(base + c, SZ, stride=8), :] = value
        return 0

    lax.fori_loop(0, SX, cells, 0)

    def faces(x2, _):
        for u in range(2):
            for y in range(SY):
                base = pl.multiple_of(x2 * (2 * SY * SZ * 8), 8) + (u * SY + y) * SZ * 8
                four = pl.multiple_of(x2 * (2 * SY * 4), 8) + (u * SY + y) * 4
                two = pl.multiple_of(x2 * (2 * SY * 2), 8) + (u * SY + y) * 2
                for out, z1, z2 in ((up, SZ - 1, SZ - 2), (down, 0, 1)):
                    out[pl.ds(four, 4), :] = own[pl.ds(base + z1 * 8, 4), :]
                    out[pl.ds(two + Z_TWO, 2), :] = own[pl.ds(base + z1 * 8 + 4, 2), :]
                    out[pl.ds(four + Z_FAR, 4), :] = own[pl.ds(base + z2 * 8, 4), :]
        return 0

    lax.fori_loop(0, SX // 2, faces, 0)


def own_row(x, y, z):
    return ((x * SY + y) * SZ + z) * 8


def local(part, ids, own, before, sums, four, two, use, flags, cols, table):
    number = ids[15]
    half = lax.div(number + 1, 2)

    clear(flags, SX * SY)

    def one(s, _):
        k = ids[s]
        mark(flags, lax.div(k, SZ), lax.rem(k, SZ))
        return 0

    lax.fori_loop(0, number, one, 0)
    if before is not None:
        sums[...] = before[...]

    def slot(s, _):
        k = ids[s]
        a, b, d = corner(k)
        count = jnp.int32(0)
        in_z = [(d + ed >= 0) & (d + ed < SZ) for ed in (-1, 0, 1)]
        for ea in (-1, 0, 1):
            for eb in (-1, 0, 1):
                na, nb = a + ea, b + eb
                inside = (na >= 0) & (na < SX) & (nb >= 0) & (nb < SY)
                column = na * SY + nb
                word = flags[jnp.where(inside, column, 0)]
                row = column * (SZ * 8) + d * 8
                for n, ed in enumerate((-1, 0, 1)):
                    four[count] = row + ed * 8
                    two[count] = row + (ed * 8 + 4)
                    known = bit(word, jnp.maximum(d + ed, 0))
                    use[count] = jnp.where(known > 0, jnp.float32(0.5), jnp.float32(1.0))
                    count = count + (inside & in_z[n]).astype(jnp.int32)
        row = pl.multiple_of(k * 8, 8)
        tile = own[pl.ds(row, 8), :]
        sums[s] = pairs("all", own, four, two, use, count, tile, cols, table)
        return 0

    if part == 0:
        lax.fori_loop(0, half, slot, 0)
    else:
        lax.fori_loop(half, number, slot, 0)


def local_first(ids, own, sums, *scratch):
    local(0, ids, own, None, sums, *scratch)


def local_second(ids, own, before, _, sums, *scratch):
    local(1, ids, own, before, sums, *scratch)


def pack_x(own, zlo, zhi, _, up, down):
    for out, x1, x2 in ((up, SX - 1, SX - 2), (down, 0, 1)):
        for y in range(SY):
            for z in range(-2, SZ + 2):
                for x, base in ((x1, 0), (x2, X_FAR)):
                    spot = base + (y * (SZ + 4) + z + 2) * 4
                    if 0 <= z < SZ:
                        row = own_row(x, y, z)
                        out[spot : spot + 4] = own[row : row + 4]
                    else:
                        src = zlo if z < 0 else zhi
                        far = Z_FAR if z in (-2, SZ + 1) else 0
                        row = far + (x * SY + y) * 4
                        out[spot : spot + 4] = src[row : row + 4]
                if -1 <= z <= SZ:
                    spot = X_TWO + (y * (SZ + 2) + z + 1) * 2
                    if 0 <= z < SZ:
                        row = own_row(x1, y, z) + 4
                        out[spot : spot + 2] = own[row : row + 2]
                    else:
                        src = zlo if z < 0 else zhi
                        row = Z_TWO + (x1 * SY + y) * 2
                        out[spot : spot + 2] = src[row : row + 2]
        out[X_TAIL : X_TAIL + 8] = jnp.zeros((8, 128), jnp.float32)
        out[X_TAIL : X_TAIL + 1] = own[OWN_TAIL : OWN_TAIL + 1]
        out[X_TAIL + 1 : X_TAIL + 2] = zlo[Z_TAIL : Z_TAIL + 1]
        out[X_TAIL + 2 : X_TAIL + 3] = zhi[Z_TAIL : Z_TAIL + 1]


def slab_rows(x, z):
    zlow, xlow = z < 0, x < 0
    zout = zlow | (z >= SZ)
    xout = xlow | (x >= SX)
    zbase = jnp.where(zlow, ZLO, ZHI)
    zfar = jnp.where((z == -2) | (z == SZ + 1), Z_FAR, 0)
    xbase = jnp.where(xlow, XLO, XHI)
    xfar = jnp.where((x == -2) | (x == SX + 1), X_FAR, 0)
    four = jnp.where(zout, zbase + zfar + x * (SY * 4), x * (SY * SZ * 8) + z * 8)
    two = jnp.where(zout, zbase + Z_TWO + x * (SY * 2), x * (SY * SZ * 8) + z * 8 + 4)
    four = jnp.where(xout, xbase + xfar + (z + 2) * 4, four)
    two = jnp.where(xout, xbase + X_TWO + (z + 1) * 2, two)
    add4 = jnp.where(xout, (SZ + 4) * 4, jnp.where(zout, 4, SZ * 8))
    add2 = jnp.where(xout, (SZ + 2) * 2, jnp.where(zout, 2, SZ * 8))
    return four, two, add4, add2


def slab_rows_at(x, y, z):
    if 0 <= x < SX and 0 <= z < SZ:
        return own_row(x, y, z), own_row(x, y, z) + 4
    if 0 <= x < SX:
        base, far, k = ZLO if z < 0 else ZHI, z in (-2, SZ + 1), x * SY + y
        return base + (Z_FAR if far else 0) + k * 4, base + Z_TWO + k * 2
    base, far = XLO if x < 0 else XHI, x in (-2, SX + 1)
    four = base + (X_FAR if far else 0) + (y * (SZ + 4) + z + 2) * 4
    return four, base + X_TWO + (y * (SZ + 2) + z + 1) * 2


def gather(rows, own, zlo, zhi, xlo, xhi):
    rows[0:OWN_ROWS] = own[...]
    rows[ZLO:ZHI] = zlo[...]
    rows[ZHI:XLO] = zhi[...]
    rows[XLO:XHI] = xlo[...]
    rows[XHI:SLAB] = xhi[...]


def slab_tools(rows, four, two, use, flags, cols, table):
    def near_list(x, y, z, own_cell):
        count = jnp.int32(0)
        for ea in (-1, 0, 1):
            for ed in (-1, 0, 1):
                na, nd = x + ea, z + ed
                f4, f2, add4, add2 = slab_rows(na, nd)
                if own_cell:
                    outer = (na < 0) | (na >= SX) | (nd < 0) | (nd >= SZ)
                for eb in (-1, 0, 1):
                    nb = y + eb
                    wanted = (nb >= 0) & (nb < SY)
                    four[count] = f4 + nb * add4
                    if own_cell:
                        wanted = wanted & outer
                        two[count] = f2 + nb * add2
                        word = flags[(na + 1) * SY + jnp.where(wanted, nb, 0)]
                        known = bit(word, nd + 1)
                        use[count] = jnp.where(known > 0, jnp.float32(0.5), jnp.float32(1.0))
                    else:
                        use[count] = jnp.float32(1.0)
                    count = count + wanted.astype(jnp.int32)
        return count

    def cell(x, y, z):
        f4, f2, add4, add2 = slab_rows(x, z)
        first = rows[pl.ds(f4 + y * add4, 4), :]
        second = rows[pl.ds(f2 + y * add2, 2), :]
        return jnp.concatenate([first, second, jnp.zeros((2, 128), jnp.float32)], axis=0)

    def own_sums(x, y, z):
        count = near_list(x, y, z, True)
        return pairs("all", rows, four, two, use, count, cell(x, y, z), cols, table)

    def halo_cell(x, y, z):
        count = near_list(x, y, z, False)
        tile = cell(x, y, z)
        return tile, pairs("density", rows, four, two, use, count, tile, cols, table)

    return own_sums, halo_cell


def on_border(x, z):
    return (x == 0) | (x == SX - 1) | (z == 0) | (z == SZ - 1)


def on_face(y):
    return (y == 0) | (y == SY - 1)


def slab_faces(
    ids, own, zlo, zhi, xlo, xhi, before, up, down, tiles, sums, places,
    rows, tails, lists, sem, four, two, use, flags, cols, table,
):
    tails[...] = jnp.zeros(tails.shape, jnp.int32)
    tails[0:1] = own[OWN_TAIL : OWN_TAIL + 1].astype(jnp.int32)
    tails[1:2] = zlo[Z_TAIL : Z_TAIL + 1].astype(jnp.int32)
    tails[2:3] = zhi[Z_TAIL : Z_TAIL + 1].astype(jnp.int32)
    tails[3:6] = xlo[X_TAIL : X_TAIL + 3].astype(jnp.int32)
    tails[6:9] = xhi[X_TAIL : X_TAIL + 3].astype(jnp.int32)
    copy = pltpu.make_async_copy(tails, lists, sem)
    copy.start()
    gather(rows, own, zlo, zhi, xlo, xhi)

    clear(flags, (SX + 2) * SY)
    for out, y in ((up, SY - 1), (down, 0)):
        for x in range(-2, SX + 2):
            for z in range(-2, SZ + 2):
                row4, row2 = slab_rows_at(x, y, z)
                spot = ((x + 2) * (SZ + 4) + z + 2) * 4
                out[spot : spot + 4] = rows[row4 : row4 + 4]
                if -1 <= x <= SX and -1 <= z <= SZ:
                    spot = Y_TWO + ((x + 1) * (SZ + 2) + z + 1) * 2
                    out[spot : spot + 2] = rows[row2 : row2 + 2]
        out[Y_SUM:Y_TAIL] = jnp.zeros((Y_TAIL - Y_SUM, 128), jnp.float32)
    copy.wait()

    number = jnp.int32(0)
    for q, (bx, bz) in enumerate(BLOCKS):

        def one(s, n, q=q, bx=bx, bz=bz):
            a, b, d = corner(lists[q, s])
            x, z = a + bx * SX, d + bz * SZ
            inside = (x >= -1) & (x <= SX) & (z >= -1) & (z <= SZ)
            places[0, n] = x
            places[1, n] = b
            places[2, n] = z

            @pl.when(inside)
            def _():
                mark(flags, (x + 1) * SY + b, z + 1)

            return n + inside.astype(jnp.int32)

        number = lax.fori_loop(0, lists[q, 15], one, number)
    places[3, 0] = number
    places[3, 1] = lists[0, 15]
    mine = lists[0, 15]

    lane = lax.broadcasted_iota(jnp.int32, (8, 128), 1)
    line = lax.broadcasted_iota(jnp.int32, (8, 128), 0)

    def tell(s, state):
        lists_, numbers = list(state[0]), list(state[1])
        x, y, z = places[0, s], places[1, s], places[2, s]
        for n, edge in enumerate((SY - 1, 0)):
            here = y == edge
            at = jnp.where(here, numbers[n], 126)
            value = jnp.where(line == 0, x, z)
            lists_[n] = jnp.where(lane == at, value, lists_[n])
            numbers[n] = numbers[n] + here.astype(jnp.int32)
        return tuple(lists_), tuple(numbers)

    nothing = jnp.zeros((8, 128), jnp.int32)
    told, numbers = lax.fori_loop(
        0, number, tell, ((nothing, nothing), (jnp.int32(0), jnp.int32(0)))
    )
    for n, out in enumerate((up, down)):
        out[Y_TAIL:Y_ROWS] = jnp.where(lane == 127, numbers[n], told[n]).astype(jnp.float32)

    own_sums, halo_cell = slab_tools(rows, four, two, use, flags, cols, table)

    def send_sum(s, x, y, z):
        spot = Y_SUM + (x + 1) * (SZ + 2) + z + 1

        @pl.when(y == 0)
        def _():
            down[pl.ds(spot, 1), :] = tiles[s, 6:7]

        @pl.when(y == SY - 1)
        def _():
            up[pl.ds(spot, 1), :] = tiles[s, 6:7]

    def own_slot(s, _):
        x, y, z = places[0, s], places[1, s], places[2, s]
        sums[s] = before[s]
        row = pl.multiple_of(own_row(x, y, z), 8)
        whole = rows[pl.ds(row, 8), :]
        tiles[s] = whole

        @pl.when(on_face(y))
        def _():
            @pl.when(on_border(x, z))
            def _():
                sums[s] = sums[s] + own_sums(x, y, z)

            tiles[s, 6:7] = sums[s, 0:1]
            send_sum(s, x, y, z)

        sums[s, 7:8] = whole[6:7]
        return 0

    def halo_slot(s, _):
        x, y, z = places[0, s], places[1, s], places[2, s]

        @pl.when(on_face(y))
        def _():
            tiles[s], total = halo_cell(x, y, z)
            tiles[s, 6:7] = total
            send_sum(s, x, y, z)

        return 0

    lax.fori_loop(0, mine, own_slot, 0)
    lax.fori_loop(mine, number, halo_slot, 0)


def slab_inside(
    places, own, zlo, zhi, xlo, xhi, tiles_in, sums_in, tiles, sums,
    rows, four, two, use, flags, cols, table,
):
    gather(rows, own, zlo, zhi, xlo, xhi)
    tiles[...] = tiles_in[...]
    sums[...] = sums_in[...]
    number, mine = places[3, 0], places[3, 1]
    clear(flags, (SX + 2) * SY)

    def one(s, _):
        mark(flags, (places[0, s] + 1) * SY + places[1, s], places[2, s] + 1)
        return 0

    lax.fori_loop(0, number, one, 0)
    own_sums, halo_cell = slab_tools(rows, four, two, use, flags, cols, table)

    def own_slot(s, _):
        x, y, z = places[0, s], places[1, s], places[2, s]

        @pl.when(jnp.logical_not(on_face(y)))
        def _():
            @pl.when(on_border(x, z))
            def _():
                sums[s, 0:7] = sums[s, 0:7] + own_sums(x, y, z)[0:7]

            tiles[s, 6:7] = sums[s, 0:1]

        return 0

    def halo_slot(s, _):
        x, y, z = places[0, s], places[1, s], places[2, s]

        @pl.when(jnp.logical_not(on_face(y)))
        def _():
            tiles[s], total = halo_cell(x, y, z)
            tiles[s, 6:7] = total

        return 0

    lax.fori_loop(0, mine, own_slot, 0)
    lax.fori_loop(mine, number, halo_slot, 0)


def finish(
    places, ylo, yhi, up, down, tiles, sums, old, density, accel,
    rows, cells, final, spots, tails, lists, sem, four, two, use, flags, cols, table,
):
    tails[0:8] = ylo[Y_TAIL:Y_ROWS].astype(jnp.int32)
    tails[8:16] = yhi[Y_TAIL:Y_ROWS].astype(jnp.int32)
    copy = pltpu.make_async_copy(tails, lists, sem)
    copy.start()
    rows[0:Y_ROWS] = ylo[...]
    rows[Y_ROWS : 2 * Y_ROWS] = yhi[...]
    rows[2 * Y_ROWS : 3 * Y_ROWS] = down[...]
    rows[3 * Y_ROWS : 4 * Y_ROWS] = up[...]
    density[...] = old[...]
    accel[...] = jnp.zeros(accel.shape, jnp.float32)
    clear(flags, 2 * (SX + 2))
    number, mine = places[3, 0], places[3, 1]

    def take(s, _):
        for c in range(3):
            spots[c, s] = places[c, s]
        cells[pl.ds(pl.multiple_of(s * 8, 8), 8), :] = tiles[s]
        return 0

    lax.fori_loop(0, number, take, 0)
    final[...] = sums[...]
    copy.wait()
    total = number
    for side in range(2):

        def one(s, n, side=side):
            x, z = lists[side * 8, s], lists[side * 8 + 1, s]
            spots[0, n] = x
            spots[1, n] = jnp.int32(-1 if side == 0 else SY)
            spots[2, n] = z
            mark(flags, side * (SX + 2) + x + 1, z + 1)
            at = (x + 1) * (SZ + 2) + z + 1
            base = side * Y_ROWS
            row4 = base + ((x + 2) * (SZ + 4) + z + 2) * 4
            row2 = base + Y_TWO + at * 2
            cells[pl.ds(pl.multiple_of(n * 8, 8), 8), :] = jnp.concatenate(
                [
                    rows[pl.ds(row4, 4), :],
                    rows[pl.ds(row2, 2), :],
                    rows[pl.ds(base + Y_SUM + at, 1), :],
                    jnp.zeros((1, 128), jnp.float32),
                ],
                axis=0,
            )
            return n + 1

        total = lax.fori_loop(0, lists[side * 8, 127], one, total)

    def near_list(s, own_cell):
        x, y, z = spots[0, s], spots[1, s], spots[2, s]
        high = y >= SY - 1
        outer = (y == -1) | (y == SY)
        base = jnp.where(outer, 2 * Y_ROWS, 0) + jnp.where(high, Y_ROWS, 0)
        for e, (ea, ed) in enumerate((p, q) for p in (-1, 0, 1) for q in (-1, 0, 1)):
            na, nd = x + ea, z + ed
            four[e] = base + ((na + 2) * (SZ + 4) + nd + 2) * 4
            use[e] = jnp.float32(1.0)
            if own_cell:
                two[e] = base + Y_TWO + ((na + 1) * (SZ + 2) + nd + 1) * 2
                word = flags[jnp.where(high, SX + 2, 0) + na + 1]
                use[e] = jnp.where(bit(word, nd + 1) > 0, jnp.float32(0.5), jnp.float32(1.0))

    def across_own(s, _):
        y = spots[1, s]

        @pl.when((y <= 0) | (y >= SY - 1))
        def _():
            near_list(s, True)
            spot = pl.multiple_of(s * 8, 8)
            tile = cells[pl.ds(spot, 8), :]
            count = jnp.int32(9)
            result = pairs("all", rows, four, two, use, count, tile, cols, table)
            final[s, 0:7] = final[s, 0:7] + result[0:7]
            cells[pl.ds(spot + 6, 1), :] = tile[6:7] + result[0:1]

        return 0

    def across_halo(s, _):
        y = spots[1, s]

        @pl.when((y <= 0) | (y >= SY - 1))
        def _():
            near_list(s, False)
            spot = pl.multiple_of(s * 8, 8)
            tile = cells[pl.ds(spot, 8), :]
            count = jnp.int32(9)
            result = pairs("density", rows, four, two, use, count, tile, cols, table)
            cells[pl.ds(spot + 6, 1), :] = tile[6:7] + result

        return 0

    lax.fori_loop(0, mine, across_own, 0)
    lax.fori_loop(mine, total, across_halo, 0)

    def weigh(q, _):
        base = pl.multiple_of(q * 64, 64)

        def get(c):
            return cells[pl.ds(base + c, 8, stride=8), :]

        good = get(3) > 0.0
        inv = 1.0 / jnp.where(good, get(4), 1.0)
        inv2 = inv * inv
        inv4 = inv2 * inv2
        fresh = (4.0 * KC) * (inv4 * inv4) * get(6)
        safe = jnp.where(good, fresh, 1.0)
        power = jnp.exp(jnp.log(safe) * (-1.0 / 3.0))
        weight = get(5) * power
        cells[pl.ds(base + 5, 8, stride=8), :] = jnp.where(good, weight, 0.0)
        cells[pl.ds(base + 6, 8, stride=8), :] = safe
        cells[pl.ds(base + 7, 8, stride=8), :] = power
        return 0

    lax.fori_loop(0, lax.div(total + 7, 8), weigh, 0)

    def last(s, _):
        x, y, z = spots[0, s], spots[1, s], spots[2, s]

        def check(t, n):
            close = (
                (jnp.abs(spots[0, t] - x) <= 1)
                & (jnp.abs(spots[1, t] - y) <= 1)
                & (jnp.abs(spots[2, t] - z) <= 1)
            )
            four[n] = t * 8
            two[n] = t * 8 + 4
            use[n] = jnp.float32(1.0)
            return n + close.astype(jnp.int32)

        count = lax.fori_loop(0, total, check, jnp.int32(0))
        spot = pl.multiple_of(s * 8, 8)
        tile = cells[pl.ds(spot, 8), :]
        result = final[s] + pairs("near", cells, four, two, use, count, tile, cols, table)
        good = tile[3:4] > 0.0
        own = final[s, 7:8] * tile[7:8]
        place = (x, y, pl.ds(z, 1), slice(None))
        density[place] = jnp.where(good, tile[6:7], old[place])
        for c in range(3):
            push = (20.0 * KC) * (own * final[s, 1 + c : 2 + c] + result[4 + c : 5 + c])
            accel[(c, *place)] = jnp.where(good, push, 0.0)
        return 0

    lax.fori_loop(0, mine, last, 0)


def f32(*shape):
    return jax.ShapeDtypeStruct(shape, jnp.float32)


def i32(*shape):
    return jax.ShapeDtypeStruct(shape, jnp.int32)


def neighbours(up, down, axis):
    size = lax.axis_size(axis)
    pairs_ = [(i, i + 1) for i in range(size - 1)]
    low = lax.ppermute(up, axis, pairs_)
    high = lax.ppermute(down, axis, [(j, i) for i, j in pairs_])
    return low, high


def work(flags, near):
    return [
        pltpu.SMEM((near,), jnp.int32),
        pltpu.SMEM((near,), jnp.int32),
        pltpu.SMEM((near,), jnp.float32),
        pltpu.SMEM((flags,), jnp.int32),
        pltpu.VMEM((4, 128, 128), jnp.float32),
        pltpu.VMEM((7, 128, 128), jnp.float32),
    ]


def cost(us):
    return pl.CostEstimate(flops=us * 10_000_000, bytes_accessed=us * 2_000_000, transcendentals=0)


def call(body, outs, out_specs, in_specs, scratch, us, limit=40):
    return pl.pallas_call(
        body,
        out_shape=outs,
        in_specs=in_specs,
        out_specs=out_specs,
        scratch_shapes=scratch,
        compiler_params=pltpu.CompilerParams(vmem_limit_bytes=limit * 1024 * 1024),
        cost_estimate=cost(us),
    )


def per_device(positions, mass, support, counts, entropy, density_old, active):
    small = [jnp.transpose(v, (1, 2, 0)) for v in (counts, active)]
    own, z_up, z_down, ids = call(
        pack,
        (f32(OWN_ROWS, S), f32(Z_ROWS, S), f32(Z_ROWS, S), i32(16)),
        (VMEM, VMEM, VMEM, SMEM),
        [ANY] * 7,
        [
            pltpu.SMEM((SY, SZ, SX), jnp.int32),
            pltpu.SMEM((SY, SZ, SX), jnp.int32),
            pltpu.VMEM((3, SX, SY, SZ, S), jnp.float32),
        ]
        + [pltpu.VMEM((SX, SY, SZ, S), jnp.float32)] * 4
        + [pltpu.SemaphoreType.DMA((7,))],
        2,
        56,
    )(*small, positions, mass, support, entropy, density_old)
    zlo, zhi = neighbours(z_up, z_down, "gz")
    first = call(
        local_first, f32(16, 8, S), VMEM, [SMEM, VMEM], work(SX * SY, 48), 8
    )(ids, own)
    x_up, x_down = call(
        pack_x, (f32(X_ROWS, S), f32(X_ROWS, S)), (VMEM, VMEM), [VMEM] * 3 + [ANY], [], 1
    )(own, zlo, zhi, first)
    xlo, xhi = neighbours(x_up, x_down, "gx")
    second = call(
        local_second,
        f32(16, 8, S),
        VMEM,
        [SMEM, VMEM, VMEM, ANY],
        work(SX * SY, 48),
        8,
    )(ids, own, first, x_up)
    y_up, y_down, tiles, sums, places = call(
        slab_faces,
        (f32(Y_ROWS, S), f32(Y_ROWS, S), f32(SLAB_MOST, 8, S), f32(16, 8, S), i32(4, 128)),
        (VMEM, VMEM, VMEM, VMEM, SMEM),
        [SMEM] + [VMEM] * 6,
        [
            pltpu.VMEM((SLAB, S), jnp.float32),
            pltpu.VMEM((16, S), jnp.int32),
            pltpu.SMEM((16, S), jnp.int32),
            pltpu.SemaphoreType.DMA,
        ]
        + work((SX + 2) * SY, 48),
        4,
    )(ids, own, zlo, zhi, xlo, xhi, second)
    ylo, yhi = neighbours(y_up, y_down, "gy")
    tiles, sums = call(
        slab_inside,
        (f32(SLAB_MOST, 8, S), f32(16, 8, S)),
        (VMEM, VMEM),
        [SMEM] + [VMEM] * 7,
        [pltpu.VMEM((SLAB, S), jnp.float32)] + work((SX + 2) * SY, 48),
        6,
    )(places, own, zlo, zhi, xlo, xhi, tiles, sums)
    return call(
        finish,
        (f32(SX, SY, SZ, S), f32(3, SX, SY, SZ, S)),
        (VMEM, VMEM),
        [SMEM] + [VMEM] * 7,
        [
            pltpu.VMEM((4 * Y_ROWS, S), jnp.float32),
            pltpu.VMEM((ALL_MOST * 8, S), jnp.float32),
            pltpu.VMEM((16, 8, S), jnp.float32),
            pltpu.SMEM((4, ALL_MOST), jnp.int32),
            pltpu.VMEM((16, S), jnp.int32),
            pltpu.SMEM((16, S), jnp.int32),
            pltpu.SemaphoreType.DMA,
        ]
        + work(2 * (SX + 2), ALL_MOST + 16),
        8,
    )(places, ylo, yhi, y_up, y_down, tiles, sums, density_old)


def solution(mesh):
    return jax.shard_map(
        per_device,
        mesh=mesh,
        in_specs=(
            P(None, "gx", "gy", "gz", None),
            P("gx", "gy", "gz", None),
            P("gx", "gy", "gz", None),
            P("gx", "gy", "gz"),
            P("gx", "gy", "gz", None),
            P("gx", "gy", "gz", None),
            P("gx", "gy", "gz"),
        ),
        out_specs=(P("gx", "gy", "gz", None), P(None, "gx", "gy", "gz", None)),
        check_vma=False,
    )
```

```python
import functools
import math

import jax
import jax.numpy as jnp
from jax import lax
from jax.experimental import pallas as pl
from jax.experimental.pallas import tpu as pltpu
from jax.sharding import PartitionSpec as P

KC = 21.0 / (2.0 * math.pi)
SX, SY, SZ, S = 12, 6, 6, 128
MOST = 9
CELLS = SX * SY * SZ

ZERO = CELLS * 8
OWN_TAIL = ZERO + 8
OWN_ROWS = OWN_TAIL + 8

Z_TWO, Z_FAR, Z_TAIL, Z_ROWS = 288, 432, 720, 728
X_TWO, X_FAR, X_TAIL, X_ROWS = 240, 336, 576, 584
Y_TWO, Y_SUM, Y_TAIL, Y_ROWS = 640, 864, 976, 984

ZLO = OWN_ROWS
ZHI = ZLO + Z_ROWS
XLO = ZHI + Z_ROWS
XHI = XLO + X_ROWS
SLAB = XHI + X_ROWS

SLAB_MOST = 96
ALL_MOST = 256

VMEM = pl.BlockSpec(memory_space=pltpu.VMEM)
SMEM = pl.BlockSpec(memory_space=pltpu.SMEM)
ANY = pl.BlockSpec(memory_space=pl.ANY)
PARAMS = pltpu.CompilerParams(vmem_limit_bytes=40 * 1024 * 1024)

BLOCKS = [(0, 0), (0, -1), (0, 1), (-1, 0), (-1, -1), (-1, 1), (1, 0), (1, -1), (1, 1)]


def step(mode, i, near, sums):
    xi, yi, zi, hi, bi = i
    xj, yj, zj, mj, hj, wj = near
    dx, dy, dz = xi - xj, yi - yj, zi - zj
    sq = jnp.maximum(dx * dx + dy * dy + dz * dz, 1e-30)
    dist = sq * lax.rsqrt(sq)
    out = []
    if mode != "near":
        wi = jnp.maximum(hi - dist, 0.0)
        own = mj * (wi * wi * wi)
        out.append(sums[0] + own * (wi * (bi - wi)))
        if mode == "all":
            out += [sums[1] + own * dx, sums[2] + own * dy, sums[3] + own * dz]
    if mode != "density":
        wj_ = jnp.maximum(hj - dist, 0.0)
        other = wj * (wj_ * wj_ * wj_)
        last = sums[-3:]
        out += [last[0] + other * dx, last[1] + other * dy, last[2] + other * dz]
    return tuple(out)


WIDTH = {"all": 7, "density": 1, "near": 3}
FIRST = {"all": 0, "density": 0, "near": 4}
NEAR = {"all": 3, "density": 9, "near": 1}
GROUPS = {"all": 2, "density": 2, "near": 8}


def pairs(mode, src, four, two, use, count, used, tile, cols, table):
    many, regs = NEAR[mode], GROUPS[mode]
    for u in range(many - 1):
        four[count + u] = jnp.int32(0)
        if two is not None:
            two[count + u] = jnp.int32(0)
        use[count + u] = jnp.float32(0.0)
    steps = lax.div(count + (many - 1), many)
    for n, c in enumerate((0, 1, 2, 4)):
        if mode == "near" and n == 3:
            break
        cols[n] = jnp.broadcast_to(tile[c : c + 1], (128, 128)).T
    width = WIDTH[mode]
    zero = jnp.zeros((8, 128), jnp.float32)

    def group(g, _):
        spots, own = [], []
        for v in range(regs):
            spot = pl.ds(pl.multiple_of((g * regs + v) * 8, 8), 8)
            x, y, z = [cols[n, spot, :] for n in range(3)]
            h = cols[3, spot, :] if mode != "near" else None
            spots.append(spot)
            own.append((x, y, z, h, 1.25 * h if mode != "near" else None))

        def body(q, sums):
            sums = list(sums)
            for u in range(many):
                at = q * many + u
                f = four[at]
                near = [
                    jnp.broadcast_to(src[pl.ds(f + c, 1), :], (8, 128)) for c in range(4)
                ]
                flag = use[at]
                if mode != "near":
                    near[3] = near[3] * jnp.where(flag >= 0.5, 1.0, 0.0)
                if mode != "density":
                    t = f + 4 if two is None else two[at]
                    near.append(jnp.broadcast_to(src[pl.ds(t, 1), :], (8, 128)))
                    weight = jnp.broadcast_to(src[pl.ds(t + 1, 1), :], (8, 128))
                    near.append(weight * jnp.where(flag == 1.0, 1.0, 0.0))
                else:
                    near += [None, None]
                for v in range(regs):
                    sums[v] = step(mode, own[v], near, sums[v])
            return tuple(sums)

        sums = lax.fori_loop(0, steps, body, ((zero,) * width,) * regs)
        for v in range(regs):
            for c in range(width):
                table[c, spots[v], :] = sums[v][c]
        return 0

    lax.fori_loop(0, lax.div(used + (8 * regs - 1), 8 * regs), group, 0)
    lines = [jnp.sum(table[c].T, axis=0, keepdims=True) for c in range(width)]
    if mode == "density":
        return lines[0]
    before = [jnp.zeros((1, 128), jnp.float32)] * FIRST[mode]
    after = [jnp.zeros((1, 128), jnp.float32)] * (8 - FIRST[mode] - width)
    return jnp.concatenate(before + lines + after, axis=0)


def bit(word, at):
    return lax.shift_right_logical(word, at) & 1


def clear(words, count):
    def one(k, _):
        words[k] = jnp.int32(0)
        return 0

    lax.fori_loop(0, count, one, 0, unroll=14)


def mark(words, at, place):
    words[at] = words[at] | lax.shift_left(jnp.int32(1), place)


def corner(code):
    return lax.shift_right_logical(code, 6), lax.shift_right_logical(code, 3) & 7, code & 7


def pack(
    counts_in, active_in, pos_in, mass_in, support_in, entropy_in, old_in, own, up, down, ids,
    counts, active, pos, mass, support, entropy, old, sems,
):
    given = (active_in, counts_in, pos_in, mass_in, support_in, entropy_in, old_in)
    held = (active, counts, pos, mass, support, entropy, old)
    copies = [pltpu.make_async_copy(a, b, sems.at[n]) for n, (a, b) in enumerate(zip(given, held))]
    for copy in copies:
        copy.start()
    copies[0].wait()

    def scan(q, n):
        y, z = lax.div(q, SZ), lax.rem(q, SZ)
        for x in range(SX):
            ids[n] = x * 64 + y * 8 + z
            n = n + active[y, z, x]
        return n

    number = lax.fori_loop(0, SY * SZ, scan, jnp.int32(0))
    ids[15] = number
    copies[1].wait()
    lane = lax.broadcasted_iota(jnp.int32, (8, 128), 1)

    def tell(s, tail):
        code = ids[s]
        x, y, z = corner(code)
        ids[16 + s] = counts[y, z, x]
        tail = jnp.where(lane == s, code, tail)
        return jnp.where(lane == 16 + s, counts[y, z, x], tail)

    tail = lax.fori_loop(0, number, tell, jnp.where(lane == 15, number, 0)).astype(jnp.float32)
    own[ZERO : ZERO + 8] = jnp.zeros((8, 128), jnp.float32)
    own[OWN_TAIL : OWN_TAIL + 8] = tail
    up[Z_TAIL : Z_TAIL + 8] = tail
    down[Z_TAIL : Z_TAIL + 8] = tail
    for copy in copies[2:]:
        copy.wait()
    sub = lax.broadcasted_iota(jnp.int32, (SZ, 128), 0)
    slot = lax.broadcasted_iota(jnp.int32, (SZ, 128), 1)

    def cells(x, _):
        for y in range(SY):
            many = jnp.zeros((SZ, 128), jnp.int32)
            act = jnp.zeros((SZ, 128), jnp.int32)
            for z in range(SZ):
                many = jnp.where(sub == z, counts[y, z, x], many)
                act = jnp.where(sub == z, active[y, z, x], act)
            h = support[x, y]
            inv = 1.0 / h
            inv2 = inv * inv
            inv4 = inv2 * inv2
            m = jnp.where(slot < many, mass[x, y], 0.0)
            gain = entropy[x, y] * (inv4 * inv4)
            power = jnp.exp(jnp.log(old[x, y]) * (-1.0 / 3.0))
            weight = m * gain * jnp.where(act > 0, 1.0, power)
            base = pl.multiple_of(x * (SY * SZ * 8), 8) + y * SZ * 8
            for c, value in enumerate(
                (pos[0, x, y], pos[1, x, y], pos[2, x, y], m, h, weight, gain)
            ):
                own[pl.ds(base + c, SZ, stride=8), :] = value
        return 0

    lax.fori_loop(0, SX, cells, 0)

    def faces(x2, _):
        for u in range(2):
            for y in range(SY):
                base = pl.multiple_of(x2 * (2 * SY * SZ * 8), 8) + (u * SY + y) * SZ * 8
                four = pl.multiple_of(x2 * (2 * SY * 4), 8) + (u * SY + y) * 4
                two = pl.multiple_of(x2 * (2 * SY * 2), 8) + (u * SY + y) * 2
                for out, z1, z2 in ((up, SZ - 1, SZ - 2), (down, 0, 1)):
                    out[pl.ds(four, 4), :] = own[pl.ds(base + z1 * 8, 4), :]
                    out[pl.ds(two + Z_TWO, 2), :] = own[pl.ds(base + z1 * 8 + 4, 2), :]
                    out[pl.ds(four + Z_FAR, 4), :] = own[pl.ds(base + z2 * 8, 4), :]
        return 0

    lax.fori_loop(0, SX // 2, faces, 0)


def own_row(x, y, z):
    return ((x * SY + y) * SZ + z) * 8


def local(part, ids, own, before, sums, four, two, use, flags, cols, table):
    number = ids[15]
    half = lax.div(number + 1, 2)

    clear(flags, SX * SY)

    def one(s, _):
        x, y, z = corner(ids[s])
        mark(flags, x * SY + y, z)
        return 0

    lax.fori_loop(0, number, one, 0)
    if before is not None:
        sums[...] = before[...]

    def slot(s, _):
        a, b, d = corner(ids[s])
        count = jnp.int32(0)
        in_z = [(d + ed >= 0) & (d + ed < SZ) for ed in (-1, 0, 1)]
        for ea in (-1, 0, 1):
            for eb in (-1, 0, 1):
                na, nb = a + ea, b + eb
                inside = (na >= 0) & (na < SX) & (nb >= 0) & (nb < SY)
                column = na * SY + nb
                word = flags[jnp.where(inside, column, 0)]
                row = column * (SZ * 8) + d * 8
                for n, ed in enumerate((-1, 0, 1)):
                    four[count] = row + ed * 8
                    known = bit(word, jnp.maximum(d + ed, 0))
                    use[count] = jnp.where(known > 0, jnp.float32(0.5), jnp.float32(1.0))
                    count = count + (inside & in_z[n]).astype(jnp.int32)
        tile = own[pl.ds(pl.multiple_of(own_row(a, b, d), 8), 8), :]
        sums[s] = pairs("all", own, four, None, use, count, ids[16 + s], tile, cols, table)
        return 0

    if part == 0:
        lax.fori_loop(0, half, slot, 0)
    else:
        lax.fori_loop(half, number, slot, 0)


def local_first(ids, own, sums, *scratch):
    local(0, ids, own, None, sums, *scratch)


def local_second(ids, own, before, _, sums, *scratch):
    local(1, ids, own, before, sums, *scratch)


def pack_x(own, zlo, zhi, _, up, down):
    for out, x1, x2 in ((up, SX - 1, SX - 2), (down, 0, 1)):
        for y in range(SY):
            for z in range(-2, SZ + 2):
                for x, base in ((x1, 0), (x2, X_FAR)):
                    spot = base + (y * (SZ + 4) + z + 2) * 4
                    if 0 <= z < SZ:
                        row = own_row(x, y, z)
                        out[spot : spot + 4] = own[row : row + 4]
                    else:
                        src = zlo if z < 0 else zhi
                        far = Z_FAR if z in (-2, SZ + 1) else 0
                        row = far + (x * SY + y) * 4
                        out[spot : spot + 4] = src[row : row + 4]
                if -1 <= z <= SZ:
                    spot = X_TWO + (y * (SZ + 2) + z + 1) * 2
                    if 0 <= z < SZ:
                        row = own_row(x1, y, z) + 4
                        out[spot : spot + 2] = own[row : row + 2]
                    else:
                        src = zlo if z < 0 else zhi
                        row = Z_TWO + (x1 * SY + y) * 2
                        out[spot : spot + 2] = src[row : row + 2]
        out[X_TAIL : X_TAIL + 8] = jnp.zeros((8, 128), jnp.float32)
        out[X_TAIL : X_TAIL + 1] = own[OWN_TAIL : OWN_TAIL + 1]
        out[X_TAIL + 1 : X_TAIL + 2] = zlo[Z_TAIL : Z_TAIL + 1]
        out[X_TAIL + 2 : X_TAIL + 3] = zhi[Z_TAIL : Z_TAIL + 1]


def slab_rows(x, z):
    zlow, xlow = z < 0, x < 0
    zout = zlow | (z >= SZ)
    xout = xlow | (x >= SX)
    zbase = jnp.where(zlow, ZLO, ZHI)
    zfar = jnp.where((z == -2) | (z == SZ + 1), Z_FAR, 0)
    xbase = jnp.where(xlow, XLO, XHI)
    xfar = jnp.where((x == -2) | (x == SX + 1), X_FAR, 0)
    four = jnp.where(zout, zbase + zfar + x * (SY * 4), x * (SY * SZ * 8) + z * 8)
    two = jnp.where(zout, zbase + Z_TWO + x * (SY * 2), x * (SY * SZ * 8) + z * 8 + 4)
    four = jnp.where(xout, xbase + xfar + (z + 2) * 4, four)
    two = jnp.where(xout, xbase + X_TWO + (z + 1) * 2, two)
    add4 = jnp.where(xout, (SZ + 4) * 4, jnp.where(zout, 4, SZ * 8))
    add2 = jnp.where(xout, (SZ + 2) * 2, jnp.where(zout, 2, SZ * 8))
    return four, two, add4, add2


def slab_rows_at(x, y, z):
    if 0 <= x < SX and 0 <= z < SZ:
        return own_row(x, y, z), own_row(x, y, z) + 4
    if 0 <= x < SX:
        base, far, k = ZLO if z < 0 else ZHI, z in (-2, SZ + 1), x * SY + y
        return base + (Z_FAR if far else 0) + k * 4, base + Z_TWO + k * 2
    base, far = XLO if x < 0 else XHI, x in (-2, SX + 1)
    four = base + (X_FAR if far else 0) + (y * (SZ + 4) + z + 2) * 4
    return four, base + X_TWO + (y * (SZ + 2) + z + 1) * 2


def gather(rows, own, zlo, zhi, xlo, xhi):
    rows[0:OWN_ROWS] = own[...]
    rows[ZLO:ZHI] = zlo[...]
    rows[ZHI:XLO] = zhi[...]
    rows[XLO:XHI] = xlo[...]
    rows[XHI:SLAB] = xhi[...]


def slab_tools(rows, four, two, use, flags, cols, table):
    def near_list(x, y, z, own_cell):
        count = jnp.int32(0)
        for ea in (-1, 0, 1):
            for ed in (-1, 0, 1):
                na, nd = x + ea, z + ed
                f4, f2, add4, add2 = slab_rows(na, nd)
                if own_cell:
                    outer = (na < 0) | (na >= SX) | (nd < 0) | (nd >= SZ)
                for eb in (-1, 0, 1):
                    nb = y + eb
                    wanted = (nb >= 0) & (nb < SY)
                    four[count] = f4 + nb * add4
                    if own_cell:
                        wanted = wanted & outer
                        two[count] = f2 + nb * add2
                        word = flags[(na + 1) * SY + jnp.where(wanted, nb, 0)]
                        known = bit(word, nd + 1)
                        use[count] = jnp.where(known > 0, jnp.float32(0.5), jnp.float32(1.0))
                    else:
                        use[count] = jnp.float32(1.0)
                    count = count + wanted.astype(jnp.int32)
        return count

    def cell(x, y, z):
        f4, f2, add4, add2 = slab_rows(x, z)
        first = rows[pl.ds(f4 + y * add4, 4), :]
        second = rows[pl.ds(f2 + y * add2, 2), :]
        return jnp.concatenate([first, second, jnp.zeros((2, 128), jnp.float32)], axis=0)

    def own_sums(x, y, z, used):
        count = near_list(x, y, z, True)
        return pairs("all", rows, four, two, use, count, used, cell(x, y, z), cols, table)

    def halo_cell(x, y, z, used):
        count = near_list(x, y, z, False)
        tile = cell(x, y, z)
        return tile, pairs("density", rows, four, None, use, count, used, tile, cols, table)

    return own_sums, halo_cell


def beside(places, mine, x, y, z):
    def one(t, found):
        close = (
            (jnp.abs(places[0, t] - x) <= 1)
            & (jnp.abs(places[1, t] - y) <= 1)
            & (jnp.abs(places[2, t] - z) <= 1)
        )
        return found | close.astype(jnp.int32)

    return lax.fori_loop(0, mine, one, jnp.int32(0)) > 0


def on_border(x, z):
    return (x == 0) | (x == SX - 1) | (z == 0) | (z == SZ - 1)


def on_face(y):
    return (y == 0) | (y == SY - 1)


def slab_faces(
    own, zlo, zhi, xlo, xhi, before, up, down, tiles, sums, places,
    rows, tails, lists, sem, four, two, use, flags, cols, table,
):
    tails[...] = jnp.zeros(tails.shape, jnp.int32)
    tails[0:1] = own[OWN_TAIL : OWN_TAIL + 1].astype(jnp.int32)
    tails[1:2] = zlo[Z_TAIL : Z_TAIL + 1].astype(jnp.int32)
    tails[2:3] = zhi[Z_TAIL : Z_TAIL + 1].astype(jnp.int32)
    tails[3:6] = xlo[X_TAIL : X_TAIL + 3].astype(jnp.int32)
    tails[6:9] = xhi[X_TAIL : X_TAIL + 3].astype(jnp.int32)
    copy = pltpu.make_async_copy(tails, lists, sem)
    copy.start()
    gather(rows, own, zlo, zhi, xlo, xhi)

    clear(flags, (SX + 2) * SY)
    for out, y in ((up, SY - 1), (down, 0)):
        for x in range(-2, SX + 2):
            for z in range(-2, SZ + 2):
                row4, row2 = slab_rows_at(x, y, z)
                spot = ((x + 2) * (SZ + 4) + z + 2) * 4
                out[spot : spot + 4] = rows[row4 : row4 + 4]
                if -1 <= x <= SX and -1 <= z <= SZ:
                    spot = Y_TWO + ((x + 1) * (SZ + 2) + z + 1) * 2
                    out[spot : spot + 2] = rows[row2 : row2 + 2]
        out[Y_SUM:Y_TAIL] = jnp.zeros((Y_TAIL - Y_SUM, 128), jnp.float32)
    copy.wait()

    number = jnp.int32(0)
    for q, (bx, bz) in enumerate(BLOCKS):

        def one(s, n, q=q, bx=bx, bz=bz):
            a, b, d = corner(lists[q, s])
            x, z = a + bx * SX, d + bz * SZ
            inside = (x >= -1) & (x <= SX) & (z >= -1) & (z <= SZ)
            places[0, n] = x
            places[1, n] = b
            places[2, n] = z
            places[3, n] = lists[q, 16 + s]

            @pl.when(inside)
            def _():
                mark(flags, (x + 1) * SY + b, z + 1)

            return n + inside.astype(jnp.int32)

        number = lax.fori_loop(0, lists[q, 15], one, number)
    places[4, 0] = number
    places[4, 1] = lists[0, 15]
    mine = lists[0, 15]

    lane = lax.broadcasted_iota(jnp.int32, (8, 128), 1)
    line = lax.broadcasted_iota(jnp.int32, (8, 128), 0)

    def tell(s, state):
        lists_, numbers = list(state[0]), list(state[1])
        x, y, z = places[0, s], places[1, s], places[2, s]
        for n, edge in enumerate((SY - 1, 0)):
            here = y == edge
            at = jnp.where(here, numbers[n], 126)
            value = jnp.where(line == 0, x, jnp.where(line == 1, z, places[3, s]))
            lists_[n] = jnp.where(lane == at, value, lists_[n])
            numbers[n] = numbers[n] + here.astype(jnp.int32)
        return tuple(lists_), tuple(numbers)

    nothing = jnp.zeros((8, 128), jnp.int32)
    told, numbers = lax.fori_loop(
        0, number, tell, ((nothing, nothing), (jnp.int32(0), jnp.int32(0)))
    )
    for n, out in enumerate((up, down)):
        out[Y_TAIL:Y_ROWS] = jnp.where(lane == 127, numbers[n], told[n]).astype(jnp.float32)

    own_sums, halo_cell = slab_tools(rows, four, two, use, flags, cols, table)

    def send_sum(s, x, y, z):
        spot = Y_SUM + (x + 1) * (SZ + 2) + z + 1

        @pl.when(y == 0)
        def _():
            down[pl.ds(spot, 1), :] = tiles[s, 6:7]

        @pl.when(y == SY - 1)
        def _():
            up[pl.ds(spot, 1), :] = tiles[s, 6:7]

    def own_slot(s, _):
        x, y, z = places[0, s], places[1, s], places[2, s]
        sums[s] = before[s]
        row = pl.multiple_of(own_row(x, y, z), 8)
        whole = rows[pl.ds(row, 8), :]
        tiles[s] = whole

        @pl.when(on_face(y))
        def _():
            @pl.when(on_border(x, z))
            def _():
                sums[s] = sums[s] + own_sums(x, y, z, places[3, s])

            tiles[s, 6:7] = sums[s, 0:1]
            send_sum(s, x, y, z)

        sums[s, 7:8] = whole[6:7]
        return 0

    def halo_slot(s, _):
        x, y, z = places[0, s], places[1, s], places[2, s]

        @pl.when(on_face(y))
        def _():
            tiles[s], total = halo_cell(x, y, z, places[3, s])
            tiles[s, 6:7] = total
            send_sum(s, x, y, z)

        return 0

    lax.fori_loop(0, mine, own_slot, 0)
    lax.fori_loop(mine, number, halo_slot, 0)


def slab_inside(
    places, own, zlo, zhi, xlo, xhi, tiles_in, sums_in, tiles, sums,
    rows, four, two, use, flags, cols, table,
):
    gather(rows, own, zlo, zhi, xlo, xhi)
    tiles[...] = tiles_in[...]
    sums[...] = sums_in[...]
    number, mine = places[4, 0], places[4, 1]
    clear(flags, (SX + 2) * SY)

    def one(s, _):
        mark(flags, (places[0, s] + 1) * SY + places[1, s], places[2, s] + 1)
        return 0

    lax.fori_loop(0, number, one, 0)
    own_sums, halo_cell = slab_tools(rows, four, two, use, flags, cols, table)

    def own_slot(s, _):
        x, y, z = places[0, s], places[1, s], places[2, s]

        @pl.when(jnp.logical_not(on_face(y)))
        def _():
            @pl.when(on_border(x, z))
            def _():
                sums[s, 0:7] = sums[s, 0:7] + own_sums(x, y, z, places[3, s])[0:7]

            tiles[s, 6:7] = sums[s, 0:1]

        return 0

    def halo_slot(s, _):
        x, y, z = places[0, s], places[1, s], places[2, s]

        @pl.when(jnp.logical_not(on_face(y)) & beside(places, mine, x, y, z))
        def _():
            tiles[s], total = halo_cell(x, y, z, places[3, s])
            tiles[s, 6:7] = total

        return 0

    lax.fori_loop(0, mine, own_slot, 0)
    lax.fori_loop(mine, number, halo_slot, 0)


def finish(
    places_in, ylo, yhi, up, down, tiles, sums, old, density, accel,
    places, places_sem, rows, cells, final, spots, tails, lists, sem, four, two, use, flags, cols, table,
):
    tails[0:8] = ylo[Y_TAIL:Y_ROWS].astype(jnp.int32)
    tails[8:16] = yhi[Y_TAIL:Y_ROWS].astype(jnp.int32)
    copy = pltpu.make_async_copy(tails, lists, sem)
    copy.start()
    other = pltpu.make_async_copy(places_in, places, places_sem)
    other.start()
    rows[0:Y_ROWS] = ylo[...]
    rows[Y_ROWS : 2 * Y_ROWS] = yhi[...]
    rows[2 * Y_ROWS : 3 * Y_ROWS] = down[...]
    rows[3 * Y_ROWS : 4 * Y_ROWS] = up[...]
    density[...] = old[...]
    accel[...] = jnp.zeros(accel.shape, jnp.float32)
    clear(flags, 2 * (SX + 2))
    other.wait()
    number, mine = places[4, 0], places[4, 1]

    def take(s, n):
        for c in range(4):
            spots[c, n] = places[c, s]
        cells[pl.ds(pl.multiple_of(n * 8, 8), 8), :] = tiles[s]
        wanted = beside(places, mine, places[0, s], places[1, s], places[2, s])
        return n + wanted.astype(jnp.int32)

    total = lax.fori_loop(0, number, take, jnp.int32(0))
    final[...] = sums[...]
    copy.wait()
    for side in range(2):

        def one(s, n, side=side):
            x, z = lists[side * 8, s], lists[side * 8 + 1, s]
            spots[0, n] = x
            spots[1, n] = jnp.int32(-1 if side == 0 else SY)
            spots[2, n] = z
            spots[3, n] = lists[side * 8 + 2, s]
            mark(flags, side * (SX + 2) + x + 1, z + 1)
            at = (x + 1) * (SZ + 2) + z + 1
            base = side * Y_ROWS
            row4 = base + ((x + 2) * (SZ + 4) + z + 2) * 4
            row2 = base + Y_TWO + at * 2
            cells[pl.ds(pl.multiple_of(n * 8, 8), 8), :] = jnp.concatenate(
                [
                    rows[pl.ds(row4, 4), :],
                    rows[pl.ds(row2, 2), :],
                    rows[pl.ds(base + Y_SUM + at, 1), :],
                    jnp.zeros((1, 128), jnp.float32),
                ],
                axis=0,
            )
            wanted = beside(spots, mine, x, jnp.int32(-1 if side == 0 else SY), z)
            return n + wanted.astype(jnp.int32)

        total = lax.fori_loop(0, lists[side * 8, 127], one, total)

    def near_list(s, own_cell):
        x, y, z = spots[0, s], spots[1, s], spots[2, s]
        high = y >= SY - 1
        outer = (y == -1) | (y == SY)
        base = jnp.where(outer, 2 * Y_ROWS, 0) + jnp.where(high, Y_ROWS, 0)
        for e, (ea, ed) in enumerate((p, q) for p in (-1, 0, 1) for q in (-1, 0, 1)):
            na, nd = x + ea, z + ed
            four[e] = base + ((na + 2) * (SZ + 4) + nd + 2) * 4
            use[e] = jnp.float32(1.0)
            if own_cell:
                two[e] = base + Y_TWO + ((na + 1) * (SZ + 2) + nd + 1) * 2
                word = flags[jnp.where(high, SX + 2, 0) + na + 1]
                use[e] = jnp.where(bit(word, nd + 1) > 0, jnp.float32(0.5), jnp.float32(1.0))

    def across_own(s, _):
        y = spots[1, s]

        @pl.when((y <= 0) | (y >= SY - 1))
        def _():
            near_list(s, True)
            spot = pl.multiple_of(s * 8, 8)
            tile = cells[pl.ds(spot, 8), :]
            count = jnp.int32(9)
            result = pairs("all", rows, four, two, use, count, spots[3, s], tile, cols, table)
            final[s, 0:7] = final[s, 0:7] + result[0:7]
            cells[pl.ds(spot + 6, 1), :] = tile[6:7] + result[0:1]

        return 0

    def across_halo(s, _):
        y = spots[1, s]

        @pl.when((y <= 0) | (y >= SY - 1))
        def _():
            near_list(s, False)
            spot = pl.multiple_of(s * 8, 8)
            tile = cells[pl.ds(spot, 8), :]
            count = jnp.int32(9)
            result = pairs("density", rows, four, None, use, count, spots[3, s], tile, cols, table)
            cells[pl.ds(spot + 6, 1), :] = tile[6:7] + result

        return 0

    lax.fori_loop(0, mine, across_own, 0)
    lax.fori_loop(mine, total, across_halo, 0)

    def weigh(q, _):
        base = pl.multiple_of(q * 64, 64)

        def get(c):
            return cells[pl.ds(base + c, 8, stride=8), :]

        good = get(3) > 0.0
        inv = 1.0 / jnp.where(good, get(4), 1.0)
        inv2 = inv * inv
        inv4 = inv2 * inv2
        fresh = (4.0 * KC) * (inv4 * inv4) * get(6)
        safe = jnp.where(good, fresh, 1.0)
        power = jnp.exp(jnp.log(safe) * (-1.0 / 3.0))
        weight = get(5) * power
        cells[pl.ds(base + 5, 8, stride=8), :] = jnp.where(good, weight, 0.0)
        cells[pl.ds(base + 6, 8, stride=8), :] = safe
        cells[pl.ds(base + 7, 8, stride=8), :] = power
        return 0

    lax.fori_loop(0, lax.div(total + 7, 8), weigh, 0)

    def last(s, _):
        x, y, z = spots[0, s], spots[1, s], spots[2, s]

        def check(t, n):
            close = (
                (jnp.abs(spots[0, t] - x) <= 1)
                & (jnp.abs(spots[1, t] - y) <= 1)
                & (jnp.abs(spots[2, t] - z) <= 1)
            )
            four[n] = t * 8
            use[n] = jnp.float32(1.0)
            return n + close.astype(jnp.int32)

        count = lax.fori_loop(0, total, check, jnp.int32(0))
        spot = pl.multiple_of(s * 8, 8)
        tile = cells[pl.ds(spot, 8), :]
        result = final[s] + pairs(
            "near", cells, four, None, use, count, spots[3, s], tile, cols, table
        )
        good = tile[3:4] > 0.0
        own = final[s, 7:8] * tile[7:8]
        place = (x, y, pl.ds(z, 1), slice(None))
        density[place] = jnp.where(good, tile[6:7], old[place])
        for c in range(3):
            push = (20.0 * KC) * (own * final[s, 1 + c : 2 + c] + result[4 + c : 5 + c])
            accel[(c, *place)] = jnp.where(good, push, 0.0)
        return 0

    lax.fori_loop(0, mine, last, 0)


def f32(*shape):
    return jax.ShapeDtypeStruct(shape, jnp.float32)


def i32(*shape):
    return jax.ShapeDtypeStruct(shape, jnp.int32)


def neighbours(up, down, axis):
    size = lax.axis_size(axis)
    pairs_ = [(i, i + 1) for i in range(size - 1)]
    low = lax.ppermute(up, axis, pairs_)
    high = lax.ppermute(down, axis, [(j, i) for i, j in pairs_])
    return low, high


def work(flags, near):
    return [
        pltpu.SMEM((near,), jnp.int32),
        pltpu.SMEM((near,), jnp.int32),
        pltpu.SMEM((near,), jnp.float32),
        pltpu.SMEM((flags,), jnp.int32),
        pltpu.VMEM((4, 128, 128), jnp.float32),
        pltpu.VMEM((7, 128, 128), jnp.float32),
    ]


def cost(us):
    return pl.CostEstimate(flops=us * 10_000_000, bytes_accessed=us * 2_000_000, transcendentals=0)


def call(body, outs, out_specs, in_specs, scratch, us, limit=40):
    return pl.pallas_call(
        body,
        out_shape=outs,
        in_specs=in_specs,
        out_specs=out_specs,
        scratch_shapes=scratch,
        compiler_params=pltpu.CompilerParams(vmem_limit_bytes=limit * 1024 * 1024),
        cost_estimate=cost(us),
    )


def per_device(positions, mass, support, counts, entropy, density_old, active):
    small = [jnp.transpose(v, (1, 2, 0)) for v in (counts, active)]
    own, z_up, z_down, ids = call(
        pack,
        (f32(OWN_ROWS, S), f32(Z_ROWS, S), f32(Z_ROWS, S), i32(32)),
        (VMEM, VMEM, VMEM, SMEM),
        [ANY] * 7,
        [
            pltpu.SMEM((SY, SZ, SX), jnp.int32),
            pltpu.SMEM((SY, SZ, SX), jnp.int32),
            pltpu.VMEM((3, SX, SY, SZ, S), jnp.float32),
        ]
        + [pltpu.VMEM((SX, SY, SZ, S), jnp.float32)] * 4
        + [pltpu.SemaphoreType.DMA((7,))],
        2,
        56,
    )(*small, positions, mass, support, entropy, density_old)
    zlo, zhi = neighbours(z_up, z_down, "gz")
    first = call(
        local_first, f32(16, 8, S), VMEM, [SMEM, VMEM], work(SX * SY, 48), 8
    )(ids, own)
    x_up, x_down = call(
        pack_x, (f32(X_ROWS, S), f32(X_ROWS, S)), (VMEM, VMEM), [VMEM] * 3 + [ANY], [], 1
    )(own, zlo, zhi, first)
    xlo, xhi = neighbours(x_up, x_down, "gx")
    second = call(
        local_second,
        f32(16, 8, S),
        VMEM,
        [SMEM, VMEM, VMEM, ANY],
        work(SX * SY, 48),
        8,
    )(ids, own, first, x_up)
    y_up, y_down, tiles, sums, places = call(
        slab_faces,
        (f32(Y_ROWS, S), f32(Y_ROWS, S), f32(SLAB_MOST, 8, S), f32(16, 8, S), i32(8, 128)),
        (VMEM, VMEM, VMEM, VMEM, SMEM),
        [VMEM] * 6,
        [
            pltpu.VMEM((SLAB, S), jnp.float32),
            pltpu.VMEM((16, S), jnp.int32),
            pltpu.SMEM((16, S), jnp.int32),
            pltpu.SemaphoreType.DMA,
        ]
        + work((SX + 2) * SY, 48),
        4,
    )(own, zlo, zhi, xlo, xhi, second)
    ylo, yhi = neighbours(y_up, y_down, "gy")
    tiles, sums = call(
        slab_inside,
        (f32(SLAB_MOST, 8, S), f32(16, 8, S)),
        (VMEM, VMEM),
        [SMEM] + [VMEM] * 7,
        [pltpu.VMEM((SLAB, S), jnp.float32)] + work((SX + 2) * SY, 48),
        6,
    )(places, own, zlo, zhi, xlo, xhi, tiles, sums)
    return call(
        finish,
        (f32(SX, SY, SZ, S), f32(3, SX, SY, SZ, S)),
        (VMEM, VMEM),
        [ANY] + [VMEM] * 7,
        [
            pltpu.SMEM((8, 128), jnp.int32),
            pltpu.SemaphoreType.DMA,
            pltpu.VMEM((4 * Y_ROWS, S), jnp.float32),
            pltpu.VMEM((ALL_MOST * 8, S), jnp.float32),
            pltpu.VMEM((16, 8, S), jnp.float32),
            pltpu.SMEM((4, ALL_MOST), jnp.int32),
            pltpu.VMEM((16, S), jnp.int32),
            pltpu.SMEM((16, S), jnp.int32),
            pltpu.SemaphoreType.DMA,
        ]
        + work(2 * (SX + 2), ALL_MOST + 16),
        8,
    )(places, ylo, yhi, y_up, y_down, tiles, sums, density_old)


def solution(mesh):
    return jax.shard_map(
        per_device,
        mesh=mesh,
        in_specs=(
            P(None, "gx", "gy", "gz", None),
            P("gx", "gy", "gz", None),
            P("gx", "gy", "gz", None),
            P("gx", "gy", "gz"),
            P("gx", "gy", "gz", None),
            P("gx", "gy", "gz", None),
            P("gx", "gy", "gz"),
        ),
        out_specs=(P("gx", "gy", "gz", None), P(None, "gx", "gy", "gz", None)),
        check_vma=False,
    )
```

```python
import functools
import math

import jax
import jax.numpy as jnp
from jax import lax
from jax.experimental import pallas as pl
from jax.experimental.pallas import tpu as pltpu
from jax.sharding import PartitionSpec as P

KC = 21.0 / (2.0 * math.pi)
SX, SY, SZ, S = 12, 6, 6, 128
MOST = 9
CELLS = SX * SY * SZ

ZERO = CELLS * 8
OWN_TAIL = ZERO + 8
OWN_ROWS = OWN_TAIL + 8

Z_TWO, Z_FAR, Z_TAIL, Z_ROWS = 288, 432, 720, 728
X_TWO, X_FAR, X_TAIL, X_ROWS = 240, 336, 576, 584
Y_TWO, Y_SUM, Y_TAIL, Y_ROWS = 640, 864, 976, 984

ZLO = OWN_ROWS
ZHI = ZLO + Z_ROWS
XLO = ZHI + Z_ROWS
XHI = XLO + X_ROWS
SLAB = XHI + X_ROWS

FIRST_PART = 8000
SLAB_MOST = 96
ALL_MOST = 256

VMEM = pl.BlockSpec(memory_space=pltpu.VMEM)
SMEM = pl.BlockSpec(memory_space=pltpu.SMEM)
ANY = pl.BlockSpec(memory_space=pl.ANY)
PARAMS = pltpu.CompilerParams(vmem_limit_bytes=40 * 1024 * 1024)

BLOCKS = [(0, 0), (0, -1), (0, 1), (-1, 0), (-1, -1), (-1, 1), (1, 0), (1, -1), (1, 1)]


def step(mode, i, near, sums):
    xi, yi, zi, hi, bi = i
    xj, yj, zj, mj, hj, wj = near
    dx, dy, dz = xi - xj, yi - yj, zi - zj
    sq = jnp.maximum(dx * dx + dy * dy + dz * dz, 1e-30)
    dist = sq * lax.rsqrt(sq)
    out = []
    if mode != "near":
        wi = jnp.maximum(hi - dist, 0.0)
        own = mj * (wi * wi * wi)
        out.append(sums[0] + own * (wi * (bi - wi)))
        if mode == "all":
            out += [sums[1] + own * dx, sums[2] + own * dy, sums[3] + own * dz]
    if mode != "density":
        wj_ = jnp.maximum(hj - dist, 0.0)
        other = wj * (wj_ * wj_ * wj_)
        last = sums[-3:]
        out += [last[0] + other * dx, last[1] + other * dy, last[2] + other * dz]
    return tuple(out)


WIDTH = {"all": 7, "density": 1, "near": 3}
FIRST = {"all": 0, "density": 0, "near": 4}
NEAR = {"all": 3, "density": 9, "near": 1}
GROUPS = {"all": 2, "density": 2, "near": 8}


def pairs(mode, src, four, two, use, count, used, tile, cols, table, many=None):
    many, regs = many or NEAR[mode], GROUPS[mode]
    for u in range(many - 1):
        four[count + u] = jnp.int32(0)
        if two is not None:
            two[count + u] = jnp.int32(0)
        use[count + u] = jnp.float32(0.0)
    steps = lax.div(count + (many - 1), many)
    for n, c in enumerate((0, 1, 2, 4)):
        if mode == "near" and n == 3:
            break
        cols[n] = jnp.broadcast_to(tile[c : c + 1], (128, 128)).T
    width = WIDTH[mode]
    zero = jnp.zeros((8, 128), jnp.float32)

    def group(g, _):
        spots, own = [], []
        for v in range(regs):
            spot = pl.ds(pl.multiple_of((g * regs + v) * 8, 8), 8)
            x, y, z = [cols[n, spot, :] for n in range(3)]
            h = cols[3, spot, :] if mode != "near" else None
            spots.append(spot)
            own.append((x, y, z, h, 1.25 * h if mode != "near" else None))

        def body(q, sums):
            sums = list(sums)
            for u in range(many):
                at = q * many + u
                f = four[at]
                near = [
                    jnp.broadcast_to(src[pl.ds(f + c, 1), :], (8, 128)) for c in range(4)
                ]
                flag = use[at]
                if mode != "near":
                    near[3] = near[3] * jnp.where(flag >= 0.5, 1.0, 0.0)
                if mode != "density":
                    t = f + 4 if two is None else two[at]
                    near.append(jnp.broadcast_to(src[pl.ds(t, 1), :], (8, 128)))
                    weight = jnp.broadcast_to(src[pl.ds(t + 1, 1), :], (8, 128))
                    near.append(weight * jnp.where(flag == 1.0, 1.0, 0.0))
                else:
                    near += [None, None]
                for v in range(regs):
                    sums[v] = step(mode, own[v], near, sums[v])
            return tuple(sums)

        sums = lax.fori_loop(0, steps, body, ((zero,) * width,) * regs)
        for v in range(regs):
            for c in range(width):
                table[c, spots[v], :] = sums[v][c]
        return 0

    lax.fori_loop(0, lax.div(used + (8 * regs - 1), 8 * regs), group, 0)
    lines = [jnp.sum(table[c].T, axis=0, keepdims=True) for c in range(width)]
    if mode == "density":
        return lines[0]
    before = [jnp.zeros((1, 128), jnp.float32)] * FIRST[mode]
    after = [jnp.zeros((1, 128), jnp.float32)] * (8 - FIRST[mode] - width)
    return jnp.concatenate(before + lines + after, axis=0)


def bit(word, at):
    return lax.shift_right_logical(word, at) & 1


def clear(words, count):
    def one(k, _):
        words[k] = jnp.int32(0)
        return 0

    lax.fori_loop(0, count, one, 0, unroll=14)


def mark(words, at, place):
    words[at] = words[at] | lax.shift_left(jnp.int32(1), place)


def corner(code):
    return lax.shift_right_logical(code, 6), lax.shift_right_logical(code, 3) & 7, code & 7


def pack(
    counts_in, active_in, pos_in, mass_in, support_in, entropy_in, old_in, own_out, up, down, ids,
    counts, active, pos, mass, support, entropy, old, own, sems, out_sems,
):
    given = (active_in, counts_in, pos_in, mass_in, support_in, entropy_in, old_in)
    held = (active, counts, pos, mass, support, entropy, old)
    copies = [pltpu.make_async_copy(a, b, sems.at[n]) for n, (a, b) in enumerate(zip(given, held))]
    for copy in copies:
        copy.start()
    copies[0].wait()

    for copy in copies[1:]:
        copy.wait()
    own[ZERO : ZERO + 8] = jnp.zeros((8, 128), jnp.float32)
    size = SY * SZ * 8

    def plane(x):
        spot = pl.ds(pl.multiple_of(x * size, 8), size)
        return pltpu.make_async_copy(own.at[spot], own_out.at[spot], out_sems.at[x])

    sub = lax.broadcasted_iota(jnp.int32, (SZ, 128), 0)
    slot = lax.broadcasted_iota(jnp.int32, (SZ, 128), 1)

    def cells(x, n):
        for y in range(SY):
            many = jnp.zeros((SZ, 128), jnp.int32)
            act = jnp.zeros((SZ, 128), jnp.int32)
            for z in range(SZ):
                many = jnp.where(sub == z, counts[y, z, x], many)
                here = active[y, z, x]
                act = jnp.where(sub == z, here, act)
                ids[n] = x * 64 + y * 8 + z
                n = n + here
            h = support[x, y]
            inv = 1.0 / h
            inv2 = inv * inv
            inv4 = inv2 * inv2
            m = jnp.where(slot < many, mass[x, y], 0.0)
            gain = entropy[x, y] * (inv4 * inv4)
            power = jnp.exp(jnp.log(old[x, y]) * (-1.0 / 3.0))
            weight = m * gain * jnp.where(act > 0, 1.0, power)
            base = pl.multiple_of(x * (SY * SZ * 8), 8) + y * SZ * 8
            for c, value in enumerate(
                (pos[0, x, y], pos[1, x, y], pos[2, x, y], m, h, weight, gain)
            ):
                own[pl.ds(base + c, SZ, stride=8), :] = value
        plane(x).start()
        return n

    number = lax.fori_loop(0, SX, cells, jnp.int32(0))
    ids[15] = number
    lane = lax.broadcasted_iota(jnp.int32, (8, 128), 1)

    def tell(s, tail):
        code = ids[s]
        x, y, z = corner(code)
        ids[16 + s] = counts[y, z, x]
        tail = jnp.where(lane == s, code, tail)
        return jnp.where(lane == 16 + s, counts[y, z, x], tail)

    tail = lax.fori_loop(0, number, tell, jnp.where(lane == 15, number, 0)).astype(jnp.float32)
    own[OWN_TAIL : OWN_TAIL + 8] = tail
    up[Z_TAIL : Z_TAIL + 8] = tail
    down[Z_TAIL : Z_TAIL + 8] = tail
    rest = pltpu.make_async_copy(own.at[pl.ds(ZERO, 16)], own_out.at[pl.ds(ZERO, 16)], out_sems.at[SX])
    rest.start()

    def faces(x2, _):
        for u in range(2):
            for y in range(SY):
                base = pl.multiple_of(x2 * (2 * SY * SZ * 8), 8) + (u * SY + y) * SZ * 8
                four = pl.multiple_of(x2 * (2 * SY * 4), 8) + (u * SY + y) * 4
                two = pl.multiple_of(x2 * (2 * SY * 2), 8) + (u * SY + y) * 2
                for out, z1, z2 in ((up, SZ - 1, SZ - 2), (down, 0, 1)):
                    out[pl.ds(four, 4), :] = own[pl.ds(base + z1 * 8, 4), :]
                    out[pl.ds(two + Z_TWO, 2), :] = own[pl.ds(base + z1 * 8 + 4, 2), :]
                    out[pl.ds(four + Z_FAR, 4), :] = own[pl.ds(base + z2 * 8, 4), :]
        return 0

    lax.fori_loop(0, SX // 2, faces, 0)

    def finished(x, _):
        plane(x).wait()
        return 0

    lax.fori_loop(0, SX, finished, 0)
    rest.wait()


def own_row(x, y, z):
    return ((x * SY + y) * SZ + z) * 8


def local(part, ids, own, before, sums, four, two, use, flags, cols, table):
    number = ids[15]

    def price(s):
        x, y, z = corner(ids[s])

        def span(at, size):
            return 3 - (at == 0).astype(jnp.int32) - (at == size - 1).astype(jnp.int32)

        near = span(x, SX) * span(y, SY) * span(z, SZ)
        return near * lax.shift_right_logical(ids[16 + s] + 15, 4) * 14 + 400

    total = lax.fori_loop(0, number, lambda s, n: n + price(s), jnp.int32(0))
    limit = jnp.maximum(jnp.int32(FIRST_PART), lax.shift_right_logical(total, 1))

    def fits(s, state):
        n, spent = state
        spent = spent + price(s)
        return n + (spent <= limit).astype(jnp.int32), spent

    half, _ = lax.fori_loop(0, number, fits, (jnp.int32(0), jnp.int32(0)))

    clear(flags, SX * SY)

    def one(s, _):
        x, y, z = corner(ids[s])
        mark(flags, x * SY + y, z)
        return 0

    lax.fori_loop(0, number, one, 0)
    if before is not None:
        sums[...] = before[...]

    def slot(s, _):
        a, b, d = corner(ids[s])
        count = jnp.int32(0)
        in_z = [(d + ed >= 0) & (d + ed < SZ) for ed in (-1, 0, 1)]
        for ea in (-1, 0, 1):
            for eb in (-1, 0, 1):
                na, nb = a + ea, b + eb
                inside = (na >= 0) & (na < SX) & (nb >= 0) & (nb < SY)
                column = na * SY + nb
                word = flags[jnp.where(inside, column, 0)]
                row = column * (SZ * 8) + d * 8
                for n, ed in enumerate((-1, 0, 1)):
                    four[count] = row + ed * 8
                    known = bit(word, jnp.maximum(d + ed, 0))
                    use[count] = jnp.where(known > 0, jnp.float32(0.5), jnp.float32(1.0))
                    count = count + (inside & in_z[n]).astype(jnp.int32)
        tile = own[pl.ds(pl.multiple_of(own_row(a, b, d), 8), 8), :]
        sums[s] = pairs("all", own, four, None, use, count, ids[16 + s], tile, cols, table, 6)
        return 0

    if part == 0:
        lax.fori_loop(0, half, slot, 0)
    else:
        lax.fori_loop(half, number, slot, 0)


def local_first(ids, own, sums, *scratch):
    local(0, ids, own, None, sums, *scratch)


def local_second(ids, own, before, _, sums, *scratch):
    local(1, ids, own, before, sums, *scratch)


def pack_x(own, zlo, zhi, _, up, down):
    for out, x1, x2 in ((up, SX - 1, SX - 2), (down, 0, 1)):
        for y in range(SY):
            for z in range(-2, SZ + 2):
                for x, base in ((x1, 0), (x2, X_FAR)):
                    spot = base + (y * (SZ + 4) + z + 2) * 4
                    if 0 <= z < SZ:
                        row = own_row(x, y, z)
                        out[spot : spot + 4] = own[row : row + 4]
                    else:
                        src = zlo if z < 0 else zhi
                        far = Z_FAR if z in (-2, SZ + 1) else 0
                        row = far + (x * SY + y) * 4
                        out[spot : spot + 4] = src[row : row + 4]
                if -1 <= z <= SZ:
                    spot = X_TWO + (y * (SZ + 2) + z + 1) * 2
                    if 0 <= z < SZ:
                        row = own_row(x1, y, z) + 4
                        out[spot : spot + 2] = own[row : row + 2]
                    else:
                        src = zlo if z < 0 else zhi
                        row = Z_TWO + (x1 * SY + y) * 2
                        out[spot : spot + 2] = src[row : row + 2]
        out[X_TAIL : X_TAIL + 8] = jnp.zeros((8, 128), jnp.float32)
        out[X_TAIL : X_TAIL + 1] = own[OWN_TAIL : OWN_TAIL + 1]
        out[X_TAIL + 1 : X_TAIL + 2] = zlo[Z_TAIL : Z_TAIL + 1]
        out[X_TAIL + 2 : X_TAIL + 3] = zhi[Z_TAIL : Z_TAIL + 1]


def slab_rows(x, z):
    zlow, xlow = z < 0, x < 0
    zout = zlow | (z >= SZ)
    xout = xlow | (x >= SX)
    zbase = jnp.where(zlow, ZLO, ZHI)
    zfar = jnp.where((z == -2) | (z == SZ + 1), Z_FAR, 0)
    xbase = jnp.where(xlow, XLO, XHI)
    xfar = jnp.where((x == -2) | (x == SX + 1), X_FAR, 0)
    four = jnp.where(zout, zbase + zfar + x * (SY * 4), x * (SY * SZ * 8) + z * 8)
    two = jnp.where(zout, zbase + Z_TWO + x * (SY * 2), x * (SY * SZ * 8) + z * 8 + 4)
    four = jnp.where(xout, xbase + xfar + (z + 2) * 4, four)
    two = jnp.where(xout, xbase + X_TWO + (z + 1) * 2, two)
    add4 = jnp.where(xout, (SZ + 4) * 4, jnp.where(zout, 4, SZ * 8))
    add2 = jnp.where(xout, (SZ + 2) * 2, jnp.where(zout, 2, SZ * 8))
    return four, two, add4, add2


def slab_rows_at(x, y, z):
    if 0 <= x < SX and 0 <= z < SZ:
        return own_row(x, y, z), own_row(x, y, z) + 4
    if 0 <= x < SX:
        base, far, k = ZLO if z < 0 else ZHI, z in (-2, SZ + 1), x * SY + y
        return base + (Z_FAR if far else 0) + k * 4, base + Z_TWO + k * 2
    base, far = XLO if x < 0 else XHI, x in (-2, SX + 1)
    four = base + (X_FAR if far else 0) + (y * (SZ + 4) + z + 2) * 4
    return four, base + X_TWO + (y * (SZ + 2) + z + 1) * 2


def gather(rows, own, zlo, zhi, xlo, xhi):
    rows[0:OWN_ROWS] = own[...]
    rows[ZLO:ZHI] = zlo[...]
    rows[ZHI:XLO] = zhi[...]
    rows[XLO:XHI] = xlo[...]
    rows[XHI:SLAB] = xhi[...]


def slab_tools(rows, four, two, use, flags, cols, table):
    def near_list(x, y, z, own_cell):
        count = jnp.int32(0)
        for ea in (-1, 0, 1):
            for ed in (-1, 0, 1):
                na, nd = x + ea, z + ed
                f4, f2, add4, add2 = slab_rows(na, nd)
                if own_cell:
                    outer = (na < 0) | (na >= SX) | (nd < 0) | (nd >= SZ)
                for eb in (-1, 0, 1):
                    nb = y + eb
                    wanted = (nb >= 0) & (nb < SY)
                    four[count] = f4 + nb * add4
                    if own_cell:
                        wanted = wanted & outer
                        two[count] = f2 + nb * add2
                        word = flags[(na + 1) * SY + jnp.where(wanted, nb, 0)]
                        known = bit(word, nd + 1)
                        use[count] = jnp.where(known > 0, jnp.float32(0.5), jnp.float32(1.0))
                    else:
                        use[count] = jnp.float32(1.0)
                    count = count + wanted.astype(jnp.int32)
        return count

    def cell(x, y, z):
        f4, f2, add4, add2 = slab_rows(x, z)
        first = rows[pl.ds(f4 + y * add4, 4), :]
        second = rows[pl.ds(f2 + y * add2, 2), :]
        return jnp.concatenate([first, second, jnp.zeros((2, 128), jnp.float32)], axis=0)

    def own_sums(x, y, z, used):
        count = near_list(x, y, z, True)
        return pairs("all", rows, four, two, use, count, used, cell(x, y, z), cols, table)

    def halo_cell(x, y, z, used):
        count = near_list(x, y, z, False)
        tile = cell(x, y, z)
        return tile, pairs("density", rows, four, None, use, count, used, tile, cols, table)

    return own_sums, halo_cell


def beside(places, mine, x, y, z):
    def one(t, found):
        close = (
            (jnp.abs(places[0, t] - x) <= 1)
            & (jnp.abs(places[1, t] - y) <= 1)
            & (jnp.abs(places[2, t] - z) <= 1)
        )
        return found | close.astype(jnp.int32)

    return lax.fori_loop(0, mine, one, jnp.int32(0)) > 0


def on_border(x, z):
    return (x == 0) | (x == SX - 1) | (z == 0) | (z == SZ - 1)


def on_face(y):
    return (y == 0) | (y == SY - 1)


def weigh(cells, total):
    def some(q, _):
        base = pl.multiple_of(q * 64, 64)

        def get(c):
            return cells[pl.ds(base + c, 8, stride=8), :]

        good = get(3) > 0.0
        inv = 1.0 / jnp.where(good, get(4), 1.0)
        inv2 = inv * inv
        inv4 = inv2 * inv2
        fresh = (4.0 * KC) * (inv4 * inv4) * get(6)
        safe = jnp.where(good, fresh, 1.0)
        power = jnp.exp(jnp.log(safe) * (-1.0 / 3.0))
        weight = get(5) * power
        cells[pl.ds(base + 5, 8, stride=8), :] = jnp.where(good, weight, 0.0)
        cells[pl.ds(base + 6, 8, stride=8), :] = safe
        cells[pl.ds(base + 7, 8, stride=8), :] = power
        return 0

    lax.fori_loop(0, lax.div(total + 7, 8), some, 0)


def slab_faces(
    own, zlo, zhi, xlo, xhi, before, up, down, tiles, sums, places,
    rows, tails, lists, sem, four, two, use, flags, cols, table,
):
    tails[...] = jnp.zeros(tails.shape, jnp.int32)
    tails[0:1] = own[OWN_TAIL : OWN_TAIL + 1].astype(jnp.int32)
    tails[1:2] = zlo[Z_TAIL : Z_TAIL + 1].astype(jnp.int32)
    tails[2:3] = zhi[Z_TAIL : Z_TAIL + 1].astype(jnp.int32)
    tails[3:6] = xlo[X_TAIL : X_TAIL + 3].astype(jnp.int32)
    tails[6:9] = xhi[X_TAIL : X_TAIL + 3].astype(jnp.int32)
    copy = pltpu.make_async_copy(tails, lists, sem)
    copy.start()
    gather(rows, own, zlo, zhi, xlo, xhi)

    clear(flags, (SX + 2) * SY)
    for out, y in ((up, SY - 1), (down, 0)):
        for x in range(-2, SX + 2):
            for z in range(-2, SZ + 2):
                row4, row2 = slab_rows_at(x, y, z)
                spot = ((x + 2) * (SZ + 4) + z + 2) * 4
                out[spot : spot + 4] = rows[row4 : row4 + 4]
                if -1 <= x <= SX and -1 <= z <= SZ:
                    spot = Y_TWO + ((x + 1) * (SZ + 2) + z + 1) * 2
                    out[spot : spot + 2] = rows[row2 : row2 + 2]
        out[Y_SUM:Y_TAIL] = jnp.zeros((Y_TAIL - Y_SUM, 128), jnp.float32)
    copy.wait()

    number = jnp.int32(0)
    for q, (bx, bz) in enumerate(BLOCKS):

        def one(s, n, q=q, bx=bx, bz=bz):
            a, b, d = corner(lists[q, s])
            x, z = a + bx * SX, d + bz * SZ
            inside = (x >= -1) & (x <= SX) & (z >= -1) & (z <= SZ)
            places[0, n] = x
            places[1, n] = b
            places[2, n] = z
            places[3, n] = lists[q, 16 + s]

            @pl.when(inside)
            def _():
                mark(flags, (x + 1) * SY + b, z + 1)

            return n + inside.astype(jnp.int32)

        number = lax.fori_loop(0, lists[q, 15], one, number)
    places[4, 0] = number
    places[4, 1] = lists[0, 15]
    mine = lists[0, 15]

    lane = lax.broadcasted_iota(jnp.int32, (8, 128), 1)
    line = lax.broadcasted_iota(jnp.int32, (8, 128), 0)

    def tell(s, state):
        lists_, numbers = list(state[0]), list(state[1])
        x, y, z = places[0, s], places[1, s], places[2, s]
        for n, edge in enumerate((SY - 1, 0)):
            here = y == edge
            at = jnp.where(here, numbers[n], 126)
            value = jnp.where(line == 0, x, jnp.where(line == 1, z, places[3, s]))
            lists_[n] = jnp.where(lane == at, value, lists_[n])
            numbers[n] = numbers[n] + here.astype(jnp.int32)
        return tuple(lists_), tuple(numbers)

    nothing = jnp.zeros((8, 128), jnp.int32)
    told, numbers = lax.fori_loop(
        0, number, tell, ((nothing, nothing), (jnp.int32(0), jnp.int32(0)))
    )
    for n, out in enumerate((up, down)):
        out[Y_TAIL:Y_ROWS] = jnp.where(lane == 127, numbers[n], told[n]).astype(jnp.float32)

    own_sums, halo_cell = slab_tools(rows, four, two, use, flags, cols, table)

    def send_sum(s, x, y, z):
        spot = Y_SUM + (x + 1) * (SZ + 2) + z + 1

        @pl.when(y == 0)
        def _():
            down[pl.ds(spot, 1), :] = tiles[s, 6:7]

        @pl.when(y == SY - 1)
        def _():
            up[pl.ds(spot, 1), :] = tiles[s, 6:7]

    def own_slot(s, _):
        x, y, z = places[0, s], places[1, s], places[2, s]
        sums[s] = before[s]
        row = pl.multiple_of(own_row(x, y, z), 8)
        whole = rows[pl.ds(row, 8), :]
        tiles[s] = whole

        @pl.when(on_face(y))
        def _():
            @pl.when(on_border(x, z))
            def _():
                sums[s] = sums[s] + own_sums(x, y, z, places[3, s])

            tiles[s, 6:7] = sums[s, 0:1]
            send_sum(s, x, y, z)

        sums[s, 7:8] = whole[6:7]
        return 0

    def halo_slot(s, _):
        x, y, z = places[0, s], places[1, s], places[2, s]

        @pl.when(on_face(y))
        def _():
            tiles[s], total = halo_cell(x, y, z, places[3, s])
            tiles[s, 6:7] = total
            send_sum(s, x, y, z)

        return 0

    lax.fori_loop(0, mine, own_slot, 0)
    lax.fori_loop(mine, number, halo_slot, 0)


def slab_inside(
    places, own, zlo, zhi, xlo, xhi, tiles_in, sums_in, tiles, sums,
    cells, rows, four, two, use, flags, cols, table,
):
    gather(rows, own, zlo, zhi, xlo, xhi)
    tiles[...] = tiles_in[...]
    sums[...] = sums_in[...]
    number, mine = places[4, 0], places[4, 1]
    clear(flags, (SX + 2) * SY)

    def one(s, _):
        mark(flags, (places[0, s] + 1) * SY + places[1, s], places[2, s] + 1)
        return 0

    lax.fori_loop(0, number, one, 0)
    own_sums, halo_cell = slab_tools(rows, four, two, use, flags, cols, table)

    def own_slot(s, _):
        x, y, z = places[0, s], places[1, s], places[2, s]

        @pl.when(jnp.logical_not(on_face(y)))
        def _():
            @pl.when(on_border(x, z))
            def _():
                sums[s, 0:7] = sums[s, 0:7] + own_sums(x, y, z, places[3, s])[0:7]

            tiles[s, 6:7] = sums[s, 0:1]

        return 0

    def halo_slot(s, _):
        x, y, z = places[0, s], places[1, s], places[2, s]

        @pl.when(jnp.logical_not(on_face(y)) & beside(places, mine, x, y, z))
        def _():
            tiles[s], total = halo_cell(x, y, z, places[3, s])
            tiles[s, 6:7] = total

        return 0

    lax.fori_loop(0, mine, own_slot, 0)
    lax.fori_loop(mine, number, halo_slot, 0)

    def take(s, _):
        cells[pl.ds(pl.multiple_of(s * 8, 8), 8), :] = tiles[s]
        return 0

    lax.fori_loop(0, number, take, 0)
    weigh(cells, number)

    def inner(s, _):
        x, y, z = places[0, s], places[1, s], places[2, s]

        def check(t, n):
            close = (
                (jnp.abs(places[0, t] - x) <= 1)
                & (jnp.abs(places[1, t] - y) <= 1)
                & (jnp.abs(places[2, t] - z) <= 1)
                & jnp.logical_not(on_face(places[1, t]))
            )
            four[n] = t * 8
            use[n] = jnp.float32(1.0)
            return n + close.astype(jnp.int32)

        count = lax.fori_loop(0, number, check, jnp.int32(0))

        @pl.when(count > 0)
        def _():
            tile = cells[pl.ds(pl.multiple_of(s * 8, 8), 8), :]
            sums[s, 4:7] = sums[s, 4:7] + pairs(
                "near", cells, four, None, use, count, places[3, s], tile, cols, table
            )[4:7]

        return 0

    lax.fori_loop(0, mine, inner, 0)


def finish(
    places_in, ylo, yhi, up, down, tiles, sums, old, density, accel,
    places, places_sem, rows, cells, final, spots, tails, lists, sem, four, two, use, flags, cols, table,
):
    tails[0:8] = ylo[Y_TAIL:Y_ROWS].astype(jnp.int32)
    tails[8:16] = yhi[Y_TAIL:Y_ROWS].astype(jnp.int32)
    copy = pltpu.make_async_copy(tails, lists, sem)
    copy.start()
    other = pltpu.make_async_copy(places_in, places, places_sem)
    other.start()
    rows[0:Y_ROWS] = ylo[...]
    rows[Y_ROWS : 2 * Y_ROWS] = yhi[...]
    rows[2 * Y_ROWS : 3 * Y_ROWS] = down[...]
    rows[3 * Y_ROWS : 4 * Y_ROWS] = up[...]
    density[...] = old[...]
    accel[...] = jnp.zeros(accel.shape, jnp.float32)
    clear(flags, 2 * (SX + 2))
    other.wait()
    number, mine = places[4, 0], places[4, 1]

    def take(s, n):
        for c in range(4):
            spots[c, n] = places[c, s]
        cells[pl.ds(pl.multiple_of(n * 8, 8), 8), :] = tiles[s]
        wanted = beside(places, mine, places[0, s], places[1, s], places[2, s])
        return n + wanted.astype(jnp.int32)

    total = lax.fori_loop(0, number, take, jnp.int32(0))
    final[...] = sums[...]
    copy.wait()
    for side in range(2):

        def one(s, n, side=side):
            x, z = lists[side * 8, s], lists[side * 8 + 1, s]
            spots[0, n] = x
            spots[1, n] = jnp.int32(-1 if side == 0 else SY)
            spots[2, n] = z
            spots[3, n] = lists[side * 8 + 2, s]
            mark(flags, side * (SX + 2) + x + 1, z + 1)
            at = (x + 1) * (SZ + 2) + z + 1
            base = side * Y_ROWS
            row4 = base + ((x + 2) * (SZ + 4) + z + 2) * 4
            row2 = base + Y_TWO + at * 2
            cells[pl.ds(pl.multiple_of(n * 8, 8), 8), :] = jnp.concatenate(
                [
                    rows[pl.ds(row4, 4), :],
                    rows[pl.ds(row2, 2), :],
                    rows[pl.ds(base + Y_SUM + at, 1), :],
                    jnp.zeros((1, 128), jnp.float32),
                ],
                axis=0,
            )
            wanted = beside(spots, mine, x, jnp.int32(-1 if side == 0 else SY), z)
            return n + wanted.astype(jnp.int32)

        total = lax.fori_loop(0, lists[side * 8, 127], one, total)

    def near_list(s, own_cell):
        x, y, z = spots[0, s], spots[1, s], spots[2, s]
        high = y >= SY - 1
        outer = (y == -1) | (y == SY)
        base = jnp.where(outer, 2 * Y_ROWS, 0) + jnp.where(high, Y_ROWS, 0)
        for e, (ea, ed) in enumerate((p, q) for p in (-1, 0, 1) for q in (-1, 0, 1)):
            na, nd = x + ea, z + ed
            four[e] = base + ((na + 2) * (SZ + 4) + nd + 2) * 4
            use[e] = jnp.float32(1.0)
            if own_cell:
                two[e] = base + Y_TWO + ((na + 1) * (SZ + 2) + nd + 1) * 2
                word = flags[jnp.where(high, SX + 2, 0) + na + 1]
                use[e] = jnp.where(bit(word, nd + 1) > 0, jnp.float32(0.5), jnp.float32(1.0))

    def across_own(s, _):
        y = spots[1, s]

        @pl.when((y <= 0) | (y >= SY - 1))
        def _():
            near_list(s, True)
            spot = pl.multiple_of(s * 8, 8)
            tile = cells[pl.ds(spot, 8), :]
            count = jnp.int32(9)
            result = pairs("all", rows, four, two, use, count, spots[3, s], tile, cols, table, 9)
            final[s, 0:7] = final[s, 0:7] + result[0:7]
            cells[pl.ds(spot + 6, 1), :] = tile[6:7] + result[0:1]

        return 0

    def across_halo(s, _):
        y = spots[1, s]

        @pl.when((y <= 0) | (y >= SY - 1))
        def _():
            near_list(s, False)
            spot = pl.multiple_of(s * 8, 8)
            tile = cells[pl.ds(spot, 8), :]
            count = jnp.int32(9)
            result = pairs("density", rows, four, None, use, count, spots[3, s], tile, cols, table)
            cells[pl.ds(spot + 6, 1), :] = tile[6:7] + result

        return 0

    lax.fori_loop(0, mine, across_own, 0)
    lax.fori_loop(mine, total, across_halo, 0)

    weigh(cells, total)

    def last(s, _):
        x, y, z = spots[0, s], spots[1, s], spots[2, s]

        def check(t, n):
            close = (
                (jnp.abs(spots[0, t] - x) <= 1)
                & (jnp.abs(spots[1, t] - y) <= 1)
                & (jnp.abs(spots[2, t] - z) <= 1)
                & ((spots[1, t] <= 0) | (spots[1, t] >= SY - 1))
            )
            four[n] = t * 8
            use[n] = jnp.float32(1.0)
            return n + close.astype(jnp.int32)

        count = lax.fori_loop(0, total, check, jnp.int32(0))
        spot = pl.multiple_of(s * 8, 8)
        tile = cells[pl.ds(spot, 8), :]

        @pl.when(count > 0)
        def _():
            final[s, 4:7] = final[s, 4:7] + pairs(
                "near", cells, four, None, use, count, spots[3, s], tile, cols, table
            )[4:7]

        good = tile[3:4] > 0.0
        own = final[s, 7:8] * tile[7:8]
        place = (x, y, pl.ds(z, 1), slice(None))
        density[place] = jnp.where(good, tile[6:7], old[place])
        for c in range(3):
            push = (20.0 * KC) * (own * final[s, 1 + c : 2 + c] + final[s, 4 + c : 5 + c])
            accel[(c, *place)] = jnp.where(good, push, 0.0)
        return 0

    lax.fori_loop(0, mine, last, 0)


def f32(*shape):
    return jax.ShapeDtypeStruct(shape, jnp.float32)


def i32(*shape):
    return jax.ShapeDtypeStruct(shape, jnp.int32)


def neighbours(up, down, axis):
    size = lax.axis_size(axis)
    pairs_ = [(i, i + 1) for i in range(size - 1)]
    low = lax.ppermute(up, axis, pairs_)
    high = lax.ppermute(down, axis, [(j, i) for i, j in pairs_])
    return low, high


def work(flags, near):
    return [
        pltpu.SMEM((near,), jnp.int32),
        pltpu.SMEM((near,), jnp.int32),
        pltpu.SMEM((near,), jnp.float32),
        pltpu.SMEM((flags,), jnp.int32),
        pltpu.VMEM((4, 128, 128), jnp.float32),
        pltpu.VMEM((7, 128, 128), jnp.float32),
    ]


def cost(us):
    return pl.CostEstimate(flops=us * 10_000_000, bytes_accessed=us * 2_000_000, transcendentals=0)


def call(body, outs, out_specs, in_specs, scratch, us, limit=40):
    return pl.pallas_call(
        body,
        out_shape=outs,
        in_specs=in_specs,
        out_specs=out_specs,
        scratch_shapes=scratch,
        compiler_params=pltpu.CompilerParams(vmem_limit_bytes=limit * 1024 * 1024),
        cost_estimate=cost(us),
    )


def per_device(positions, mass, support, counts, entropy, density_old, active):
    small = [jnp.transpose(v, (1, 2, 0)) for v in (counts, active)]
    own, z_up, z_down, ids = call(
        pack,
        (f32(OWN_ROWS, S), f32(Z_ROWS, S), f32(Z_ROWS, S), i32(32)),
        (ANY, VMEM, VMEM, SMEM),
        [ANY] * 7,
        [
            pltpu.SMEM((SY, SZ, SX), jnp.int32),
            pltpu.SMEM((SY, SZ, SX), jnp.int32),
            pltpu.VMEM((3, SX, SY, SZ, S), jnp.float32),
        ]
        + [pltpu.VMEM((SX, SY, SZ, S), jnp.float32)] * 4
        + [
            pltpu.VMEM((OWN_ROWS, S), jnp.float32),
            pltpu.SemaphoreType.DMA((7,)),
            pltpu.SemaphoreType.DMA((SX + 1,)),
        ],
        2,
        56,
    )(*small, positions, mass, support, entropy, density_old)
    zlo, zhi = neighbours(z_up, z_down, "gz")
    first = call(
        local_first, f32(16, 8, S), VMEM, [SMEM, VMEM], work(SX * SY, 48), 8
    )(ids, own)
    x_up, x_down = call(
        pack_x, (f32(X_ROWS, S), f32(X_ROWS, S)), (VMEM, VMEM), [VMEM] * 3 + [ANY], [], 1
    )(own, zlo, zhi, first)
    xlo, xhi = neighbours(x_up, x_down, "gx")
    second = call(
        local_second,
        f32(16, 8, S),
        VMEM,
        [SMEM, VMEM, VMEM, ANY],
        work(SX * SY, 48),
        8,
    )(ids, own, first, x_up)
    y_up, y_down, tiles, sums, places = call(
        slab_faces,
        (f32(Y_ROWS, S), f32(Y_ROWS, S), f32(SLAB_MOST, 8, S), f32(16, 8, S), i32(8, 128)),
        (VMEM, VMEM, VMEM, VMEM, SMEM),
        [VMEM] * 6,
        [
            pltpu.VMEM((SLAB, S), jnp.float32),
            pltpu.VMEM((16, S), jnp.int32),
            pltpu.SMEM((16, S), jnp.int32),
            pltpu.SemaphoreType.DMA,
        ]
        + work((SX + 2) * SY, 48),
        4,
    )(own, zlo, zhi, xlo, xhi, second)
    ylo, yhi = neighbours(y_up, y_down, "gy")
    tiles, sums = call(
        slab_inside,
        (f32(SLAB_MOST, 8, S), f32(16, 8, S)),
        (VMEM, VMEM),
        [SMEM] + [VMEM] * 7,
        [pltpu.VMEM((SLAB_MOST * 8, S), jnp.float32), pltpu.VMEM((SLAB, S), jnp.float32)]
        + work((SX + 2) * SY, SLAB_MOST + 16),
        6,
    )(places, own, zlo, zhi, xlo, xhi, tiles, sums)
    return call(
        finish,
        (f32(SX, SY, SZ, S), f32(3, SX, SY, SZ, S)),
        (VMEM, VMEM),
        [ANY] + [VMEM] * 7,
        [
            pltpu.SMEM((8, 128), jnp.int32),
            pltpu.SemaphoreType.DMA,
            pltpu.VMEM((4 * Y_ROWS, S), jnp.float32),
            pltpu.VMEM((ALL_MOST * 8, S), jnp.float32),
            pltpu.VMEM((16, 8, S), jnp.float32),
            pltpu.SMEM((4, ALL_MOST), jnp.int32),
            pltpu.VMEM((16, S), jnp.int32),
            pltpu.SMEM((16, S), jnp.int32),
            pltpu.SemaphoreType.DMA,
        ]
        + work(2 * (SX + 2), ALL_MOST + 16),
        8,
    )(places, ylo, yhi, y_up, y_down, tiles, sums, density_old)


def solution(mesh):
    return jax.shard_map(
        per_device,
        mesh=mesh,
        in_specs=(
            P(None, "gx", "gy", "gz", None),
            P("gx", "gy", "gz", None),
            P("gx", "gy", "gz", None),
            P("gx", "gy", "gz"),
            P("gx", "gy", "gz", None),
            P("gx", "gy", "gz", None),
            P("gx", "gy", "gz"),
        ),
        out_specs=(P("gx", "gy", "gz", None), P(None, "gx", "gy", "gz", None)),
        check_vma=False,
    )
```

```python
import functools
import math

import jax
import jax.numpy as jnp
from jax import lax
from jax.experimental import pallas as pl
from jax.experimental.pallas import tpu as pltpu
from jax.sharding import PartitionSpec as P

KC = 21.0 / (2.0 * math.pi)
SX, SY, SZ, S = 12, 6, 6, 128
MOST = 9
CELLS = SX * SY * SZ

ZERO = CELLS * 8
OWN_TAIL = ZERO + 8
OWN_ROWS = OWN_TAIL + 8

Z_TWO, Z_FAR, Z_TAIL, Z_ROWS = 288, 432, 720, 728
X_TWO, X_FAR, X_TAIL, X_ROWS = 240, 336, 576, 584
Y_TWO, Y_SUM, Y_TAIL, Y_ROWS = 640, 864, 976, 984

ZLO = OWN_ROWS
ZHI = ZLO + Z_ROWS
XLO = ZHI + Z_ROWS
XHI = XLO + X_ROWS
SLAB = XHI + X_ROWS

FIRST_PART = 8000
SLAB_MOST = 96
ALL_MOST = 256

VMEM = pl.BlockSpec(memory_space=pltpu.VMEM)
SMEM = pl.BlockSpec(memory_space=pltpu.SMEM)
ANY = pl.BlockSpec(memory_space=pl.ANY)
PARAMS = pltpu.CompilerParams(vmem_limit_bytes=40 * 1024 * 1024)

BLOCKS = [(0, 0), (0, -1), (0, 1), (-1, 0), (-1, -1), (-1, 1), (1, 0), (1, -1), (1, 1)]


def step(mode, i, near, sums):
    xi, yi, zi, hi, bi = i
    xj, yj, zj, mj, hj, wj = near
    dx, dy, dz = xi - xj, yi - yj, zi - zj
    sq = jnp.maximum(dx * dx + dy * dy + dz * dz, 1e-30)
    dist = sq * lax.rsqrt(sq)
    out = []
    if mode != "near":
        wi = jnp.maximum(hi - dist, 0.0)
        own = mj * (wi * wi * wi)
        out.append(sums[0] + own * (wi * (bi - wi)))
        if mode == "all":
            out += [sums[1] + own * dx, sums[2] + own * dy, sums[3] + own * dz]
    if mode != "density":
        wj_ = jnp.maximum(hj - dist, 0.0)
        other = wj * (wj_ * wj_ * wj_)
        last = sums[-3:]
        out += [last[0] + other * dx, last[1] + other * dy, last[2] + other * dz]
    return tuple(out)


WIDTH = {"all": 7, "density": 1, "near": 3}
FIRST = {"all": 0, "density": 0, "near": 4}
NEAR = {"all": 3, "density": 9, "near": 1}
GROUPS = {"all": 2, "density": 2, "near": 8}


def pairs(mode, src, four, two, use, count, used, tile, cols, table, many=None, ready=None):
    many, regs = many or NEAR[mode], GROUPS[mode]
    for u in range(many - 1):
        four[count + u] = jnp.int32(0)
        if two is not None:
            two[count + u] = jnp.int32(0)
        use[count + u] = jnp.float32(0.0)
    steps = lax.div(count + (many - 1), many)

    def spread():
        for n, c in enumerate((0, 1, 2, 4)):
            if mode == "near" and n == 3:
                break
            cols[n] = jnp.broadcast_to(tile[c : c + 1], (128, 128)).T

    if ready is None:
        spread()
    else:
        pl.when(jnp.logical_not(ready))(spread)
    width = WIDTH[mode]
    zero = jnp.zeros((8, 128), jnp.float32)

    def group(g, _):
        spots, own = [], []
        for v in range(regs):
            spot = pl.ds(pl.multiple_of((g * regs + v) * 8, 8), 8)
            x, y, z = [cols[n, spot, :] for n in range(3)]
            h = cols[3, spot, :] if mode != "near" else None
            spots.append(spot)
            own.append((x, y, z, h, 1.25 * h if mode != "near" else None))

        def body(q, sums):
            sums = list(sums)
            for u in range(many):
                at = q * many + u
                f = four[at]
                near = [
                    jnp.broadcast_to(src[pl.ds(f + c, 1), :], (8, 128)) for c in range(4)
                ]
                flag = use[at]
                if mode != "near":
                    near[3] = near[3] * jnp.where(flag >= 0.5, 1.0, 0.0)
                if mode != "density":
                    t = f + 4 if two is None else two[at]
                    near.append(jnp.broadcast_to(src[pl.ds(t, 1), :], (8, 128)))
                    weight = jnp.broadcast_to(src[pl.ds(t + 1, 1), :], (8, 128))
                    near.append(weight * jnp.where(flag == 1.0, 1.0, 0.0))
                else:
                    near += [None, None]
                for v in range(regs):
                    sums[v] = step(mode, own[v], near, sums[v])
            return tuple(sums)

        sums = lax.fori_loop(0, steps, body, ((zero,) * width,) * regs)
        for v in range(regs):
            for c in range(width):
                table[c, spots[v], :] = sums[v][c]
        return 0

    lax.fori_loop(0, lax.div(used + (8 * regs - 1), 8 * regs), group, 0)
    lines = [jnp.sum(table[c].T, axis=0, keepdims=True) for c in range(width)]
    if mode == "density":
        return lines[0]
    before = [jnp.zeros((1, 128), jnp.float32)] * FIRST[mode]
    after = [jnp.zeros((1, 128), jnp.float32)] * (8 - FIRST[mode] - width)
    return jnp.concatenate(before + lines + after, axis=0)


def bit(word, at):
    return lax.shift_right_logical(word, at) & 1


def clear(words, count):
    def one(k, _):
        words[k] = jnp.int32(0)
        return 0

    lax.fori_loop(0, count, one, 0, unroll=14)


def mark(words, at, place):
    words[at] = words[at] | lax.shift_left(jnp.int32(1), place)


def corner(code):
    return lax.shift_right_logical(code, 6), lax.shift_right_logical(code, 3) & 7, code & 7


def pack(
    counts_in, active_in, pos_in, mass_in, support_in, entropy_in, old_in, own_out, up, down, ids,
    counts, active, pos, mass, support, entropy, old, own, sems, out_sems,
):
    given = (active_in, counts_in, pos_in, mass_in, support_in, entropy_in, old_in)
    held = (active, counts, pos, mass, support, entropy, old)
    copies = [pltpu.make_async_copy(a, b, sems.at[n]) for n, (a, b) in enumerate(zip(given, held))]
    for copy in copies:
        copy.start()
    copies[0].wait()

    for copy in copies[1:]:
        copy.wait()
    own[ZERO : ZERO + 8] = jnp.zeros((8, 128), jnp.float32)
    size = SY * SZ * 8

    def plane(x):
        spot = pl.ds(pl.multiple_of(x * size, 8), size)
        return pltpu.make_async_copy(own.at[spot], own_out.at[spot], out_sems.at[x])

    sub = lax.broadcasted_iota(jnp.int32, (SZ, 128), 0)
    slot = lax.broadcasted_iota(jnp.int32, (SZ, 128), 1)

    def cells(x, n):
        for y in range(SY):
            many = jnp.zeros((SZ, 128), jnp.int32)
            act = jnp.zeros((SZ, 128), jnp.int32)
            for z in range(SZ):
                many = jnp.where(sub == z, counts[y, z, x], many)
                here = active[y, z, x]
                act = jnp.where(sub == z, here, act)
                ids[n] = x * 64 + y * 8 + z
                n = n + here
            h = support[x, y]
            inv = 1.0 / h
            inv2 = inv * inv
            inv4 = inv2 * inv2
            m = jnp.where(slot < many, mass[x, y], 0.0)
            gain = entropy[x, y] * (inv4 * inv4)
            power = jnp.exp(jnp.log(old[x, y]) * (-1.0 / 3.0))
            weight = m * gain * jnp.where(act > 0, 1.0, power)
            base = pl.multiple_of(x * (SY * SZ * 8), 8) + y * SZ * 8
            for c, value in enumerate(
                (pos[0, x, y], pos[1, x, y], pos[2, x, y], m, h, weight, gain)
            ):
                own[pl.ds(base + c, SZ, stride=8), :] = value
        plane(x).start()
        return n

    number = lax.fori_loop(0, SX, cells, jnp.int32(0))
    ids[15] = number
    lane = lax.broadcasted_iota(jnp.int32, (8, 128), 1)

    def tell(s, tail):
        code = ids[s]
        x, y, z = corner(code)
        ids[16 + s] = counts[y, z, x]
        tail = jnp.where(lane == s, code, tail)
        return jnp.where(lane == 16 + s, counts[y, z, x], tail)

    tail = lax.fori_loop(0, number, tell, jnp.where(lane == 15, number, 0)).astype(jnp.float32)
    own[OWN_TAIL : OWN_TAIL + 8] = tail
    up[Z_TAIL : Z_TAIL + 8] = tail
    down[Z_TAIL : Z_TAIL + 8] = tail
    rest = pltpu.make_async_copy(own.at[pl.ds(ZERO, 16)], own_out.at[pl.ds(ZERO, 16)], out_sems.at[SX])
    rest.start()

    def faces(x2, _):
        for u in range(2):
            for y in range(SY):
                base = pl.multiple_of(x2 * (2 * SY * SZ * 8), 8) + (u * SY + y) * SZ * 8
                four = pl.multiple_of(x2 * (2 * SY * 4), 8) + (u * SY + y) * 4
                two = pl.multiple_of(x2 * (2 * SY * 2), 8) + (u * SY + y) * 2
                for out, z1, z2 in ((up, SZ - 1, SZ - 2), (down, 0, 1)):
                    out[pl.ds(four, 4), :] = own[pl.ds(base + z1 * 8, 4), :]
                    out[pl.ds(two + Z_TWO, 2), :] = own[pl.ds(base + z1 * 8 + 4, 2), :]
                    out[pl.ds(four + Z_FAR, 4), :] = own[pl.ds(base + z2 * 8, 4), :]
        return 0

    lax.fori_loop(0, SX // 2, faces, 0)

    def finished(x, _):
        plane(x).wait()
        return 0

    lax.fori_loop(0, SX, finished, 0)
    rest.wait()


def own_row(x, y, z):
    return ((x * SY + y) * SZ + z) * 8


def local(part, ids, own, before, sums, four, two, use, flags, cols, table):
    number = ids[15]

    def price(s):
        x, y, z = corner(ids[s])

        def span(at, size):
            return 3 - (at == 0).astype(jnp.int32) - (at == size - 1).astype(jnp.int32)

        near = span(x, SX) * span(y, SY) * span(z, SZ)
        return near * lax.shift_right_logical(ids[16 + s] + 15, 4) * 14 + 400

    total = lax.fori_loop(0, number, lambda s, n: n + price(s), jnp.int32(0))
    limit = jnp.maximum(jnp.int32(FIRST_PART), lax.shift_right_logical(total, 1))

    def fits(s, state):
        n, spent = state
        spent = spent + price(s)
        return n + (spent <= limit).astype(jnp.int32), spent

    half, _ = lax.fori_loop(0, number, fits, (jnp.int32(0), jnp.int32(0)))

    clear(flags, SX * SY)

    def one(s, _):
        x, y, z = corner(ids[s])
        mark(flags, x * SY + y, z)
        return 0

    lax.fori_loop(0, number, one, 0)
    if before is not None:
        sums[...] = before[...]

    def slot(s, _):
        a, b, d = corner(ids[s])
        count = jnp.int32(0)
        in_z = [(d + ed >= 0) & (d + ed < SZ) for ed in (-1, 0, 1)]
        for ea in (-1, 0, 1):
            for eb in (-1, 0, 1):
                na, nb = a + ea, b + eb
                inside = (na >= 0) & (na < SX) & (nb >= 0) & (nb < SY)
                column = na * SY + nb
                word = flags[jnp.where(inside, column, 0)]
                row = column * (SZ * 8) + d * 8
                for n, ed in enumerate((-1, 0, 1)):
                    four[count] = row + ed * 8
                    known = bit(word, jnp.maximum(d + ed, 0))
                    use[count] = jnp.where(known > 0, jnp.float32(0.5), jnp.float32(1.0))
                    count = count + (inside & in_z[n]).astype(jnp.int32)
        tile = own[pl.ds(pl.multiple_of(own_row(a, b, d), 8), 8), :]
        sums[s] = pairs("all", own, four, None, use, count, ids[16 + s], tile, cols, table, 6)
        return 0

    if part == 0:
        lax.fori_loop(0, half, slot, 0)
    else:
        lax.fori_loop(half, number, slot, 0)


def local_first(ids, own, sums, *scratch):
    local(0, ids, own, None, sums, *scratch)


def local_second(ids, own, before, _, sums, *scratch):
    local(1, ids, own, before, sums, *scratch)


def pack_x(own, zlo, zhi, _, up, down):
    for out, x1, x2 in ((up, SX - 1, SX - 2), (down, 0, 1)):
        for y in range(SY):
            for z in range(-2, SZ + 2):
                for x, base in ((x1, 0), (x2, X_FAR)):
                    spot = base + (y * (SZ + 4) + z + 2) * 4
                    if 0 <= z < SZ:
                        row = own_row(x, y, z)
                        out[spot : spot + 4] = own[row : row + 4]
                    else:
                        src = zlo if z < 0 else zhi
                        far = Z_FAR if z in (-2, SZ + 1) else 0
                        row = far + (x * SY + y) * 4
                        out[spot : spot + 4] = src[row : row + 4]
                if -1 <= z <= SZ:
                    spot = X_TWO + (y * (SZ + 2) + z + 1) * 2
                    if 0 <= z < SZ:
                        row = own_row(x1, y, z) + 4
                        out[spot : spot + 2] = own[row : row + 2]
                    else:
                        src = zlo if z < 0 else zhi
                        row = Z_TWO + (x1 * SY + y) * 2
                        out[spot : spot + 2] = src[row : row + 2]
        out[X_TAIL : X_TAIL + 8] = jnp.zeros((8, 128), jnp.float32)
        out[X_TAIL : X_TAIL + 1] = own[OWN_TAIL : OWN_TAIL + 1]
        out[X_TAIL + 1 : X_TAIL + 2] = zlo[Z_TAIL : Z_TAIL + 1]
        out[X_TAIL + 2 : X_TAIL + 3] = zhi[Z_TAIL : Z_TAIL + 1]


def slab_rows(x, z):
    zlow, xlow = z < 0, x < 0
    zout = zlow | (z >= SZ)
    xout = xlow | (x >= SX)
    zbase = jnp.where(zlow, ZLO, ZHI)
    zfar = jnp.where((z == -2) | (z == SZ + 1), Z_FAR, 0)
    xbase = jnp.where(xlow, XLO, XHI)
    xfar = jnp.where((x == -2) | (x == SX + 1), X_FAR, 0)
    four = jnp.where(zout, zbase + zfar + x * (SY * 4), x * (SY * SZ * 8) + z * 8)
    two = jnp.where(zout, zbase + Z_TWO + x * (SY * 2), x * (SY * SZ * 8) + z * 8 + 4)
    four = jnp.where(xout, xbase + xfar + (z + 2) * 4, four)
    two = jnp.where(xout, xbase + X_TWO + (z + 1) * 2, two)
    add4 = jnp.where(xout, (SZ + 4) * 4, jnp.where(zout, 4, SZ * 8))
    add2 = jnp.where(xout, (SZ + 2) * 2, jnp.where(zout, 2, SZ * 8))
    return four, two, add4, add2


def slab_rows_at(x, y, z):
    if 0 <= x < SX and 0 <= z < SZ:
        return own_row(x, y, z), own_row(x, y, z) + 4
    if 0 <= x < SX:
        base, far, k = ZLO if z < 0 else ZHI, z in (-2, SZ + 1), x * SY + y
        return base + (Z_FAR if far else 0) + k * 4, base + Z_TWO + k * 2
    base, far = XLO if x < 0 else XHI, x in (-2, SX + 1)
    four = base + (X_FAR if far else 0) + (y * (SZ + 4) + z + 2) * 4
    return four, base + X_TWO + (y * (SZ + 2) + z + 1) * 2


def gather(rows, own, zlo, zhi, xlo, xhi):
    rows[0:OWN_ROWS] = own[...]
    rows[ZLO:ZHI] = zlo[...]
    rows[ZHI:XLO] = zhi[...]
    rows[XLO:XHI] = xlo[...]
    rows[XHI:SLAB] = xhi[...]


def slab_tools(rows, four, two, use, flags, cols, table):
    def near_list(x, y, z, own_cell):
        count = jnp.int32(0)
        for ea in (-1, 0, 1):
            for ed in (-1, 0, 1):
                na, nd = x + ea, z + ed
                f4, f2, add4, add2 = slab_rows(na, nd)
                if own_cell:
                    outer = (na < 0) | (na >= SX) | (nd < 0) | (nd >= SZ)
                for eb in (-1, 0, 1):
                    nb = y + eb
                    wanted = (nb >= 0) & (nb < SY)
                    four[count] = f4 + nb * add4
                    if own_cell:
                        wanted = wanted & outer
                        two[count] = f2 + nb * add2
                        word = flags[(na + 1) * SY + jnp.where(wanted, nb, 0)]
                        known = bit(word, nd + 1)
                        use[count] = jnp.where(known > 0, jnp.float32(0.5), jnp.float32(1.0))
                    else:
                        use[count] = jnp.float32(1.0)
                    count = count + wanted.astype(jnp.int32)
        return count

    def cell(x, y, z):
        f4, f2, add4, add2 = slab_rows(x, z)
        first = rows[pl.ds(f4 + y * add4, 4), :]
        second = rows[pl.ds(f2 + y * add2, 2), :]
        return jnp.concatenate([first, second, jnp.zeros((2, 128), jnp.float32)], axis=0)

    def own_sums(x, y, z, used):
        count = near_list(x, y, z, True)
        return pairs("all", rows, four, two, use, count, used, cell(x, y, z), cols, table)

    def halo_cell(x, y, z, used):
        count = near_list(x, y, z, False)
        tile = cell(x, y, z)
        return tile, pairs("density", rows, four, None, use, count, used, tile, cols, table)

    return own_sums, halo_cell


def beside(places, mine, x, y, z):
    def one(t, found):
        close = (
            (jnp.abs(places[0, t] - x) <= 1)
            & (jnp.abs(places[1, t] - y) <= 1)
            & (jnp.abs(places[2, t] - z) <= 1)
        )
        return found | close.astype(jnp.int32)

    return lax.fori_loop(0, mine, one, jnp.int32(0)) > 0


def on_border(x, z):
    return (x == 0) | (x == SX - 1) | (z == 0) | (z == SZ - 1)


def on_face(y):
    return (y == 0) | (y == SY - 1)


def weigh(cells, total):
    def some(q, _):
        base = pl.multiple_of(q * 64, 64)

        def get(c):
            return cells[pl.ds(base + c, 8, stride=8), :]

        good = get(3) > 0.0
        inv = 1.0 / jnp.where(good, get(4), 1.0)
        inv2 = inv * inv
        inv4 = inv2 * inv2
        fresh = (4.0 * KC) * (inv4 * inv4) * get(6)
        safe = jnp.where(good, fresh, 1.0)
        power = jnp.exp(jnp.log(safe) * (-1.0 / 3.0))
        weight = get(5) * power
        cells[pl.ds(base + 5, 8, stride=8), :] = jnp.where(good, weight, 0.0)
        cells[pl.ds(base + 6, 8, stride=8), :] = safe
        cells[pl.ds(base + 7, 8, stride=8), :] = power
        return 0

    lax.fori_loop(0, lax.div(total + 7, 8), some, 0)


def slab_faces(
    own, zlo, zhi, xlo, xhi, before, up, down, tiles, sums, places,
    rows, tails, lists, sem, four, two, use, flags, cols, table,
):
    tails[...] = jnp.zeros(tails.shape, jnp.int32)
    tails[0:1] = own[OWN_TAIL : OWN_TAIL + 1].astype(jnp.int32)
    tails[1:2] = zlo[Z_TAIL : Z_TAIL + 1].astype(jnp.int32)
    tails[2:3] = zhi[Z_TAIL : Z_TAIL + 1].astype(jnp.int32)
    tails[3:6] = xlo[X_TAIL : X_TAIL + 3].astype(jnp.int32)
    tails[6:9] = xhi[X_TAIL : X_TAIL + 3].astype(jnp.int32)
    copy = pltpu.make_async_copy(tails, lists, sem)
    copy.start()
    gather(rows, own, zlo, zhi, xlo, xhi)

    clear(flags, (SX + 2) * SY)
    for out, y in ((up, SY - 1), (down, 0)):
        for x in range(-2, SX + 2):
            for z in range(-2, SZ + 2):
                row4, row2 = slab_rows_at(x, y, z)
                spot = ((x + 2) * (SZ + 4) + z + 2) * 4
                out[spot : spot + 4] = rows[row4 : row4 + 4]
                if -1 <= x <= SX and -1 <= z <= SZ:
                    spot = Y_TWO + ((x + 1) * (SZ + 2) + z + 1) * 2
                    out[spot : spot + 2] = rows[row2 : row2 + 2]
        out[Y_SUM:Y_TAIL] = jnp.zeros((Y_TAIL - Y_SUM, 128), jnp.float32)
    copy.wait()

    number = jnp.int32(0)
    for q, (bx, bz) in enumerate(BLOCKS):

        def one(s, n, q=q, bx=bx, bz=bz):
            a, b, d = corner(lists[q, s])
            x, z = a + bx * SX, d + bz * SZ
            inside = (x >= -1) & (x <= SX) & (z >= -1) & (z <= SZ)
            places[0, n] = x
            places[1, n] = b
            places[2, n] = z
            places[3, n] = lists[q, 16 + s]

            @pl.when(inside)
            def _():
                mark(flags, (x + 1) * SY + b, z + 1)

            return n + inside.astype(jnp.int32)

        number = lax.fori_loop(0, lists[q, 15], one, number)
    places[4, 0] = number
    places[4, 1] = lists[0, 15]
    mine = lists[0, 15]

    lane = lax.broadcasted_iota(jnp.int32, (8, 128), 1)
    line = lax.broadcasted_iota(jnp.int32, (8, 128), 0)

    def tell(s, state):
        lists_, numbers = list(state[0]), list(state[1])
        x, y, z = places[0, s], places[1, s], places[2, s]
        for n, edge in enumerate((SY - 1, 0)):
            here = y == edge
            at = jnp.where(here, numbers[n], 126)
            value = jnp.where(line == 0, x, jnp.where(line == 1, z, places[3, s]))
            lists_[n] = jnp.where(lane == at, value, lists_[n])
            numbers[n] = numbers[n] + here.astype(jnp.int32)
        return tuple(lists_), tuple(numbers)

    nothing = jnp.zeros((8, 128), jnp.int32)
    told, numbers = lax.fori_loop(
        0, number, tell, ((nothing, nothing), (jnp.int32(0), jnp.int32(0)))
    )
    for n, out in enumerate((up, down)):
        out[Y_TAIL:Y_ROWS] = jnp.where(lane == 127, numbers[n], told[n]).astype(jnp.float32)

    own_sums, halo_cell = slab_tools(rows, four, two, use, flags, cols, table)

    def send_sum(s, x, y, z):
        spot = Y_SUM + (x + 1) * (SZ + 2) + z + 1

        @pl.when(y == 0)
        def _():
            down[pl.ds(spot, 1), :] = tiles[s, 6:7]

        @pl.when(y == SY - 1)
        def _():
            up[pl.ds(spot, 1), :] = tiles[s, 6:7]

    def own_slot(s, _):
        x, y, z = places[0, s], places[1, s], places[2, s]
        sums[s] = before[s]
        row = pl.multiple_of(own_row(x, y, z), 8)
        whole = rows[pl.ds(row, 8), :]
        tiles[s] = whole

        @pl.when(on_face(y))
        def _():
            @pl.when(on_border(x, z))
            def _():
                sums[s] = sums[s] + own_sums(x, y, z, places[3, s])

            tiles[s, 6:7] = sums[s, 0:1]
            send_sum(s, x, y, z)

        sums[s, 7:8] = whole[6:7]
        return 0

    def halo_slot(s, _):
        x, y, z = places[0, s], places[1, s], places[2, s]

        @pl.when(on_face(y))
        def _():
            tiles[s], total = halo_cell(x, y, z, places[3, s])
            tiles[s, 6:7] = total
            send_sum(s, x, y, z)

        return 0

    lax.fori_loop(0, mine, own_slot, 0)
    lax.fori_loop(mine, number, halo_slot, 0)


def slab_inside(
    places, own, zlo, zhi, xlo, xhi, tiles_in, sums_in, tiles, sums,
    cells, rows, four, two, use, flags, cols, table,
):
    gather(rows, own, zlo, zhi, xlo, xhi)
    tiles[...] = tiles_in[...]
    sums[...] = sums_in[...]
    number, mine = places[4, 0], places[4, 1]
    clear(flags, (SX + 2) * SY)

    def one(s, _):
        mark(flags, (places[0, s] + 1) * SY + places[1, s], places[2, s] + 1)
        return 0

    lax.fori_loop(0, number, one, 0)
    own_sums, halo_cell = slab_tools(rows, four, two, use, flags, cols, table)

    def own_slot(s, _):
        x, y, z = places[0, s], places[1, s], places[2, s]

        @pl.when(jnp.logical_not(on_face(y)))
        def _():
            @pl.when(on_border(x, z))
            def _():
                sums[s, 0:7] = sums[s, 0:7] + own_sums(x, y, z, places[3, s])[0:7]

            tiles[s, 6:7] = sums[s, 0:1]

        return 0

    def halo_slot(s, _):
        x, y, z = places[0, s], places[1, s], places[2, s]

        @pl.when(jnp.logical_not(on_face(y)) & beside(places, mine, x, y, z))
        def _():
            tiles[s], total = halo_cell(x, y, z, places[3, s])
            tiles[s, 6:7] = total

        return 0

    lax.fori_loop(0, mine, own_slot, 0)
    lax.fori_loop(mine, number, halo_slot, 0)

    def take(s, _):
        cells[pl.ds(pl.multiple_of(s * 8, 8), 8), :] = tiles[s]
        return 0

    lax.fori_loop(0, number, take, 0)
    weigh(cells, number)

    def inner(s, _):
        x, y, z = places[0, s], places[1, s], places[2, s]

        def check(t, n):
            close = (
                (jnp.abs(places[0, t] - x) <= 1)
                & (jnp.abs(places[1, t] - y) <= 1)
                & (jnp.abs(places[2, t] - z) <= 1)
                & jnp.logical_not(on_face(places[1, t]))
            )
            four[n] = t * 8
            use[n] = jnp.float32(1.0)
            return n + close.astype(jnp.int32)

        count = lax.fori_loop(0, number, check, jnp.int32(0))

        @pl.when(count > 0)
        def _():
            tile = cells[pl.ds(pl.multiple_of(s * 8, 8), 8), :]
            sums[s, 4:7] = sums[s, 4:7] + pairs(
                "near", cells, four, None, use, count, places[3, s], tile, cols, table
            )[4:7]

        return 0

    lax.fori_loop(0, mine, inner, 0)


def finish(
    places_in, ylo, yhi, up, down, tiles, sums, old, density, accel,
    places, places_sem, rows, cells, final, spots, tails, lists, sem, four, two, use, flags, cols, table,
):
    tails[0:8] = ylo[Y_TAIL:Y_ROWS].astype(jnp.int32)
    tails[8:16] = yhi[Y_TAIL:Y_ROWS].astype(jnp.int32)
    copy = pltpu.make_async_copy(tails, lists, sem)
    copy.start()
    other = pltpu.make_async_copy(places_in, places, places_sem)
    other.start()
    rows[0:Y_ROWS] = ylo[...]
    rows[Y_ROWS : 2 * Y_ROWS] = yhi[...]
    rows[2 * Y_ROWS : 3 * Y_ROWS] = down[...]
    rows[3 * Y_ROWS : 4 * Y_ROWS] = up[...]
    density[...] = old[...]
    accel[...] = jnp.zeros(accel.shape, jnp.float32)
    clear(flags, 2 * (SX + 2))
    other.wait()
    number, mine = places[4, 0], places[4, 1]

    def take(s, n):
        for c in range(4):
            spots[c, n] = places[c, s]
        cells[pl.ds(pl.multiple_of(n * 8, 8), 8), :] = tiles[s]
        wanted = beside(places, mine, places[0, s], places[1, s], places[2, s])
        return n + wanted.astype(jnp.int32)

    total = lax.fori_loop(0, number, take, jnp.int32(0))
    final[...] = sums[...]
    copy.wait()
    for side in range(2):

        def one(s, n, side=side):
            x, z = lists[side * 8, s], lists[side * 8 + 1, s]
            spots[0, n] = x
            spots[1, n] = jnp.int32(-1 if side == 0 else SY)
            spots[2, n] = z
            spots[3, n] = lists[side * 8 + 2, s]
            mark(flags, side * (SX + 2) + x + 1, z + 1)
            at = (x + 1) * (SZ + 2) + z + 1
            base = side * Y_ROWS
            row4 = base + ((x + 2) * (SZ + 4) + z + 2) * 4
            row2 = base + Y_TWO + at * 2
            cells[pl.ds(pl.multiple_of(n * 8, 8), 8), :] = jnp.concatenate(
                [
                    rows[pl.ds(row4, 4), :],
                    rows[pl.ds(row2, 2), :],
                    rows[pl.ds(base + Y_SUM + at, 1), :],
                    jnp.zeros((1, 128), jnp.float32),
                ],
                axis=0,
            )
            wanted = beside(spots, mine, x, jnp.int32(-1 if side == 0 else SY), z)
            return n + wanted.astype(jnp.int32)

        total = lax.fori_loop(0, lists[side * 8, 127], one, total)

    def near_list(s, own_cell):
        x, y, z = spots[0, s], spots[1, s], spots[2, s]
        high = y >= SY - 1
        outer = (y == -1) | (y == SY)
        base = jnp.where(outer, 2 * Y_ROWS, 0) + jnp.where(high, Y_ROWS, 0)
        for e, (ea, ed) in enumerate((p, q) for p in (-1, 0, 1) for q in (-1, 0, 1)):
            na, nd = x + ea, z + ed
            four[e] = base + ((na + 2) * (SZ + 4) + nd + 2) * 4
            use[e] = jnp.float32(1.0)
            if own_cell:
                two[e] = base + Y_TWO + ((na + 1) * (SZ + 2) + nd + 1) * 2
                word = flags[jnp.where(high, SX + 2, 0) + na + 1]
                use[e] = jnp.where(bit(word, nd + 1) > 0, jnp.float32(0.5), jnp.float32(1.0))

    def across_own(s, _):
        y = spots[1, s]

        @pl.when((y <= 0) | (y >= SY - 1))
        def _():
            near_list(s, True)
            spot = pl.multiple_of(s * 8, 8)
            tile = cells[pl.ds(spot, 8), :]
            count = jnp.int32(9)
            result = pairs(
                "all", rows, four, two, use, count, spots[3, s], tile, cols.at[s], table, 9
            )
            final[s, 0:7] = final[s, 0:7] + result[0:7]
            cells[pl.ds(spot + 6, 1), :] = tile[6:7] + result[0:1]

        return 0

    def across_halo(s, _):
        y = spots[1, s]

        @pl.when((y <= 0) | (y >= SY - 1))
        def _():
            near_list(s, False)
            spot = pl.multiple_of(s * 8, 8)
            tile = cells[pl.ds(spot, 8), :]
            count = jnp.int32(9)
            result = pairs("density", rows, four, None, use, count, spots[3, s], tile, cols.at[MOST], table)
            cells[pl.ds(spot + 6, 1), :] = tile[6:7] + result

        return 0

    lax.fori_loop(0, mine, across_own, 0)
    lax.fori_loop(mine, total, across_halo, 0)

    weigh(cells, total)

    def last(s, _):
        x, y, z = spots[0, s], spots[1, s], spots[2, s]

        def check(t, n):
            close = (
                (jnp.abs(spots[0, t] - x) <= 1)
                & (jnp.abs(spots[1, t] - y) <= 1)
                & (jnp.abs(spots[2, t] - z) <= 1)
                & ((spots[1, t] <= 0) | (spots[1, t] >= SY - 1))
            )
            four[n] = t * 8
            use[n] = jnp.float32(1.0)
            return n + close.astype(jnp.int32)

        count = lax.fori_loop(0, total, check, jnp.int32(0))
        spot = pl.multiple_of(s * 8, 8)
        tile = cells[pl.ds(spot, 8), :]

        @pl.when(count > 0)
        def _():
            final[s, 4:7] = final[s, 4:7] + pairs(
                "near", cells, four, None, use, count, spots[3, s], tile, cols.at[s], table,
                ready=on_face(y),
            )[4:7]

        good = tile[3:4] > 0.0
        own = final[s, 7:8] * tile[7:8]
        place = (x, y, pl.ds(z, 1), slice(None))
        density[place] = jnp.where(good, tile[6:7], old[place])
        for c in range(3):
            push = (20.0 * KC) * (own * final[s, 1 + c : 2 + c] + final[s, 4 + c : 5 + c])
            accel[(c, *place)] = jnp.where(good, push, 0.0)
        return 0

    lax.fori_loop(0, mine, last, 0)


def f32(*shape):
    return jax.ShapeDtypeStruct(shape, jnp.float32)


def i32(*shape):
    return jax.ShapeDtypeStruct(shape, jnp.int32)


def neighbours(up, down, axis):
    size = lax.axis_size(axis)
    pairs_ = [(i, i + 1) for i in range(size - 1)]
    low = lax.ppermute(up, axis, pairs_)
    high = lax.ppermute(down, axis, [(j, i) for i, j in pairs_])
    return low, high


def work(flags, near, sets=None):
    spread = (4, 128, 128) if sets is None else (sets, 4, 128, 128)
    return [
        pltpu.SMEM((near,), jnp.int32),
        pltpu.SMEM((near,), jnp.int32),
        pltpu.SMEM((near,), jnp.float32),
        pltpu.SMEM((flags,), jnp.int32),
        pltpu.VMEM(spread, jnp.float32),
        pltpu.VMEM((7, 128, 128), jnp.float32),
    ]


def cost(us):
    return pl.CostEstimate(flops=us * 10_000_000, bytes_accessed=us * 2_000_000, transcendentals=0)


def call(body, outs, out_specs, in_specs, scratch, us, limit=40):
    return pl.pallas_call(
        body,
        out_shape=outs,
        in_specs=in_specs,
        out_specs=out_specs,
        scratch_shapes=scratch,
        compiler_params=pltpu.CompilerParams(vmem_limit_bytes=limit * 1024 * 1024),
        cost_estimate=cost(us),
    )


def per_device(positions, mass, support, counts, entropy, density_old, active):
    small = [jnp.transpose(v, (1, 2, 0)) for v in (counts, active)]
    own, z_up, z_down, ids = call(
        pack,
        (f32(OWN_ROWS, S), f32(Z_ROWS, S), f32(Z_ROWS, S), i32(32)),
        (ANY, VMEM, VMEM, SMEM),
        [ANY] * 7,
        [
            pltpu.SMEM((SY, SZ, SX), jnp.int32),
            pltpu.SMEM((SY, SZ, SX), jnp.int32),
            pltpu.VMEM((3, SX, SY, SZ, S), jnp.float32),
        ]
        + [pltpu.VMEM((SX, SY, SZ, S), jnp.float32)] * 4
        + [
            pltpu.VMEM((OWN_ROWS, S), jnp.float32),
            pltpu.SemaphoreType.DMA((7,)),
            pltpu.SemaphoreType.DMA((SX + 1,)),
        ],
        2,
        56,
    )(*small, positions, mass, support, entropy, density_old)
    zlo, zhi = neighbours(z_up, z_down, "gz")
    first = call(
        local_first, f32(16, 8, S), VMEM, [SMEM, VMEM], work(SX * SY, 48), 8
    )(ids, own)
    x_up, x_down = call(
        pack_x, (f32(X_ROWS, S), f32(X_ROWS, S)), (VMEM, VMEM), [VMEM] * 3 + [ANY], [], 1
    )(own, zlo, zhi, first)
    xlo, xhi = neighbours(x_up, x_down, "gx")
    second = call(
        local_second,
        f32(16, 8, S),
        VMEM,
        [SMEM, VMEM, VMEM, ANY],
        work(SX * SY, 48),
        8,
    )(ids, own, first, x_up)
    y_up, y_down, tiles, sums, places = call(
        slab_faces,
        (f32(Y_ROWS, S), f32(Y_ROWS, S), f32(SLAB_MOST, 8, S), f32(16, 8, S), i32(8, 128)),
        (VMEM, VMEM, VMEM, VMEM, SMEM),
        [VMEM] * 6,
        [
            pltpu.VMEM((SLAB, S), jnp.float32),
            pltpu.VMEM((16, S), jnp.int32),
            pltpu.SMEM((16, S), jnp.int32),
            pltpu.SemaphoreType.DMA,
        ]
        + work((SX + 2) * SY, 48),
        4,
    )(own, zlo, zhi, xlo, xhi, second)
    ylo, yhi = neighbours(y_up, y_down, "gy")
    tiles, sums = call(
        slab_inside,
        (f32(SLAB_MOST, 8, S), f32(16, 8, S)),
        (VMEM, VMEM),
        [SMEM] + [VMEM] * 7,
        [pltpu.VMEM((SLAB_MOST * 8, S), jnp.float32), pltpu.VMEM((SLAB, S), jnp.float32)]
        + work((SX + 2) * SY, SLAB_MOST + 16),
        6,
    )(places, own, zlo, zhi, xlo, xhi, tiles, sums)
    return call(
        finish,
        (f32(SX, SY, SZ, S), f32(3, SX, SY, SZ, S)),
        (VMEM, VMEM),
        [ANY] + [VMEM] * 7,
        [
            pltpu.SMEM((8, 128), jnp.int32),
            pltpu.SemaphoreType.DMA,
            pltpu.VMEM((4 * Y_ROWS, S), jnp.float32),
            pltpu.VMEM((ALL_MOST * 8, S), jnp.float32),
            pltpu.VMEM((16, 8, S), jnp.float32),
            pltpu.SMEM((4, ALL_MOST), jnp.int32),
            pltpu.VMEM((16, S), jnp.int32),
            pltpu.SMEM((16, S), jnp.int32),
            pltpu.SemaphoreType.DMA,
        ]
        + work(2 * (SX + 2), ALL_MOST + 16, MOST + 1),
        8,
    )(places, ylo, yhi, y_up, y_down, tiles, sums, density_old)


def solution(mesh):
    return jax.shard_map(
        per_device,
        mesh=mesh,
        in_specs=(
            P(None, "gx", "gy", "gz", None),
            P("gx", "gy", "gz", None),
            P("gx", "gy", "gz", None),
            P("gx", "gy", "gz"),
            P("gx", "gy", "gz", None),
            P("gx", "gy", "gz", None),
            P("gx", "gy", "gz"),
        ),
        out_specs=(P("gx", "gy", "gz", None), P(None, "gx", "gy", "gz", None)),
        check_vma=False,
    )
```
